32 devices in a mesh: groups: 2 (over y), graph: 4 (over z), dp: 4 (over x, core).
Axes of the slice: x: 2, y: 2, z: 4, core: 2. Of those that a mesh axis runs over, the one named last changes fastest.
Arguments:
- edge_emb: bfloat16 [8, 4096, 512], P(('groups', 'dp'), 'graph'), parts along dimension 0, may hold values from -6 to 6
- cotangent: bfloat16 [8, 4096, 512], P(('groups', 'dp'), 'graph'), parts along dimension 0, may hold values from -6 to 6
- fetch_rows: int32 [8, 4, 4, 64], P(('groups', 'dp'), 'graph'), parts along dimension 0, may hold values from 0 to 1023, as said below
- store_rows: int32 [8, 4, 4, 64], P(('groups', 'dp'), 'graph'), parts along dimension 0, may hold values from 0 to 1023, as said below
- trip_src: int32 [8, 128, 128], P(('groups', 'dp'), 'graph'), parts along dimension 0, may hold values from 0 to 255
- trip_dst: int32 [8, 128, 128], P(('groups', 'dp'), 'graph'), parts along dimension 0, may hold values from 0 to 255
- trip_basis: bfloat16 [8, 16384, 128], P(('groups', 'dp'), 'graph'), parts along dimension 0, may hold values from -6 to 6
- block_count: int32 [8, 4], P(('groups', 'dp'), 'graph'), parts along dimension 0, may hold values from 1 to 32, as said below
- w_basis: bfloat16 [128, 512], replicated, may hold values from -0.5 to 0.5
- w_out: bfloat16 [512, 512], replicated, may hold values from -0.25 to 0.25
Outputs:
- updated: bfloat16 [8, 4096, 512], P(('groups', 'dp'), 'graph'), parts along dimension 0
- grad_edges: bfloat16 [8, 4096, 512], P(('groups', 'dp'), 'graph'), parts along dimension 0
- grad_out: float32 [1024, 512], P('groups'), parts along dimension 0
- grad_basis: float32 [256, 512], P('groups'), parts along dimension 0
The draws below stay inside these ranges and needn't reach their ends.
There are 2 independent parts, one for each index of `groups`. The reference program is written for one: setup_inputs(seed, part) draws one part's arguments, and reference() takes and returns one part's arrays. A program takes and returns all parts, laid end to end along the dimension named above; an argument that names none is the same for every part. Nothing has to cross between parts.
Inputs may be any that keep to these rules, and one draw needn't show every extreme that they name: `fetch_rows`: within one device's list for one owner the 64 indices are distinct. `store_rows`: within one device's list for one owner the 64 indices are distinct. `block_count`: in each graph batch some device uses all 32 blocks.
All inputs are finite; a program needn't handle non-finite values.
Results may differ from the reference program's by a relative error of at most 0.01.
Values may be sent and summed in bfloat16 or wider, within the bound.
No kernel may reach another device: no remote copies, remote signals or barrier semaphores. Data moves between devices by JAX's collectives and lax.ppermute only.
A program may use at most 64 MiB of HBM per device.

```python
import jax
import jax.numpy as jnp
from jax import lax

D = 512
NB = 128
EDGE_DEV = 1024
FETCH_DEV = 256
TRIP_BLOCKS = 32
BLOCK = 128
CAP = 64
EDGES = 4096
TRIPLETS = 16384
N_GRAPH = 4
N_DP = 4


def pick_rows(key):
    count = N_DP * N_GRAPH * N_GRAPH
    keys = jax.random.split(key, count)
    chosen = jax.vmap(lambda k: jax.random.permutation(k, EDGE_DEV)[:CAP])(keys)
    return chosen.astype(jnp.int32).reshape(N_DP, N_GRAPH, N_GRAPH, CAP)


def draw_fetch_rows(key, part):
    key = jax.random.fold_in(key, 1)
    return pick_rows(key)


def draw_store_rows(key, part):
    key = jax.random.fold_in(key, 2)
    return pick_rows(key)


def draw_block_count(key, part):
    key = jax.random.fold_in(key, 3)
    first, second = jax.random.split(key)
    counts = jax.random.randint(first, (N_DP, N_GRAPH), 1, TRIP_BLOCKS + 1)
    fullest = jax.random.randint(second, (N_DP,), 0, N_GRAPH)
    column = jnp.arange(N_GRAPH, dtype=jnp.int32)[None, :]
    return jnp.where(column == fullest[:, None], TRIP_BLOCKS, counts).astype(jnp.int32)


def touch_ends(result, own_key, smallest, high):
    longest = result.shape.index(max(result.shape))
    spots = []
    for shift in (0, 1):
        where = [jax.random.randint(jax.random.fold_in(own_key, axis), (), 0, length) for axis, length in enumerate(result.shape)]
        where[longest] = (where[longest] + shift) % result.shape[longest]
        spots.append(tuple(where))
    return result.at[spots[0]].set(smallest).at[spots[1]].set(high)


def levels(rng, extent, pieces, low, top_value):
    level, own = 1.0, jax.random.fold_in(rng, 6)
    for dim, shards_of in pieces:
        draws = jnp.exp(jax.random.uniform(jax.random.fold_in(own, dim), (shards_of,), jnp.float32, low / len(pieces), top_value / len(pieces)))
        level = level * jnp.repeat(draws, extent[dim] // shards_of).reshape([-1 if axis == dim else 1 for axis in range(len(extent))])
    return level


def noise(own_key, extent, scale, limit, cuts=(), held_as=jnp.bfloat16):
    values = jax.random.normal(own_key, extent, jnp.float32) * scale
    if len(cuts) > 0:
        values = levels(own_key, extent, cuts, -0.22, 0.18) * values
    return jnp.clip(values, min=-limit, max=limit).astype(held_as)


def setup_inputs(seed: int = 0, part: int = 0) -> dict:
    seeds = jax.random.split(jax.random.key(seed), 11)
    own_keys = jax.random.split(jax.random.fold_in(seeds[10], part), 11)
    return {
        "edge_emb": noise(own_keys[0], (N_DP, EDGES, D), 1.0, 6.0, ((0, 4), (1, 4))),
        "cotangent": noise(own_keys[1], (N_DP, EDGES, D), 1.0, 6.0, ((0, 4), (1, 4))),
        "fetch_rows": draw_fetch_rows(jax.random.fold_in(jax.random.fold_in(seeds[10], part), 71), part),
        "store_rows": draw_store_rows(jax.random.fold_in(jax.random.fold_in(seeds[10], part), 71), part),
        "trip_src": touch_ends(jax.random.randint(own_keys[4], (N_DP, N_GRAPH * TRIP_BLOCKS, BLOCK), 0, FETCH_DEV), jax.random.fold_in(own_keys[4], 1), 0, FETCH_DEV - 1).astype(jnp.int32),
        "trip_dst": touch_ends(jax.random.randint(own_keys[5], (N_DP, N_GRAPH * TRIP_BLOCKS, BLOCK), 0, FETCH_DEV), jax.random.fold_in(own_keys[5], 1), 0, FETCH_DEV - 1).astype(jnp.int32),
        "trip_basis": noise(own_keys[6], (N_DP, TRIPLETS, NB), 1.0, 6.0, ((0, 4), (1, 4))),
        "block_count": draw_block_count(jax.random.fold_in(jax.random.fold_in(seeds[10], part), 71), part),
        "w_basis": noise(seeds[8], (NB, D), NB ** -0.5, 0.5),
        "w_out": noise(seeds[9], (D, D), D ** -0.5, 0.25),
    }


def silu_grad(value):
    sig = jax.nn.sigmoid(value)
    return sig * (1.0 + value * (1.0 - sig))

def triplet_forward(fetched, src, dst, basis, live, w_basis):
    pre = jnp.dot(basis, w_basis, preferred_element_type=jnp.float32)
    filt = jax.nn.silu(pre)
    message = jnp.take(fetched, src, axis=0).astype(jnp.float32) * filt * live[:, None]
    return jax.ops.segment_sum(message, dst, num_segments=fetched.shape[0])

def triplet_backward(fetched, dpartial, src, dst, basis, live, w_basis):
    pre = jnp.dot(basis, w_basis, preferred_element_type=jnp.float32)
    filt = jax.nn.silu(pre)
    dmsg = jnp.take(dpartial, dst, axis=0).astype(jnp.float32) * live[:, None]
    dfilt = dmsg * jnp.take(fetched, src, axis=0).astype(jnp.float32)
    dpre = (dfilt * silu_grad(pre)).astype(jnp.bfloat16)
    dweight = jnp.dot(basis.T, dpre, preferred_element_type=jnp.float32)
    dsource = jax.ops.segment_sum(dmsg * filt, src, num_segments=fetched.shape[0])
    return (dweight, dsource)

def reference(edge_emb, cotangent, fetch_rows, store_rows, trip_src, trip_dst, trip_basis, block_count, w_basis, w_out):
    slots = N_GRAPH * CAP
    width = trip_src.shape[2]
    rows = TRIP_BLOCKS * width
    owner = (jnp.arange(N_GRAPH, dtype=jnp.int32) * EDGE_DEV)[None, :, None]
    grad_w_out = jnp.zeros((D, D), jnp.float32)
    grad_w_basis = jnp.zeros((NB, D), jnp.float32)
    updated_list = []
    grad_list = []
    for batch in range(N_DP):
        edges = edge_emb[batch]
        upstream = cotangent[batch]
        read_ids = (fetch_rows[batch] + owner).reshape(N_GRAPH, slots)
        store_ids = (store_rows[batch] + owner).reshape(-1)
        fetched = jnp.take(edges, read_ids, axis=0)
        src = trip_src[batch].reshape(N_GRAPH, rows)
        dst = trip_dst[batch].reshape(N_GRAPH, rows)
        basis = trip_basis[batch].reshape(N_GRAPH, rows, NB)
        position = jnp.arange(rows, dtype=jnp.int32)[None, :] // width
        live = (position < block_count[batch][:, None]).astype(jnp.float32)
        partial_value = lax.map(lambda a: triplet_forward(a[0], a[1], a[2], a[3], a[4], w_basis), (fetched, src, dst, basis, live))
        agg = jax.ops.segment_sum(partial_value.reshape(-1, D), store_ids, num_segments=EDGES)
        hidden = jax.nn.silu(agg).astype(jnp.bfloat16)
        updated = (edges.astype(jnp.float32) + jnp.dot(hidden, w_out, preferred_element_type=jnp.float32)).astype(jnp.bfloat16)
        grad_w_out = grad_w_out + jnp.dot(hidden.T, upstream, preferred_element_type=jnp.float32)
        dhidden = jnp.dot(upstream, w_out.T, preferred_element_type=jnp.float32)
        dagg = (dhidden * silu_grad(agg)).astype(jnp.bfloat16)
        dpartial = jnp.take(dagg, store_ids, axis=0).reshape(N_GRAPH, slots, D)
        dweights, dsources = lax.map(lambda a: triplet_backward(a[0], a[1], a[2], a[3], a[4], a[5], w_basis), (fetched, dpartial, src, dst, basis, live))
        grad_w_basis = grad_w_basis + lax.optimization_barrier(jnp.sum(dweights, axis=0))
        returned = jax.ops.segment_sum(dsources.reshape(-1, D), read_ids.reshape(-1), num_segments=EDGES)
        grad_edge = (upstream.astype(jnp.float32) + returned).astype(jnp.bfloat16)
        updated_list.append(updated)
        grad_list.append(grad_edge)
    grad_w_out = grad_w_out / jnp.sqrt(jnp.float32(N_DP * EDGES))
    grad_w_basis = grad_w_basis / jnp.sqrt(jnp.float32(N_DP * TRIPLETS))
    return (jnp.stack(updated_list), jnp.stack(grad_list), grad_w_out, grad_w_basis)
```

```python
import functools

import jax
import jax.numpy as jnp
from jax import lax
from jax.experimental import pallas as pl
from jax.experimental.pallas import tpu as pltpu
from jax.sharding import PartitionSpec as P

BF16 = jnp.bfloat16
F32 = jnp.float32
VMEM = pl.BlockSpec(memory_space=pltpu.VMEM)
SMEM = pl.BlockSpec(memory_space=pltpu.SMEM)
NN = (((1,), (0,)), ((), ()))
NT = (((1,), (1,)), ((), ()))


def dot(a, b, dims=NN):
    return lax.dot_general(a, b, dims, preferred_element_type=F32)


def silu_parts(value):
    sig = 0.5 * jnp.tanh(0.5 * value) + 0.5
    act = value * sig
    return act, sig + act * (1.0 - sig)


def call(body, outs, args, specs=None, flops=0, scratch=(), vmem=48):
    moved = sum(a.size * a.dtype.itemsize for a in args) + sum(
        o.size * o.dtype.itemsize for o in outs
    )
    return pl.pallas_call(
        body,
        out_shape=tuple(outs),
        in_specs=[VMEM] * len(args) if specs is None else specs,
        out_specs=tuple([VMEM] * len(outs)),
        scratch_shapes=list(scratch),
        cost_estimate=pl.CostEstimate(flops=flops, bytes_accessed=moved, transcendentals=0),
        compiler_params=pltpu.CompilerParams(vmem_limit_bytes=vmem << 20),
    )(*args)


def shape(dims, dtype=BF16):
    return jax.ShapeDtypeStruct(dims, dtype)


def prepare_kernel(per_owner, ranks, step, me, count, src, dst, basis, weight, filt, slope, s_hot, d_hot):
    slots = ranks * per_owner
    block = src.shape[1]
    weight_t = weight[...].T
    offset = me[0] * per_owner
    rows = lax.broadcasted_iota(jnp.int32, (slots, block), 0)

    def turn(i, carry):
        start = pl.multiple_of(i * step, step)
        pre = dot(weight_t, basis[pl.ds(start, step), :], NT)
        lane = lax.broadcasted_iota(jnp.int32, (1, step), 1) + start
        live = (lane < count[0, 0] * block).astype(F32)
        act, grad = silu_parts(pre)
        filt[:, pl.ds(start, step)] = (act * live).astype(BF16)
        slope[:, pl.ds(start, step)] = (grad * live).astype(BF16)
        for k in range(step // block):
            b = i * (step // block) + k
            at = pl.multiple_of(start + k * block, block)
            for index, hot in ((src, s_hot), (dst, d_hot)):
                slot = index[pl.ds(b, 1), :] - offset
                slot = jnp.where(slot < 0, slot + slots, slot)
                hot[:, pl.ds(at, block)] = jnp.where(rows == slot, 1.0, 0.0).astype(BF16)
        return carry

    lax.fori_loop(0, basis.shape[0] // step, turn, 0)


def lend_kernel(per_owner, ranks, me, *refs):
    lists, edges = refs[:ranks], refs[ranks]
    outs = refs[ranks + 1 : 2 * ranks + 1]
    lent_hot, kept_hot = refs[2 * ranks + 1], refs[2 * ranks + 2]
    edge_dev = edges.shape[0]
    columns = lax.broadcasted_iota(jnp.int32, (per_owner, edge_dev), 1).astype(F32)
    for s in range(ranks):
        row = lists[s][pl.ds(me[0], 1), :].astype(F32)
        column = jnp.broadcast_to(row, (8, row.shape[1])).T[:, :1]
        rows = pl.ds(s * per_owner, per_owner)
        lent_hot[rows, :] = jnp.where(columns == column[:per_owner], 1.0, 0.0).astype(BF16)
        kept_hot[rows, :] = jnp.where(
            columns == column[per_owner : 2 * per_owner], 1.0, 0.0
        ).astype(BF16)
    got = dot(lent_hot[...], edges[...]).astype(BF16)
    for s in range(ranks):
        outs[s][...] = got[s * per_owner : (s + 1) * per_owner]


def owner_kernel(kept_hot, upstream, w_out, same, dhidden):
    hot = kept_hot[...]
    same[...] = dot(hot, hot, NT).astype(BF16)
    picked = dot(hot, upstream[...]).astype(BF16)
    dhidden[...] = dot(picked, w_out[...], NT)


def gathered(pieces):
    return jnp.concatenate([p[...] for p in pieces], axis=0)


def forward_kernel(ranks, step, *refs):
    pieces, (filt, s_hot, d_hot) = refs[:ranks], refs[ranks : ranks + 3]
    outs, total = refs[ranks + 3 : 2 * ranks + 3], refs[2 * ranks + 3]
    table = gathered(pieces).T
    total[...] = jnp.zeros_like(total)

    def turn(i, carry):
        at = pl.ds(pl.multiple_of(i * step, step), step)
        rows = dot(table, s_hot[:, at]).astype(BF16)
        total[...] += dot(rows * filt[:, at], d_hot[:, at], NT)
        return carry

    lax.fori_loop(0, filt.shape[1] // step, turn, 0)
    result = total[...].astype(BF16).T
    per = result.shape[0] // ranks
    for s in range(ranks):
        outs[s][...] = result[s * per : (s + 1) * per]


def slope_kernel(ranks, step, *refs):
    pieces, (slope, s_hot, out) = refs[:ranks], refs[ranks:]
    table = gathered(pieces).T

    def turn(i, carry):
        at = pl.ds(pl.multiple_of(i * step, step), step)
        out[:, at] = dot(table, s_hot[:, at]).astype(BF16) * slope[:, at]
        return carry

    lax.fori_loop(0, slope.shape[1] // step, turn, 0)


def return_kernel(ranks, *refs):
    pieces, (same, dhidden) = refs[:ranks], refs[ranks : ranks + 2]
    outs = refs[ranks + 2 :]
    agg = dot(same[...], gathered(pieces))
    back = (dhidden[...] * silu_parts(agg)[1]).astype(BF16)
    per = back.shape[0] // ranks
    for s in range(ranks):
        outs[s][...] = back[s * per : (s + 1) * per]


def update_kernel(ranks, step, *refs):
    pieces = refs[:ranks]
    kept_hot, edges, upstream, w_out, updated, term, hot_t = refs[ranks:]
    home = gathered(pieces)
    hot_t[...] = kept_hot[...].T
    term[...] = jnp.zeros_like(term)
    for i in range(edges.shape[0] // step):
        at = pl.ds(i * step, step)
        agg = dot(hot_t[at, :], home)
        hidden = silu_parts(agg)[0].astype(BF16)
        fresh = edges[at, :].astype(F32) + dot(hidden, w_out[...])
        updated[at, :] = fresh.astype(BF16)
        term[...] += dot(hidden.T, upstream[at, :])


def backward_kernel(ranks, step, *refs):
    pieces, (filt, slope, s_hot, d_hot, basis) = refs[:ranks], refs[ranks : ranks + 5]
    outs = refs[ranks + 5 : 2 * ranks + 5]
    weight, total, dweight = refs[2 * ranks + 5 :]
    table = gathered(pieces).T
    total[...] = jnp.zeros_like(total)
    dweight[...] = jnp.zeros_like(dweight)

    def turn(i, carry):
        at = pl.ds(pl.multiple_of(i * step, step), step)
        rows = dot(table, d_hot[:, at]).astype(BF16)
        dweight[...] += dot(rows * slope[:, at], basis[at, :])
        total[...] += dot(rows * filt[:, at], s_hot[:, at], NT)
        return carry

    lax.fori_loop(0, filt.shape[1] // step, turn, 0)
    weight[...] = dweight[...].T
    result = total[...].astype(BF16).T
    per = result.shape[0] // ranks
    for s in range(ranks):
        outs[s][...] = result[s * per : (s + 1) * per]


def final_kernel(ranks, step, *refs):
    pieces, (lent_hot, upstream, out, hot_t) = refs[:ranks], refs[ranks:]
    back = gathered(pieces)
    hot_t[...] = lent_hot[...].T
    for i in range(upstream.shape[0] // step):
        at = pl.ds(i * step, step)
        out[at, :] = (upstream[at, :].astype(F32) + dot(hot_t[at, :], back)).astype(BF16)


def shift(value, axis, by):
    count = lax.axis_size(axis)
    return lax.ppermute(value, axis, [(k, (k + by) % count) for k in range(count)])


def spread(pieces, axis, sign):
    return [pieces[0]] + [shift(pieces[s], axis, sign * s) for s in range(1, len(pieces))]


def reduce_all(term):
    copies, ranks = lax.axis_size("dp"), lax.axis_size("graph")
    mine, me = lax.axis_index("dp"), lax.axis_index("graph")
    bits = copies.bit_length() - 1
    value = term
    for bit in range(bits):
        half = value.reshape(2, value.shape[0] // 2, value.shape[1])
        own = (mine >> bit) & 1
        away = lax.dynamic_index_in_dim(half, 1 - own, 0, keepdims=False).astype(BF16)
        got = lax.ppermute(away, "dp", [(k, k ^ (1 << bit)) for k in range(copies)])
        value = lax.dynamic_index_in_dim(half, own, 0, keepdims=False) + got.astype(F32)
    parts = value.reshape(ranks, value.shape[0] // ranks, value.shape[1])
    total = lax.dynamic_index_in_dim(parts, me, 0, keepdims=False)
    for s in range(1, ranks):
        away = lax.dynamic_index_in_dim(parts, (me + s) % ranks, 0, keepdims=False)
        total = total + shift(away.astype(BF16), "graph", s).astype(F32)
    piece = total.astype(BF16)
    ring = [piece] + [shift(piece, "graph", -s) for s in range(1, ranks)]
    twice = jnp.concatenate(ring + ring, axis=0)
    rows = piece.shape[0]
    value = lax.dynamic_slice_in_dim(twice, ((ranks - me) % ranks) * rows, ranks * rows, 0)
    for bit in reversed(range(bits)):
        got = lax.ppermute(value, "dp", [(k, k ^ (1 << bit)) for k in range(copies)])
        low = ((mine >> bit) & 1) == 0
        value = jnp.where(low, jnp.concatenate([value, got]), jnp.concatenate([got, value]))
    return value.astype(F32)


def per_device(
    edge_emb,
    cotangent,
    fetch_rows,
    store_rows,
    trip_src,
    trip_dst,
    trip_basis,
    block_count,
    w_basis,
    w_out,
):
    edges, upstream, basis = edge_emb[0], cotangent[0], trip_basis[0]
    ranks, copies = lax.axis_size("graph"), lax.axis_size("dp")
    me = lax.axis_index("graph").astype(jnp.int32).reshape(1)
    edge_dev, width = edges.shape
    per_owner = fetch_rows.shape[3]
    slots = ranks * per_owner
    blocks, block_rows = trip_src.shape[1:]
    triplets, basis_width = basis.shape
    piece = shape((per_owner, width))
    step = 512
    wide = 2 * triplets * slots * width

    both = jnp.concatenate([fetch_rows[0, 0], store_rows[0, 0]], axis=1)
    lists = [both] + [shift(both, "graph", s) for s in range(1, ranks)]

    filt, slope, s_hot, d_hot = call(
        functools.partial(prepare_kernel, per_owner, ranks, step),
        [shape((width, triplets))] * 2 + [shape((slots, triplets))] * 2,
        [me, block_count, trip_src[0], trip_dst[0], basis, w_basis],
        [SMEM, SMEM] + [VMEM] * 4,
        flops=6 * triplets * width * basis_width,
    )

    *lend, lent_hot, kept_hot = call(
        functools.partial(lend_kernel, per_owner, ranks),
        [piece] * ranks + [shape((slots, edge_dev))] * 2,
        [me] + lists + [edges],
        [SMEM] + [VMEM] * (ranks + 1),
        flops=2 * slots * edge_dev * width,
    )
    rows = spread(lend, "graph", -1)

    same, dhidden = call(
        owner_kernel,
        [shape((slots, slots)), shape((slots, width), F32)],
        [kept_hot, upstream, w_out],
        flops=4 * slots * edge_dev * width,
    )

    partial_rows = call(
        functools.partial(forward_kernel, ranks, step),
        [piece] * ranks,
        list(rows) + [filt, s_hot, d_hot],
        flops=2 * wide,
        scratch=[pltpu.VMEM((width, slots), F32)],
    )
    home = spread(partial_rows, "graph", 1)

    (weighted,) = call(
        functools.partial(slope_kernel, ranks, step),
        [shape((width, triplets))],
        list(rows) + [slope, s_hot],
        flops=wide,
    )

    back = call(
        functools.partial(return_kernel, ranks),
        [piece] * ranks,
        list(home) + [same, dhidden],
        flops=2 * slots * slots * width,
    )
    dpartial = spread(back, "graph", -1)

    updated, out_term = call(
        functools.partial(update_kernel, ranks, 256),
        [shape((edge_dev, width)), shape((width, width), F32)],
        list(home) + [kept_hot, edges, upstream, w_out],
        flops=2 * edge_dev * width * (2 * width + slots),
        scratch=[pltpu.VMEM((edge_dev, slots), BF16)],
    )
    out_scale = jnp.sqrt(F32(copies * ranks * edge_dev))
    grad_w_out = reduce_all(out_term) / out_scale

    *dfetch, basis_term = call(
        functools.partial(backward_kernel, ranks, step),
        [piece] * ranks + [shape((basis_width, width), F32)],
        list(dpartial) + [filt, weighted, s_hot, d_hot, basis],
        flops=2 * wide,
        scratch=[pltpu.VMEM((width, slots), F32), pltpu.VMEM((width, basis_width), F32)],
    )
    basis_scale = jnp.sqrt(F32(copies * ranks * blocks * block_rows))
    grad_w_basis = reduce_all(basis_term) / basis_scale
    returned = spread(dfetch, "graph", 1)

    (grad_edge,) = call(
        functools.partial(final_kernel, ranks, 256),
        [shape((edge_dev, width))],
        list(returned) + [lent_hot, upstream],
        flops=2 * slots * edge_dev * width,
        scratch=[pltpu.VMEM((edge_dev, slots), BF16)],
    )
    return (updated[None], grad_edge[None], grad_w_out, grad_w_basis)


def solution(mesh):
    placed = (
        P(("groups", "dp"), "graph", None),
        P(("groups", "dp"), "graph", None),
        P(("groups", "dp"), "graph", None, None),
        P(("groups", "dp"), "graph", None, None),
        P(("groups", "dp"), "graph", None),
        P(("groups", "dp"), "graph", None),
        P(("groups", "dp"), "graph", None),
        P(("groups", "dp"), "graph"),
        P(),
        P(),
    )
    return jax.shard_map(
        per_device,
        mesh=mesh,
        in_specs=placed,
        out_specs=(
            P(("groups", "dp"), "graph", None),
            P(("groups", "dp"), "graph", None),
            P("groups", None),
            P("groups", None),
        ),
        check_vma=False,
    )
```

```python
import functools

import jax
import jax.numpy as jnp
from jax import lax
from jax.experimental import pallas as pl
from jax.experimental.pallas import tpu as pltpu
from jax.sharding import PartitionSpec as P

BF16 = jnp.bfloat16
F32 = jnp.float32
VMEM = pl.BlockSpec(memory_space=pltpu.VMEM)
SMEM = pl.BlockSpec(memory_space=pltpu.SMEM)
ANY = pl.BlockSpec(memory_space=pl.ANY)
NN = (((1,), (0,)), ((), ()))
NT = (((1,), (1,)), ((), ()))


def dot(a, b, dims=NN):
    return lax.dot_general(a, b, dims, preferred_element_type=F32)


def silu_parts(value):
    sig = 0.5 * jnp.tanh(0.5 * value) + 0.5
    act = value * sig
    return act, sig + act * (1.0 - sig)


def call(body, outs, args, flops=0, scratch=(), vmem=20, smem=(), order=()):
    args = list(args) + list(order)
    moved = sum(a.size * a.dtype.itemsize for a in args) + sum(
        o.size * o.dtype.itemsize for o in outs
    )
    keep = len(args) - len(order)
    specs = [SMEM if i in smem else VMEM if i < keep else ANY for i in range(len(args))]

    def inner(*refs):
        body(*refs[:keep], *refs[len(args) :])

    return pl.pallas_call(
        inner if order else body,
        out_shape=tuple(outs),
        in_specs=specs,
        out_specs=tuple([VMEM] * len(outs)),
        scratch_shapes=list(scratch),
        cost_estimate=pl.CostEstimate(flops=flops, bytes_accessed=moved, transcendentals=0),
        compiler_params=pltpu.CompilerParams(vmem_limit_bytes=vmem << 20),
    )(*args)


def shape(dims, dtype=BF16):
    return jax.ShapeDtypeStruct(dims, dtype)


def prepare_kernel(step, count, src, dst, basis, weight, filt, s_hot, d_hot):
    blocks, block = src.shape
    slots = s_hot.shape[0]
    weight_t = weight[...].T
    rows = lax.broadcasted_iota(jnp.int32, (slots, block), 0)
    for i in range(basis.shape[0] // step):
        at = pl.ds(i * step, step)
        filt[:, at] = silu_parts(dot(weight_t, basis[at, :], NT))[0].astype(BF16)
    for b in range(blocks):
        at = pl.ds(b * block, block)
        s_hot[:, at] = jnp.where(rows == src[pl.ds(b, 1), :], 1.0, 0.0).astype(BF16)
        slot = jnp.where(b < count[0, 0], dst[pl.ds(b, 1), :], -1)
        d_hot[:, at] = jnp.where(rows == slot, 1.0, 0.0).astype(BF16)


def lend_kernel(lists, edges, out, lent_hot, kept_hot):
    ranks, per_owner = lists.shape[0], lists.shape[1] // 2
    edge_dev = edges.shape[0]
    columns = lax.broadcasted_iota(jnp.int32, (per_owner, edge_dev), 1).astype(F32)
    for s in range(ranks):
        row = lists[pl.ds(s, 1), :].astype(F32)
        column = jnp.broadcast_to(row, (8, row.shape[1])).T[:, :1]
        rows = pl.ds(s * per_owner, per_owner)
        lent_hot[rows, :] = jnp.where(columns == column[:per_owner], 1.0, 0.0).astype(BF16)
        kept_hot[rows, :] = jnp.where(columns == column[per_owner:], 1.0, 0.0).astype(BF16)
    out[...] = dot(lent_hot[...], edges[...]).astype(BF16)


def owner_kernel(kept_hot, upstream, w_out, same, dhidden):
    hot = kept_hot[...]
    same[...] = dot(hot, hot, NT).astype(BF16)
    picked = dot(hot, upstream[...]).astype(BF16)
    dhidden[...] = dot(picked, w_out[...], NT)


def forward_kernel(step, fetched, filt, s_hot, d_hot, out, message):
    table = fetched[...].T
    for i in range(filt.shape[1] // step):
        at = pl.ds(i * step, step)
        message[:, at] = dot(table, s_hot[:, at]).astype(BF16) * filt[:, at]
    out[...] = dot(d_hot[...], message[...], NT).astype(BF16)


def slope_kernel(step, fetched, s_hot, basis, weight, out):
    table = fetched[...].T
    weight_t = weight[...].T
    for i in range(out.shape[1] // step):
        at = pl.ds(i * step, step)
        slope = silu_parts(dot(weight_t, basis[at, :], NT))[1]
        out[:, at] = (dot(table, s_hot[:, at]) * slope).astype(BF16)


def return_kernel(home, same, dhidden, out):
    agg = dot(same[...], home[...])
    out[...] = (dhidden[...] * silu_parts(agg)[1]).astype(BF16)


def update_kernel(step, home, kept_hot, edges, upstream, w_out, updated, term, hot_t, hidden):
    hot_t[...] = kept_hot[...].T
    rows = edges.shape[0]
    for i in range(rows // step):
        at = pl.ds(i * step, step)
        fresh = silu_parts(dot(hot_t[at, :], home[...]))[0].astype(BF16)
        hidden[:, at] = fresh.T
        updated[at, :] = (edges[at, :].astype(F32) + dot(fresh, w_out[...])).astype(BF16)
    term[...] = dot(hidden[...], upstream[...])


def weight_kernel(step, rows_in, filt, weighted, d_hot, basis, weight, dmessage, dpre):
    table = rows_in[...].T
    for i in range(filt.shape[1] // step):
        at = pl.ds(i * step, step)
        rows = dot(table, d_hot[:, at]).astype(BF16)
        dpre[:, at] = rows * weighted[:, at]
        dmessage[:, at] = rows * filt[:, at]
    weight[...] = dot(dpre[...], basis[...]).T


def source_kernel(dmessage, s_hot, out):
    out[...] = dot(s_hot[...], dmessage[...], NT).astype(BF16)


def final_kernel(step, back, lent_hot, upstream, out, hot_t):
    hot_t[...] = lent_hot[...].T
    for i in range(upstream.shape[0] // step):
        at = pl.ds(i * step, step)
        out[at, :] = (upstream[at, :].astype(F32) + dot(hot_t[at, :], back[...])).astype(BF16)


def swap(value, axis, mask):
    return lax.ppermute(value, axis, [(k, k ^ mask) for k in range(lax.axis_size(axis))])


def exchange(value):
    return lax.all_to_all(value, "graph", split_axis=0, concat_axis=0, tiled=True)


def halve(value, mine, bit):
    half = value.reshape(2, value.shape[0] // 2, value.shape[1])
    own = (mine >> bit) & 1
    away = lax.dynamic_index_in_dim(half, 1 - own, 0, keepdims=False).astype(BF16)
    kept = lax.dynamic_index_in_dim(half, own, 0, keepdims=False)
    return kept + swap(away, "dp", 1 << bit).astype(F32)


def double(value, mine, bit):
    got = swap(value, "dp", 1 << bit)
    low = ((mine >> bit) & 1) == 0
    return jnp.where(low, jnp.concatenate([value, got]), jnp.concatenate([got, value]))


def reduce_large(term):
    copies, ranks = lax.axis_size("dp"), lax.axis_size("graph")
    mine, me = lax.axis_index("dp"), lax.axis_index("graph")
    bits = range(copies.bit_length() - 1)
    value = term
    for bit in bits:
        value = halve(value, mine, bit)
    parts = value.reshape(ranks, value.shape[0] // ranks, value.shape[1])
    total = lax.dynamic_index_in_dim(parts, me, 0, keepdims=False)
    for s in range(1, ranks):
        away = lax.dynamic_index_in_dim(parts, me ^ s, 0, keepdims=False)
        total = total + swap(away.astype(BF16), "graph", s).astype(F32)
    piece = total.astype(BF16)
    value = jnp.zeros((ranks,) + piece.shape, BF16)
    for s in range(ranks):
        got = swap(piece, "graph", s) if s else piece
        value = lax.dynamic_update_index_in_dim(value, got, me ^ s, 0)
    value = value.reshape(-1, piece.shape[1])
    for bit in reversed(bits):
        value = double(value, mine, bit)
    return value.astype(F32)


def reduce_small(term):
    copies, ranks = lax.axis_size("dp"), lax.axis_size("graph")
    mine = lax.axis_index("dp")
    value = halve(term, mine, 0)
    for bit in range(1, copies.bit_length() - 1):
        own = value.astype(BF16)
        value = own.astype(F32) + swap(own, "dp", 1 << bit).astype(F32)
    own = value.astype(BF16)
    level = [own.astype(F32)] + [swap(own, "graph", s).astype(F32) for s in range(1, ranks)]
    while len(level) > 1:
        level = [level[k] + level[k + 1] for k in range(0, len(level), 2)]
    return double(level[0].astype(BF16), mine, 0).astype(F32)


def per_device(
    edge_emb,
    cotangent,
    fetch_rows,
    store_rows,
    trip_src,
    trip_dst,
    trip_basis,
    block_count,
    w_basis,
    w_out,
):
    edges, upstream, basis = edge_emb[0], cotangent[0], trip_basis[0]
    ranks, copies = lax.axis_size("graph"), lax.axis_size("dp")
    edge_dev, width = edges.shape
    slots = ranks * fetch_rows.shape[3]
    blocks, block_rows = trip_src.shape[1:]
    triplets, basis_width = basis.shape
    table = shape((slots, width))
    plane = shape((width, triplets))
    hot = shape((slots, triplets))
    step = 512
    wide = 2 * triplets * slots * width
    narrow = 2 * triplets * basis_width * width

    lists = exchange(jnp.concatenate([fetch_rows[0, 0], store_rows[0, 0]], axis=1))
    filt, s_hot, d_hot = call(
        functools.partial(prepare_kernel, step),
        [plane, hot, hot],
        [block_count, trip_src[0], trip_dst[0], basis, w_basis],
        flops=8 * narrow,
        smem=(0,),
    )
    lend, lent_hot, kept_hot = call(
        lend_kernel,
        [table] + [shape((slots, edge_dev))] * 2,
        [lists, edges],
        flops=2 * slots * edge_dev * width,
    )
    fetched = exchange(lend)
    same, dhidden = call(
        owner_kernel,
        [shape((slots, slots)), shape((slots, width), F32)],
        [kept_hot, upstream, w_out],
        flops=4 * slots * edge_dev * width,
    )
    (partial_rows,) = call(
        functools.partial(forward_kernel, step),
        [table],
        [fetched, filt, s_hot, d_hot],
        flops=2 * wide,
        scratch=[pltpu.VMEM(plane.shape, BF16)],
    )
    home = exchange(partial_rows)
    (weighted,) = call(
        functools.partial(slope_kernel, step),
        [plane],
        [fetched, s_hot, basis, w_basis],
        flops=wide + 8 * narrow,
    )
    (back,) = call(
        return_kernel,
        [table],
        [home, same, dhidden],
        flops=2 * slots * slots * width,
        order=[weighted],
    )
    dpartial = exchange(back)
    updated, out_term = call(
        functools.partial(update_kernel, 256),
        [shape((edge_dev, width)), shape((width, width), F32)],
        [home, kept_hot, edges, upstream, w_out],
        flops=2 * edge_dev * width * (2 * width + slots),
        scratch=[pltpu.VMEM((edge_dev, slots), BF16), pltpu.VMEM((width, edge_dev), BF16)],
    )
    out_scale = jnp.sqrt(F32(copies * ranks * edge_dev))
    grad_w_out = reduce_large(out_term) / out_scale
    basis_term, dmessage = call(
        functools.partial(weight_kernel, step),
        [shape((basis_width, width), F32), plane],
        [dpartial, filt, weighted, d_hot, basis],
        flops=wide + narrow,
        scratch=[pltpu.VMEM(plane.shape, BF16)],
        order=[out_term],
    )
    basis_scale = jnp.sqrt(F32(copies * ranks * blocks * block_rows))
    grad_w_basis = reduce_small(basis_term) / basis_scale
    (dfetch,) = call(source_kernel, [table], [dmessage, s_hot], flops=wide)
    (grad_edge,) = call(
        functools.partial(final_kernel, 256),
        [shape((edge_dev, width))],
        [exchange(dfetch), lent_hot, upstream],
        flops=2 * slots * edge_dev * width,
        scratch=[pltpu.VMEM((edge_dev, slots), BF16)],
    )
    return (updated[None], grad_edge[None], grad_w_out, grad_w_basis)


def solution(mesh):
    placed = (
        P(("groups", "dp"), "graph", None),
        P(("groups", "dp"), "graph", None),
        P(("groups", "dp"), "graph", None, None),
        P(("groups", "dp"), "graph", None, None),
        P(("groups", "dp"), "graph", None),
        P(("groups", "dp"), "graph", None),
        P(("groups", "dp"), "graph", None),
        P(("groups", "dp"), "graph"),
        P(),
        P(),
    )
    return jax.shard_map(
        per_device,
        mesh=mesh,
        in_specs=placed,
        out_specs=(
            P(("groups", "dp"), "graph", None),
            P(("groups", "dp"), "graph", None),
            P("groups", None),
            P("groups", None),
        ),
        check_vma=False,
    )
```

```python
import functools

import jax
import jax.numpy as jnp
from jax import lax
from jax.experimental import pallas as pl
from jax.experimental.pallas import tpu as pltpu
from jax.sharding import PartitionSpec as P

BF16 = jnp.bfloat16
F32 = jnp.float32
VMEM = pl.BlockSpec(memory_space=pltpu.VMEM)
SMEM = pl.BlockSpec(memory_space=pltpu.SMEM)
ANY = pl.BlockSpec(memory_space=pl.ANY)
NN = (((1,), (0,)), ((), ()))
NT = (((1,), (1,)), ((), ()))


def dot(a, b, dims=NN):
    return lax.dot_general(a, b, dims, preferred_element_type=F32)


def silu_parts(value):
    sig = 0.5 * jnp.tanh(0.5 * value) + 0.5
    act = value * sig
    return act, sig + act * (1.0 - sig)


def call(body, outs, args, flops=0, scratch=(), smem=(), far=(), far_out=(), order=()):
    args = list(args) + list(order)
    moved = sum(a.size * a.dtype.itemsize for a in args) + sum(
        o.size * o.dtype.itemsize for o in outs
    )
    keep = len(args) - len(order)
    specs = [
        SMEM if i in smem else ANY if i in far or i >= keep else VMEM for i in range(len(args))
    ]

    def inner(*refs):
        body(*refs[:keep], *refs[len(args) :])

    return pl.pallas_call(
        inner if order else body,
        out_shape=tuple(outs),
        in_specs=specs,
        out_specs=tuple(ANY if i in far_out else VMEM for i in range(len(outs))),
        scratch_shapes=list(scratch),
        cost_estimate=pl.CostEstimate(flops=flops, bytes_accessed=moved, transcendentals=0),
        compiler_params=pltpu.CompilerParams(vmem_limit_bytes=58 << 20),
    )(*args)


def shape(dims, dtype=BF16):
    return jax.ShapeDtypeStruct(dims, dtype)


def held(array):
    return pltpu.VMEM(array.shape, array.dtype)


def lane_copies(source, target, sems, step):
    return [
        pltpu.make_async_copy(
            source.at[:, pl.ds(i * step, step)], target.at[:, pl.ds(i * step, step)], sems.at[i]
        )
        for i in range(target.shape[1] // step)
    ]


def started(copies):
    for copy in copies:
        copy.start()
    return copies


def hot_lanes(index, first, count, slots, dead=None):
    block = index.shape[1]
    rows = lax.broadcasted_iota(jnp.int32, (slots, block), 0)
    parts = []
    for b in range(first, first + count):
        slot = index[pl.ds(b, 1), :]
        if dead is not None:
            slot = jnp.where(b < dead, slot, -1)
        parts.append(jnp.where(rows == slot, 1.0, 0.0).astype(BF16))
    return jnp.concatenate(parts, axis=1)


def turned(index, per_owner, ranks, me):
    slot = index[...] - me * per_owner
    return jnp.where(slot < 0, slot + ranks * per_owner, slot)


def gathered(pieces):
    return jnp.concatenate([p[...] for p in pieces], axis=0)


def scattered(value, outs):
    per = outs[0].shape[0]
    for s, out in enumerate(outs):
        out[...] = value[s * per : (s + 1) * per]


def columns_of(lists, me, kept, per_owner):
    parts = []
    for ref in lists:
        row = ref[pl.ds(me, 1), :].astype(F32)
        column = jnp.broadcast_to(row, (8, row.shape[1])).T[:, :1]
        parts.append(column[per_owner : 2 * per_owner] if kept else column[:per_owner])
    return jnp.concatenate(parts, axis=0)


def hot_rows(column, edge_dev):
    edges = lax.broadcasted_iota(jnp.int32, (column.shape[0], edge_dev), 1).astype(F32)
    return jnp.where(column == edges, 1.0, 0.0).astype(BF16)


def prepare_kernel(step, basis, weight, filt, buffer, sems):
    weight_t = weight[...].T
    leave = lane_copies(buffer, filt, sems, step)
    for i, copy in enumerate(leave):
        at = pl.ds(i * step, step)
        buffer[:, at] = silu_parts(dot(weight_t, basis[at, :], NT))[0].astype(BF16)
        copy.start()
    for copy in leave:
        copy.wait()


def lend_kernel(ranks, me, *refs):
    lists, edges, outs = refs[:ranks], refs[ranks], refs[ranks + 1 :]
    column = columns_of(lists, me[0], False, outs[0].shape[0])
    scattered(dot(hot_rows(column, edges.shape[0]), edges[...]).astype(BF16), outs)


def owner_kernel(ranks, me, *refs):
    lists, (upstream, w_out, same, dhidden) = refs[:ranks], refs[ranks:]
    hot = hot_rows(columns_of(lists, me[0], True, same.shape[0] // ranks), upstream.shape[0])
    same[...] = dot(hot, hot, NT).astype(BF16)
    dhidden[...] = dot(dot(hot, upstream[...]).astype(BF16), w_out[...], NT)


def forward_kernel(ranks, step, me, count, *refs):
    pieces, (src, dst, filt) = refs[:ranks], refs[ranks : ranks + 3]
    outs = refs[ranks + 3 : 2 * ranks + 3]
    filt_v, message, total, sems = refs[2 * ranks + 3 :]
    arrive = started(lane_copies(filt, filt_v, sems, step))
    per_owner = outs[0].shape[0]
    slots, block = ranks * per_owner, src.shape[1]
    table = gathered(pieces).T
    src_t = turned(src, per_owner, ranks, me[0])
    dst_t = turned(dst, per_owner, ranks, me[0])
    each = step // block
    for i, copy in enumerate(arrive):
        at = pl.ds(i * step, step)
        rows = dot(table, hot_lanes(src_t, i * each, each, slots)).astype(BF16)
        copy.wait()
        message[:, at] = rows * filt_v[:, at]
    hot = hot_lanes(dst_t, 0, src.shape[0], slots, count[0, 0])
    total[...] = dot(hot, message[...], NT)
    scattered(total[...].astype(BF16), outs)


def slope_kernel(ranks, step, me, *refs):
    pieces, (src, basis, weight, out, buffer, sems) = refs[:ranks], refs[ranks:]
    per_owner = pieces[0].shape[0]
    slots, block = ranks * per_owner, src.shape[1]
    table = gathered(pieces).T
    weight_t = weight[...].T
    src_t = turned(src, per_owner, ranks, me[0])
    each = step // block
    leave = lane_copies(buffer, out, sems, step)
    for i, copy in enumerate(leave):
        at = pl.ds(i * step, step)
        slope = silu_parts(dot(weight_t, basis[at, :], NT))[1]
        rows = dot(table, hot_lanes(src_t, i * each, each, slots))
        buffer[:, at] = (rows * slope).astype(BF16)
        copy.start()
    for copy in leave:
        copy.wait()


def return_kernel(ranks, *refs):
    pieces, (same, dhidden), outs = refs[:ranks], refs[ranks : ranks + 2], refs[ranks + 2 :]
    agg = dot(same[...], gathered(pieces))
    scattered((dhidden[...] * silu_parts(agg)[1]).astype(BF16), outs)


def update_kernel(ranks, step, me, *refs):
    lists, pieces = refs[:ranks], refs[ranks : 2 * ranks]
    edges, upstream, w_out, updated, term, hot_t, hidden = refs[2 * ranks :]
    home = gathered(pieces)
    rows = edges.shape[0]
    hot_t[...] = hot_rows(columns_of(lists, me[0], True, pieces[0].shape[0]), rows).T
    for i in range(rows // step):
        at = pl.ds(i * step, step)
        fresh = silu_parts(dot(hot_t[at, :], home))[0].astype(BF16)
        hidden[:, at] = fresh.T
        updated[at, :] = (edges[at, :].astype(F32) + dot(fresh, w_out[...])).astype(BF16)
    term[...] = dot(hidden[...], upstream[...])


def weight_kernel(ranks, step, me, count, *refs):
    pieces, (dst, filt, weighted, basis) = refs[:ranks], refs[ranks : ranks + 4]
    weight, dmessage, filt_v, weighted_v, dpre, sems = refs[ranks + 4 :]
    arrive = started(lane_copies(weighted, weighted_v, sems.at[0], step))
    arrive_filt = started(lane_copies(filt, filt_v, sems.at[1], step))
    per_owner = pieces[0].shape[0]
    slots, block = ranks * per_owner, dst.shape[1]
    table = gathered(pieces).T
    dst_t = turned(dst, per_owner, ranks, me[0])
    each = step // block
    for i in range(len(arrive)):
        at = pl.ds(i * step, step)
        rows = dot(table, hot_lanes(dst_t, i * each, each, slots, count[0, 0])).astype(BF16)
        arrive[i].wait()
        dpre[:, at] = rows * weighted_v[:, at]
        arrive_filt[i].wait()
        dmessage[:, at] = rows * filt_v[:, at]
    weight[...] = dot(dpre[...], basis[...]).T


def source_kernel(ranks, me, src, dmessage, *outs):
    per_owner = outs[0].shape[0]
    src_t = turned(src, per_owner, ranks, me[0])
    hot = hot_lanes(src_t, 0, src.shape[0], ranks * per_owner)
    scattered(dot(hot, dmessage[...], NT).astype(BF16), outs)


def final_kernel(ranks, step, me, *refs):
    lists, pieces = refs[:ranks], refs[ranks : 2 * ranks]
    upstream, out, hot_t = refs[2 * ranks :]
    back = gathered(pieces)
    rows = upstream.shape[0]
    hot_t[...] = hot_rows(columns_of(lists, me[0], False, pieces[0].shape[0]), rows).T
    for i in range(rows // step):
        at = pl.ds(i * step, step)
        out[at, :] = (upstream[at, :].astype(F32) + dot(hot_t[at, :], back)).astype(BF16)


def swap(value, axis, mask):
    return lax.ppermute(value, axis, [(k, k ^ mask) for k in range(lax.axis_size(axis))])


def shift(value, axis, by):
    count = lax.axis_size(axis)
    return lax.ppermute(value, axis, [(k, (k + by) % count) for k in range(count)])


def exchange(pieces, sign):
    return [pieces[0]] + [shift(pieces[s], "graph", sign * s) for s in range(1, len(pieces))]


def halve(value, mine, bit):
    half = value.reshape(2, value.shape[0] // 2, value.shape[1])
    own = (mine >> bit) & 1
    away = lax.dynamic_index_in_dim(half, 1 - own, 0, keepdims=False).astype(BF16)
    kept = lax.dynamic_index_in_dim(half, own, 0, keepdims=False)
    return kept + swap(away, "dp", 1 << bit).astype(F32)


def double(value, mine, bit):
    got = swap(value, "dp", 1 << bit)
    low = ((mine >> bit) & 1) == 0
    return jnp.where(low, jnp.concatenate([value, got]), jnp.concatenate([got, value]))


def reduce_large(term):
    copies, ranks = lax.axis_size("dp"), lax.axis_size("graph")
    mine, me = lax.axis_index("dp"), lax.axis_index("graph")
    bits = range(copies.bit_length() - 1)
    value = term
    for bit in bits:
        value = halve(value, mine, bit)
    parts = value.reshape(ranks, value.shape[0] // ranks, value.shape[1])
    total = lax.dynamic_index_in_dim(parts, me, 0, keepdims=False)
    for s in range(1, ranks):
        away = lax.dynamic_index_in_dim(parts, me ^ s, 0, keepdims=False)
        total = total + swap(away.astype(BF16), "graph", s).astype(F32)
    piece = total.astype(BF16)
    value = jnp.zeros((ranks,) + piece.shape, BF16)
    for s in range(ranks):
        got = swap(piece, "graph", s) if s else piece
        value = lax.dynamic_update_index_in_dim(value, got, me ^ s, 0)
    value = value.reshape(-1, piece.shape[1])
    for bit in reversed(bits):
        value = double(value, mine, bit)
    return value.astype(F32)


def reduce_small(term):
    copies, ranks = lax.axis_size("dp"), lax.axis_size("graph")
    mine = lax.axis_index("dp")
    value = halve(term, mine, 0)
    for bit in range(1, copies.bit_length() - 1):
        own = value.astype(BF16)
        value = own.astype(F32) + swap(own, "dp", 1 << bit).astype(F32)
    own = value.astype(BF16)
    level = [own.astype(F32)] + [swap(own, "graph", s).astype(F32) for s in range(1, ranks)]
    while len(level) > 1:
        level = [level[k] + level[k + 1] for k in range(0, len(level), 2)]
    return double(level[0].astype(BF16), mine, 0).astype(F32)


def per_device(
    edge_emb,
    cotangent,
    fetch_rows,
    store_rows,
    trip_src,
    trip_dst,
    trip_basis,
    block_count,
    w_basis,
    w_out,
):
    edges, upstream, basis = edge_emb[0], cotangent[0], trip_basis[0]
    ranks, copies = lax.axis_size("graph"), lax.axis_size("dp")
    me = lax.axis_index("graph").astype(jnp.int32).reshape(1)
    edge_dev, width = edges.shape
    per_owner = fetch_rows.shape[3]
    slots = ranks * per_owner
    blocks, block_rows = trip_src.shape[1:]
    triplets, basis_width = basis.shape
    src, dst = trip_src[0], trip_dst[0]
    pieces = [shape((per_owner, width))] * ranks
    plane = shape((width, triplets))
    step = 512
    turns = triplets // step
    wide = 2 * triplets * slots * width
    narrow = 2 * triplets * basis_width * width

    both = jnp.concatenate([fetch_rows[0, 0], store_rows[0, 0]], axis=1)
    lists = exchange([both] * ranks, 1)
    (filt,) = call(
        functools.partial(prepare_kernel, step),
        [plane],
        [basis, w_basis],
        flops=8 * narrow,
        far_out=(0,),
        scratch=[held(plane), pltpu.SemaphoreType.DMA((turns,))],
    )
    lend = call(
        functools.partial(lend_kernel, ranks),
        pieces,
        [me] + lists + [edges],
        smem=(0,),
        flops=2 * slots * edge_dev * width,
    )
    fetched = exchange(lend, -1)
    same, dhidden = call(
        functools.partial(owner_kernel, ranks),
        [shape((slots, slots)), shape((slots, width), F32)],
        [me] + lists + [upstream, w_out],
        smem=(0,),
        flops=4 * slots * edge_dev * width,
    )
    partial_rows = call(
        functools.partial(forward_kernel, ranks, step),
        pieces,
        [me, block_count] + fetched + [src, dst, filt],
        smem=(0, 1),
        far=(ranks + 4,),
        flops=2 * wide,
        scratch=[
            held(plane),
            held(plane),
            pltpu.VMEM((slots, width), F32),
            pltpu.SemaphoreType.DMA((turns,)),
        ],
    )
    home = exchange(partial_rows, 1)
    (weighted,) = call(
        functools.partial(slope_kernel, ranks, step),
        [plane],
        [me] + fetched + [src, basis, w_basis],
        smem=(0,),
        far_out=(0,),
        flops=wide + 8 * narrow,
        scratch=[held(plane), pltpu.SemaphoreType.DMA((turns,))],
    )
    back = call(
        functools.partial(return_kernel, ranks),
        pieces,
        home + [same, dhidden],
        flops=2 * slots * slots * width,
        order=[weighted],
    )
    dpartial = exchange(back, -1)
    updated, out_term = call(
        functools.partial(update_kernel, ranks, 256),
        [shape((edge_dev, width)), shape((width, width), F32)],
        [me] + lists + home + [edges, upstream, w_out],
        smem=(0,),
        flops=2 * edge_dev * width * (2 * width + slots),
        scratch=[pltpu.VMEM((edge_dev, slots), BF16), pltpu.VMEM((width, edge_dev), BF16)],
    )
    out_scale = jnp.sqrt(F32(copies * ranks * edge_dev))
    grad_w_out = reduce_large(out_term) / out_scale
    basis_term, dmessage = call(
        functools.partial(weight_kernel, ranks, step),
        [shape((basis_width, width), F32), plane],
        [me, block_count] + dpartial + [dst, filt, weighted, basis],
        smem=(0, 1),
        far=(ranks + 3, ranks + 4),
        flops=wide + narrow,
        scratch=[held(plane)] * 3 + [pltpu.SemaphoreType.DMA((2, turns))],
        order=[out_term],
    )
    basis_scale = jnp.sqrt(F32(copies * ranks * blocks * block_rows))
    grad_w_basis = reduce_small(basis_term) / basis_scale
    dfetch = call(
        functools.partial(source_kernel, ranks),
        pieces,
        [me, src, dmessage],
        smem=(0,),
        flops=wide,
    )
    (grad_edge,) = call(
        functools.partial(final_kernel, ranks, 256),
        [shape((edge_dev, width))],
        [me] + lists + exchange(dfetch, 1) + [upstream],
        smem=(0,),
        flops=2 * slots * edge_dev * width,
        scratch=[pltpu.VMEM((edge_dev, slots), BF16)],
    )
    return (updated[None], grad_edge[None], grad_w_out, grad_w_basis)


def solution(mesh):
    placed = (
        P(("groups", "dp"), "graph", None),
        P(("groups", "dp"), "graph", None),
        P(("groups", "dp"), "graph", None, None),
        P(("groups", "dp"), "graph", None, None),
        P(("groups", "dp"), "graph", None),
        P(("groups", "dp"), "graph", None),
        P(("groups", "dp"), "graph", None),
        P(("groups", "dp"), "graph"),
        P(),
        P(),
    )
    return jax.shard_map(
        per_device,
        mesh=mesh,
        in_specs=placed,
        out_specs=(
            P(("groups", "dp"), "graph", None),
            P(("groups", "dp"), "graph", None),
            P("groups", None),
            P("groups", None),
        ),
        check_vma=False,
    )
```

```python
import functools

import jax
import jax.numpy as jnp
from jax import lax
from jax.experimental import pallas as pl
from jax.experimental.pallas import tpu as pltpu
from jax.sharding import PartitionSpec as P

BF16 = jnp.bfloat16
F32 = jnp.float32
VMEM = pl.BlockSpec(memory_space=pltpu.VMEM)
SMEM = pl.BlockSpec(memory_space=pltpu.SMEM)
ANY = pl.BlockSpec(memory_space=pl.ANY)
NN = (((1,), (0,)), ((), ()))
NT = (((1,), (1,)), ((), ()))


def dot(a, b, dims=NN):
    return lax.dot_general(a, b, dims, preferred_element_type=F32)


def silu_parts(value):
    sig = 0.5 * jnp.tanh(0.5 * value) + 0.5
    act = value * sig
    return act, sig + act * (1.0 - sig)


def call(body, outs, args, flops=0, scratch=(), smem=(), far=(), far_out=(), order=()):
    args = list(args) + list(order)
    moved = sum(a.size * a.dtype.itemsize for a in args) + sum(
        o.size * o.dtype.itemsize for o in outs
    )
    keep = len(args) - len(order)
    specs = [
        SMEM if i in smem else ANY if i in far or i >= keep else VMEM for i in range(len(args))
    ]

    def inner(*refs):
        body(*refs[:keep], *refs[len(args) :])

    return pl.pallas_call(
        inner if order else body,
        out_shape=tuple(outs),
        in_specs=specs,
        out_specs=tuple(ANY if i in far_out else VMEM for i in range(len(outs))),
        scratch_shapes=list(scratch),
        cost_estimate=pl.CostEstimate(flops=flops, bytes_accessed=moved, transcendentals=0),
        compiler_params=pltpu.CompilerParams(vmem_limit_bytes=58 << 20),
    )(*args)


def shape(dims, dtype=BF16):
    return jax.ShapeDtypeStruct(dims, dtype)


def held(array):
    return pltpu.VMEM(array.shape, array.dtype)


def lane_copies(source, target, sems, step):
    return [
        pltpu.make_async_copy(
            source.at[:, pl.ds(i * step, step)], target.at[:, pl.ds(i * step, step)], sems.at[i]
        )
        for i in range(target.shape[1] // step)
    ]


def started(copies):
    for copy in copies:
        copy.start()
    return copies


def waited(copies):
    for copy in copies:
        copy.wait()


def loads(sources, targets, sems):
    return started(
        [pltpu.make_async_copy(a, b, sems.at[i]) for i, (a, b) in enumerate(zip(sources, targets))]
    )


def hot_lanes(index, first, count, slots, dead=None):
    block = index.shape[1]
    rows = lax.broadcasted_iota(jnp.int32, (slots, block), 0)
    parts = []
    for b in range(first, first + count):
        slot = index[pl.ds(b, 1), :]
        if dead is not None:
            slot = jnp.where(b < dead, slot, -1)
        parts.append(jnp.where(rows == slot, 1.0, 0.0).astype(BF16))
    return jnp.concatenate(parts, axis=1)


def turned(index, per_owner, ranks, me):
    slot = index[...] - me * per_owner
    return jnp.where(slot < 0, slot + ranks * per_owner, slot)


def gathered(pieces):
    return jnp.concatenate([p[...] for p in pieces], axis=0)


def scattered(value, outs):
    per = outs[0].shape[0]
    for s, out in enumerate(outs):
        out[...] = value[s * per : (s + 1) * per]


def columns_of(lists, me, kept, per_owner):
    parts = []
    for ref in lists:
        row = ref[pl.ds(me, 1), :].astype(F32)
        column = jnp.broadcast_to(row, (8, row.shape[1])).T[:, :1]
        parts.append(column[per_owner : 2 * per_owner] if kept else column[:per_owner])
    return jnp.concatenate(parts, axis=0)


def hot_rows(column, edge_dev):
    edges = lax.broadcasted_iota(jnp.int32, (column.shape[0], edge_dev), 1).astype(F32)
    return jnp.where(column == edges, 1.0, 0.0).astype(BF16)


def prepare_kernel(step, part, basis, weight, filt, slope, basis_v, filt_v, slope_v, in_sems, sems):
    rows = basis_v.shape[0]
    arrive = loads([basis.at[pl.ds(part * rows, rows), :]], [basis_v], in_sems)
    weight_t = weight[...].T
    waited(arrive)
    leave = lane_copies(filt_v, filt, sems.at[0], step), lane_copies(slope_v, slope, sems.at[1], step)
    for i in range(len(leave[0])):
        at = pl.ds(i * step, step)
        act, grad = silu_parts(dot(weight_t, basis_v[at, :], NT))
        filt_v[:, at] = act.astype(BF16)
        leave[0][i].start()
        slope_v[:, at] = grad.astype(BF16)
        leave[1][i].start()
    waited(leave[0] + leave[1])


def lend_kernel(ranks, me, *refs):
    lists, edges, outs = refs[:ranks], refs[ranks], refs[ranks + 1 : 2 * ranks + 1]
    edges_v, sems = refs[2 * ranks + 1 :]
    arrive = loads([edges], [edges_v], sems)
    hot = hot_rows(columns_of(lists, me[0], False, outs[0].shape[0]), edges.shape[0])
    waited(arrive)
    scattered(dot(hot, edges_v[...]).astype(BF16), outs)


def owner_kernel(ranks, me, *refs):
    lists, (upstream, w_out, same, dhidden) = refs[:ranks], refs[ranks : ranks + 4]
    upstream_v, w_out_v, sems = refs[ranks + 4 :]
    arrive = loads([upstream, w_out], [upstream_v, w_out_v], sems)
    hot = hot_rows(columns_of(lists, me[0], True, same.shape[0] // ranks), upstream.shape[0])
    same[...] = dot(hot, hot, NT).astype(BF16)
    waited(arrive)
    dhidden[...] = dot(dot(hot, upstream_v[...]).astype(BF16), w_out_v[...], NT)


def forward_kernel(ranks, step, me, count, *refs):
    pieces, (src, dst), filt = refs[:ranks], refs[ranks : ranks + 2], refs[ranks + 2 : ranks + 4]
    outs = refs[ranks + 4 : 2 * ranks + 4]
    filt_v, message, hot, sems = refs[2 * ranks + 4 :]
    half = filt[0].shape[1]
    arrive = loads(filt, [filt_v.at[:, pl.ds(i * half, half)] for i in range(2)], sems)
    per_owner = outs[0].shape[0]
    slots, block = ranks * per_owner, src.shape[1]
    table = gathered(pieces).T
    src_t = turned(src, per_owner, ranks, me[0])
    dst_t = turned(dst, per_owner, ranks, me[0])
    each = step // block
    spans = [pl.ds(i * step, step) for i in range(2 * half // step)]
    for i, at in enumerate(spans):
        message[:, at] = dot(table, hot_lanes(src_t, i * each, each, slots)).astype(BF16)
    for i, at in enumerate(spans):
        hot[:, at] = hot_lanes(dst_t, i * each, each, slots, count[0, 0])
    waited(arrive)
    for at in spans:
        message[:, at] = message[:, at] * filt_v[:, at]
    scattered(dot(hot[...], message[...], NT).astype(BF16), outs)


def return_kernel(ranks, *refs):
    pieces, (same, dhidden), outs = refs[:ranks], refs[ranks : ranks + 2], refs[ranks + 2 :]
    agg = dot(same[...], gathered(pieces))
    scattered((dhidden[...] * silu_parts(agg)[1]).astype(BF16), outs)


def update_kernel(ranks, step, me, *refs):
    lists, pieces = refs[:ranks], refs[ranks : 2 * ranks]
    edges, upstream, w_out, updated, term = refs[2 * ranks : 2 * ranks + 5]
    edges_v, upstream_v, w_out_v, updated_v, hidden, sems, out_sems = refs[2 * ranks + 5 :]
    arrive = loads([w_out, edges, upstream], [w_out_v, edges_v, upstream_v], sems)
    home = gathered(pieces)
    rows = edges.shape[0]
    hot_t = hot_rows(columns_of(lists, me[0], True, pieces[0].shape[0]), rows).T
    turns = rows // step
    spans = [pl.ds(i * step, step) for i in range(turns)]
    leave = [
        pltpu.make_async_copy(updated_v.at[at, :], updated.at[at, :], out_sems.at[i])
        for i, at in enumerate(spans)
    ]
    fresh = [
        silu_parts(dot(hot_t[i * step : (i + 1) * step], home))[0].astype(BF16) for i in range(turns)
    ]
    waited(arrive)
    for i, at in enumerate(spans):
        total = edges_v[at, :].astype(F32) + dot(fresh[i], w_out_v[...])
        updated_v[at, :] = total.astype(BF16)
        leave[i].start()
        hidden[:, at] = fresh[i].T
    term[...] = dot(hidden[...], upstream_v[...]).astype(BF16)
    waited(leave)


def backward_kernel(ranks, step, me, count, *refs):
    fetched, pieces = refs[:ranks], refs[ranks : 2 * ranks]
    src, dst, basis = refs[2 * ranks : 2 * ranks + 3]
    filt, slope = refs[2 * ranks + 3 : 2 * ranks + 5], refs[2 * ranks + 5 : 2 * ranks + 7]
    weight, outs = refs[2 * ranks + 7], refs[2 * ranks + 8 : 3 * ranks + 8]
    basis_v, filt_v, slope_v, message, dpre, hot, sems = refs[3 * ranks + 8 :]
    half = filt[0].shape[1]
    halves = [pl.ds(i * half, half) for i in range(2)]
    first = loads(slope, [slope_v.at[:, at] for at in halves], sems.at[0])
    second = loads([basis], [basis_v], sems.at[1])
    third = loads(filt, [filt_v.at[:, at] for at in halves], sems.at[2])
    per_owner = outs[0].shape[0]
    slots, block = ranks * per_owner, src.shape[1]
    src_t = turned(src, per_owner, ranks, me[0])
    dst_t = turned(dst, per_owner, ranks, me[0])
    near, back = gathered(fetched).T, gathered(pieces).T
    each = step // block
    spans = [pl.ds(i * step, step) for i in range(2 * half // step)]
    for i, at in enumerate(spans):
        hot[:, at] = hot_lanes(src_t, i * each, each, slots)
        rows = dot(back, hot_lanes(dst_t, i * each, each, slots, count[0, 0])).astype(BF16)
        message[:, at] = rows
        dpre[:, at] = rows * dot(near, hot[:, at]).astype(BF16)
    waited(first + second)
    for at in spans:
        dpre[:, at] = dpre[:, at] * slope_v[:, at]
    weight[...] = dot(dpre[...], basis_v[...]).T
    waited(third)
    for at in spans:
        message[:, at] = message[:, at] * filt_v[:, at]
    scattered(dot(hot[...], message[...], NT).astype(BF16), outs)


def final_kernel(ranks, step, me, *refs):
    lists, pieces = refs[:ranks], refs[ranks : 2 * ranks]
    upstream, out, upstream_v, out_v, sems, out_sems = refs[2 * ranks :]
    arrive = loads([upstream], [upstream_v], sems)
    back = gathered(pieces)
    rows = upstream.shape[0]
    hot_t = hot_rows(columns_of(lists, me[0], False, pieces[0].shape[0]), rows).T
    waited(arrive)
    leave = []
    for i in range(rows // step):
        at = pl.ds(i * step, step)
        total = upstream_v[at, :].astype(F32) + dot(hot_t[i * step : (i + 1) * step], back)
        out_v[at, :] = total.astype(BF16)
        leave.append(pltpu.make_async_copy(out_v.at[at, :], out.at[at, :], out_sems.at[i]))
        leave[i].start()
    waited(leave)


def swap(value, axis, mask):
    return lax.ppermute(value, axis, [(k, k ^ mask) for k in range(lax.axis_size(axis))])


def shift(value, axis, by):
    count = lax.axis_size(axis)
    return lax.ppermute(value, axis, [(k, (k + by) % count) for k in range(count)])


def exchange(pieces, sign):
    return [pieces[0]] + [shift(pieces[s], "graph", sign * s) for s in range(1, len(pieces))]


def halve(value, axis, bit):
    half = value.reshape(2, value.shape[0] // 2, value.shape[1])
    own = (lax.axis_index(axis) >> bit) & 1
    away = lax.dynamic_index_in_dim(half, 1 - own, 0, keepdims=False).astype(BF16)
    kept = lax.dynamic_index_in_dim(half, own, 0, keepdims=False)
    return kept.astype(F32) + swap(away, axis, 1 << bit).astype(F32)


def double(value, got, axis, bit):
    low = ((lax.axis_index(axis) >> bit) & 1) == 0
    return jnp.where(low, jnp.concatenate([value, got]), jnp.concatenate([got, value]))


def bits_of(axis):
    return range(lax.axis_size(axis).bit_length() - 1)


def reduce_out(term):
    for bit in bits_of("dp"):
        term = halve(term, "dp", bit)
    for bit in reversed(bits_of("graph")):
        term = halve(term, "graph", bit)
    return term.astype(BF16)


def reduce_both(out, basis):
    for bit in bits_of("dp"):
        basis = halve(basis, "dp", bit)
    basis = basis.astype(BF16)
    rows = basis.shape[0]
    for bit in bits_of("graph"):
        got = swap(jnp.concatenate([basis, out]), "graph", 1 << bit)
        basis = (basis.astype(F32) + got[:rows].astype(F32)).astype(BF16)
        out = double(out, got[rows:], "graph", bit)
    for bit in reversed(bits_of("dp")):
        rows = basis.shape[0]
        got = swap(jnp.concatenate([basis, out]), "dp", 1 << bit)
        basis = double(basis, got[:rows], "dp", bit)
        out = double(out, got[rows:], "dp", bit)
    return out.astype(F32), basis.astype(F32)


def per_device(
    edge_emb,
    cotangent,
    fetch_rows,
    store_rows,
    trip_src,
    trip_dst,
    trip_basis,
    block_count,
    w_basis,
    w_out,
):
    edges, upstream, basis = edge_emb[0], cotangent[0], trip_basis[0]
    ranks, copies = lax.axis_size("graph"), lax.axis_size("dp")
    me = lax.axis_index("graph").astype(jnp.int32).reshape(1)
    edge_dev, width = edges.shape
    per_owner = fetch_rows.shape[3]
    slots = ranks * per_owner
    blocks, block_rows = trip_src.shape[1:]
    triplets, basis_width = basis.shape
    src, dst = trip_src[0], trip_dst[0]
    pieces = [shape((per_owner, width))] * ranks
    half = shape((width, triplets // 2))
    plane, hot = shape((width, triplets)), shape((slots, triplets))
    step = 512
    wide = 2 * triplets * slots * width
    narrow = 2 * triplets * basis_width * width
    dma = pltpu.SemaphoreType.DMA

    both = jnp.concatenate([fetch_rows[0, 0], store_rows[0, 0]], axis=1)
    lists = exchange([both] * ranks, 1)

    def prepare(part):
        rows = triplets // 2
        return call(
            functools.partial(prepare_kernel, step, part),
            [half, half],
            [basis, w_basis],
            flops=4 * narrow,
            far=(0,),
            far_out=(0, 1),
            scratch=[pltpu.VMEM((rows, basis_width), BF16), held(half), held(half)]
            + [dma((1,)), dma((2, rows // step))],
        )

    early = prepare(0)
    lend = call(
        functools.partial(lend_kernel, ranks),
        pieces,
        [me] + lists + [edges],
        smem=(0,),
        far=(ranks + 1,),
        flops=2 * slots * edge_dev * width,
        scratch=[held(edges), dma((1,))],
        order=[early[0]],
    )
    fetched = exchange(lend, -1)
    late = prepare(1)
    filt, slope = [early[0], late[0]], [early[1], late[1]]
    partial_rows = call(
        functools.partial(forward_kernel, ranks, step),
        pieces,
        [me, block_count] + fetched + [src, dst] + filt,
        smem=(0, 1),
        far=(ranks + 4, ranks + 5),
        flops=2 * wide,
        scratch=[held(plane), held(plane), held(hot), dma((2,))],
    )
    home = exchange(partial_rows, 1)
    same, dhidden = call(
        functools.partial(owner_kernel, ranks),
        [shape((slots, slots)), shape((slots, width), F32)],
        [me] + lists + [upstream, w_out],
        smem=(0,),
        far=(ranks + 1, ranks + 2),
        flops=4 * slots * edge_dev * width,
        scratch=[held(upstream), held(w_out), dma((2,))],
        order=[partial_rows[0]],
    )
    back = call(
        functools.partial(return_kernel, ranks),
        pieces,
        home + [same, dhidden],
        flops=2 * slots * slots * width,
    )
    dpartial = exchange(back, -1)
    updated, out_term = call(
        functools.partial(update_kernel, ranks, 256),
        [shape((edge_dev, width)), shape((width, width))],
        [me] + lists + home + [edges, upstream, w_out],
        smem=(0,),
        far=(2 * ranks + 1, 2 * ranks + 2, 2 * ranks + 3),
        far_out=(0,),
        flops=2 * edge_dev * width * (2 * width + slots),
        scratch=[held(edges), held(upstream), held(w_out), held(edges)]
        + [pltpu.VMEM((width, edge_dev), BF16), dma((3,)), dma((edge_dev // 256,))],
        order=[back[0]],
    )
    out_part = reduce_out(out_term)
    basis_term, *dfetch = call(
        functools.partial(backward_kernel, ranks, step),
        [shape((basis_width, width), F32)] + pieces,
        [me, block_count] + fetched + dpartial + [src, dst, basis] + filt + slope,
        smem=(0, 1),
        far=tuple(range(2 * ranks + 4, 2 * ranks + 9)),
        flops=3 * wide + narrow,
        scratch=[held(basis)] + [held(plane)] * 4 + [held(hot), dma((3, 2))],
        order=[out_term],
    )
    grad_w_out, grad_w_basis = reduce_both(out_part, basis_term)
    (grad_edge,) = call(
        functools.partial(final_kernel, ranks, 256),
        [shape((edge_dev, width))],
        [me] + lists + exchange(dfetch, 1) + [upstream],
        smem=(0,),
        far=(2 * ranks + 1,),
        far_out=(0,),
        flops=2 * slots * edge_dev * width,
        scratch=[held(upstream), held(upstream), dma((1,)), dma((edge_dev // 256,))],
    )
    out_scale = jnp.sqrt(F32(copies * ranks * edge_dev))
    basis_scale = jnp.sqrt(F32(copies * ranks * blocks * block_rows))
    return (updated[None], grad_edge[None], grad_w_out / out_scale, grad_w_basis / basis_scale)


def solution(mesh):
    placed = (
        P(("groups", "dp"), "graph", None),
        P(("groups", "dp"), "graph", None),
        P(("groups", "dp"), "graph", None, None),
        P(("groups", "dp"), "graph", None, None),
        P(("groups", "dp"), "graph", None),
        P(("groups", "dp"), "graph", None),
        P(("groups", "dp"), "graph", None),
        P(("groups", "dp"), "graph"),
        P(),
        P(),
    )
    return jax.shard_map(
        per_device,
        mesh=mesh,
        in_specs=placed,
        out_specs=(
            P(("groups", "dp"), "graph", None),
            P(("groups", "dp"), "graph", None),
            P("groups", None),
            P("groups", None),
        ),
        check_vma=False,
    )
```

```python
import functools

import jax
import jax.numpy as jnp
from jax import lax
from jax.experimental import pallas as pl
from jax.experimental.pallas import tpu as pltpu
from jax.sharding import PartitionSpec as P

BF16 = jnp.bfloat16
F32 = jnp.float32
VMEM = pl.BlockSpec(memory_space=pltpu.VMEM)
SMEM = pl.BlockSpec(memory_space=pltpu.SMEM)
ANY = pl.BlockSpec(memory_space=pl.ANY)
NN = (((1,), (0,)), ((), ()))
NT = (((1,), (1,)), ((), ()))


def dot(a, b, dims=NN):
    return lax.dot_general(a, b, dims, preferred_element_type=F32)


def silu_parts(half):
    tanh = jnp.tanh(half)
    upper = 1.0 + tanh
    act = half * upper
    return act, upper + act * (1.0 - tanh)


def call(body, outs, args, flops=0, scratch=(), smem=(), far=(), far_out=(), order=()):
    args = list(args) + list(order)
    moved = sum(a.size * a.dtype.itemsize for a in args) + sum(
        o.size * o.dtype.itemsize for o in outs
    )
    keep = len(args) - len(order)
    specs = [
        SMEM if i in smem else ANY if i in far or i >= keep else VMEM for i in range(len(args))
    ]

    def inner(*refs):
        body(*refs[:keep], *refs[len(args) :])

    return pl.pallas_call(
        inner if order else body,
        out_shape=tuple(outs),
        in_specs=specs,
        out_specs=tuple(ANY if i in far_out else VMEM for i in range(len(outs))),
        scratch_shapes=list(scratch),
        cost_estimate=pl.CostEstimate(flops=flops, bytes_accessed=moved, transcendentals=0),
        compiler_params=pltpu.CompilerParams(vmem_limit_bytes=58 << 20),
    )(*args)


def shape(dims, dtype=BF16):
    return jax.ShapeDtypeStruct(dims, dtype)


def held(array):
    return pltpu.VMEM(array.shape, array.dtype)


def started(copies):
    for copy in copies:
        copy.start()
    return copies


def waited(copies):
    for copy in copies:
        copy.wait()


def loads(sources, targets, sems):
    return started(
        [pltpu.make_async_copy(a, b, sems.at[i]) for i, (a, b) in enumerate(zip(sources, targets))]
    )


def hot_lanes(index, first, count, slots, dead=None):
    block = index.shape[1]
    rows = lax.broadcasted_iota(jnp.int32, (slots, block), 0)
    parts = []
    for b in range(first, first + count):
        slot = index[pl.ds(b, 1), :]
        if dead is not None:
            slot = jnp.where(b < dead, slot, -1)
        parts.append(jnp.where(rows == slot, 1.0, 0.0).astype(BF16))
    return jnp.concatenate(parts, axis=1)


def turned(index, per_owner, ranks, me):
    slot = index[...] - me * per_owner
    return jnp.where(slot < 0, slot + ranks * per_owner, slot)


def gathered(pieces):
    return jnp.concatenate([p[...] for p in pieces], axis=0)


def scattered(value, outs):
    per = outs[0].shape[0]
    for s, out in enumerate(outs):
        out[...] = value[s * per : (s + 1) * per]


def columns_of(lists, me, kept, per_owner):
    parts = []
    for ref in lists:
        row = ref[pl.ds(me, 1), :].astype(F32)
        column = jnp.broadcast_to(row, (8, row.shape[1])).T[:, :1]
        parts.append(column[per_owner : 2 * per_owner] if kept else column[:per_owner])
    return jnp.concatenate(parts, axis=0)


def hot_rows(column, edge_dev):
    edges = lax.broadcasted_iota(jnp.int32, (column.shape[0], edge_dev), 1).astype(F32)
    return jnp.where(column == edges, 1.0, 0.0).astype(BF16)


def lend_kernel(ranks, me, *refs):
    lists, edges, outs = refs[:ranks], refs[ranks], refs[ranks + 1 : 2 * ranks + 1]
    edges_v, sems = refs[2 * ranks + 1 :]
    arrive = loads([edges], [edges_v], sems)
    hot = hot_rows(columns_of(lists, me[0], False, outs[0].shape[0]), edges.shape[0])
    waited(arrive)
    scattered(dot(hot, edges_v[...]).astype(BF16), outs)


def owner_kernel(ranks, me, *refs):
    lists, (upstream, w_out, same, dhidden) = refs[:ranks], refs[ranks : ranks + 4]
    upstream_v, w_out_v, sems = refs[ranks + 4 :]
    arrive = loads([upstream, w_out], [upstream_v, w_out_v], sems)
    hot = hot_rows(columns_of(lists, me[0], True, same.shape[0] // ranks), upstream.shape[0])
    same[...] = dot(hot, hot, NT).astype(BF16)
    waited(arrive)
    dhidden[...] = dot(dot(hot, upstream_v[...]).astype(BF16), w_out_v[...], NT)


def forward_kernel(ranks, step, place, count, *refs):
    pieces, (src, dst, weight, basis) = refs[:ranks], refs[ranks : ranks + 4]
    outs = refs[ranks + 4 : 2 * ranks + 4]
    basis_v, message, hot, near_hot, sems = refs[2 * ranks + 4 :]
    arrive = loads([basis], [basis_v], sems)
    per_owner = outs[0].shape[0]
    slots, block = ranks * per_owner, src.shape[1]
    table, weight_t = gathered(pieces).T, (0.5 * weight[...]).T
    src_t = turned(src, per_owner, ranks, place[0])
    dst_t = turned(dst, per_owner, ranks, place[0])
    each = step // block
    spans = [pl.ds(i * step, step) for i in range(basis.shape[0] // step)]
    for i, at in enumerate(spans):
        near_hot[:, at] = hot_lanes(src_t, i * each, each, slots)
        hot[:, at] = hot_lanes(dst_t, i * each, each, slots, count[0, 0])
    waited(arrive)
    for at in spans:
        act = silu_parts(dot(weight_t, basis_v[at, :], NT))[0]
        message[:, at] = (dot(table, near_hot[:, at]) * act).astype(BF16)
    scattered(dot(hot[...], message[...], NT).astype(BF16), outs)


def return_kernel(ranks, *refs):
    pieces, (same, dhidden), outs = refs[:ranks], refs[ranks : ranks + 2], refs[ranks + 2 :]
    agg = dot(same[...], gathered(pieces))
    scattered((dhidden[...] * (0.5 * silu_parts(0.5 * agg)[1])).astype(BF16), outs)


def update_kernel(ranks, step, me, *refs):
    lists, pieces = refs[:ranks], refs[ranks : 2 * ranks]
    edges, upstream, w_out, updated, kept, away = refs[2 * ranks : 2 * ranks + 6]
    edges_v, upstream_v, w_out_v, updated_v, hidden, sems, out_sems = refs[2 * ranks + 6 :]
    arrive = loads([w_out, edges, upstream], [w_out_v, edges_v, upstream_v], sems)
    home = gathered(pieces)
    rows = edges.shape[0]
    hot_t = hot_rows(columns_of(lists, me[0], True, pieces[0].shape[0]), rows).T
    turns = rows // step
    spans = [pl.ds(i * step, step) for i in range(turns)]
    leave = [
        pltpu.make_async_copy(updated_v.at[at, :], updated.at[at, :], out_sems.at[i])
        for i, at in enumerate(spans)
    ]
    fresh = [
        silu_parts(0.5 * dot(hot_t[i * step : (i + 1) * step], home))[0].astype(BF16)
        for i in range(turns)
    ]
    waited(arrive)
    for i, at in enumerate(spans):
        total = edges_v[at, :].astype(F32) + dot(fresh[i], w_out_v[...])
        updated_v[at, :] = total.astype(BF16)
        leave[i].start()
        hidden[:, at] = fresh[i].T
    half = kept.shape[0]
    own = pl.multiple_of(me[1] * half, half)
    other = pl.multiple_of((1 - me[1]) * half, half)
    away[...] = dot(hidden[pl.ds(other, half), :], upstream_v[...]).astype(BF16)
    kept[...] = dot(hidden[pl.ds(own, half), :], upstream_v[...])
    waited(leave)


def backward_kernel(ranks, step, place, count, *refs):
    fetched, pieces = refs[:ranks], refs[ranks : 2 * ranks]
    src, dst, weight, basis, kept, away = refs[2 * ranks : 2 * ranks + 6]
    outs = refs[2 * ranks + 6 : 3 * ranks + 6]
    basis_v, message, dpre, hot, back_hot, total, sems = refs[3 * ranks + 6 :]
    arrive = loads([basis], [basis_v], sems)
    per_owner = outs[0].shape[0]
    slots, block = ranks * per_owner, src.shape[1]
    src_t = turned(src, per_owner, ranks, place[0])
    dst_t = turned(dst, per_owner, ranks, place[0])
    near, back = gathered(fetched).T, gathered(pieces).T
    weight_t = (0.5 * weight[...]).T
    each = step // block
    spans = [pl.ds(i * step, step) for i in range(basis.shape[0] // step)]
    for i, at in enumerate(spans):
        hot[:, at] = hot_lanes(src_t, i * each, each, slots)
        back_hot[:, at] = hot_lanes(dst_t, i * each, each, slots, count[0, 0])
    waited(arrive)
    for at in spans:
        act, slope = silu_parts(dot(weight_t, basis_v[at, :], NT))
        rows = dot(back, back_hot[:, at]).astype(BF16)
        message[:, at] = rows * act.astype(BF16)
        dpre[:, at] = rows * dot(near, hot[:, at]).astype(BF16) * slope.astype(BF16)
    total[...] = dot(dpre[...], basis_v[...]).T
    half = kept.shape[0]
    kept[...] = total[pl.ds(pl.multiple_of(place[1] * half, half), half), :]
    away[...] = total[pl.ds(pl.multiple_of((1 - place[1]) * half, half), half), :].astype(BF16)
    scattered(dot(hot[...], message[...], NT).astype(BF16), outs)


def final_kernel(ranks, step, me, *refs):
    lists, pieces = refs[:ranks], refs[ranks : 2 * ranks]
    upstream, out, upstream_v, out_v, sems, out_sems = refs[2 * ranks :]
    arrive = loads([upstream], [upstream_v], sems)
    back = gathered(pieces)
    rows = upstream.shape[0]
    hot_t = hot_rows(columns_of(lists, me[0], False, pieces[0].shape[0]), rows).T
    waited(arrive)
    leave = []
    for i in range(rows // step):
        at = pl.ds(i * step, step)
        total = upstream_v[at, :].astype(F32) + dot(hot_t[i * step : (i + 1) * step], back)
        out_v[at, :] = total.astype(BF16)
        leave.append(pltpu.make_async_copy(out_v.at[at, :], out.at[at, :], out_sems.at[i]))
        leave[i].start()
    waited(leave)


def swap(value, axis, mask):
    return lax.ppermute(value, axis, [(k, k ^ mask) for k in range(lax.axis_size(axis))])


def shift(value, axis, by):
    count = lax.axis_size(axis)
    return lax.ppermute(value, axis, [(k, (k + by) % count) for k in range(count)])


def exchange(pieces, sign):
    return [pieces[0]] + [shift(pieces[s], "graph", sign * s) for s in range(1, len(pieces))]


def halve(value, axis, bit):
    half = value.reshape(2, value.shape[0] // 2, value.shape[1])
    own = (lax.axis_index(axis) >> bit) & 1
    away = lax.dynamic_index_in_dim(half, 1 - own, 0, keepdims=False).astype(BF16)
    kept = lax.dynamic_index_in_dim(half, own, 0, keepdims=False)
    return kept.astype(F32) + swap(away, axis, 1 << bit).astype(F32)


def double(value, got, axis, bit):
    low = ((lax.axis_index(axis) >> bit) & 1) == 0
    return jnp.where(low, jnp.concatenate([value, got]), jnp.concatenate([got, value]))


def bits_of(axis):
    return range(lax.axis_size(axis).bit_length() - 1)


def joined(kept, away):
    return kept + swap(away, "dp", 1).astype(F32)


def summed(value, axis, bit):
    own = value.astype(BF16)
    return own.astype(F32) + swap(own, axis, 1 << bit).astype(F32)


def finish(out, basis):
    out, basis = out.astype(BF16), basis.astype(BF16)
    rows = basis.shape[0]
    for bit in bits_of("graph"):
        own = jnp.concatenate([basis, out])
        got = swap(own, "graph", 1 << bit)
        basis = (basis.astype(F32) + got[:rows].astype(F32)).astype(BF16)
        out = (out.astype(F32) + got[rows:].astype(F32)).astype(BF16)
    for bit in reversed(bits_of("dp")[1:]):
        out = double(out, swap(out, "dp", 1 << bit), "dp", bit)
    got = swap(jnp.concatenate([basis, out]), "dp", 1)
    return double(out, got[rows:], "dp", 0).astype(F32), double(basis, got[:rows], "dp", 0).astype(F32)


def per_device(
    edge_emb,
    cotangent,
    fetch_rows,
    store_rows,
    trip_src,
    trip_dst,
    trip_basis,
    block_count,
    w_basis,
    w_out,
):
    edges, upstream, basis = edge_emb[0], cotangent[0], trip_basis[0]
    ranks, copies = lax.axis_size("graph"), lax.axis_size("dp")
    place = jnp.stack([lax.axis_index("graph"), lax.axis_index("dp") & 1]).astype(jnp.int32)
    edge_dev, width = edges.shape
    per_owner = fetch_rows.shape[3]
    slots = ranks * per_owner
    blocks, block_rows = trip_src.shape[1:]
    triplets, basis_width = basis.shape
    src, dst = trip_src[0], trip_dst[0]
    pieces = [shape((per_owner, width))] * ranks
    plane, hot = shape((width, triplets)), shape((slots, triplets))
    step = 256
    wide = 2 * triplets * slots * width
    narrow = 2 * triplets * basis_width * width
    dma = pltpu.SemaphoreType.DMA

    both = jnp.concatenate([fetch_rows[0, 0], store_rows[0, 0]], axis=1)
    lists = exchange([both] * ranks, 1)
    lend = call(
        functools.partial(lend_kernel, ranks),
        pieces,
        [place] + lists + [edges],
        smem=(0,),
        far=(ranks + 1,),
        flops=2 * slots * edge_dev * width,
        scratch=[held(edges), dma((1,))],
    )
    fetched = exchange(lend, -1)
    same, dhidden = call(
        functools.partial(owner_kernel, ranks),
        [shape((slots, slots)), shape((slots, width), F32)],
        [place] + lists + [upstream, w_out],
        smem=(0,),
        far=(ranks + 1, ranks + 2),
        flops=4 * slots * edge_dev * width,
        scratch=[held(upstream), held(w_out), dma((2,))],
        order=[lend[0]],
    )
    partial_rows = call(
        functools.partial(forward_kernel, ranks, step),
        pieces,
        [place, block_count] + fetched + [src, dst, w_basis, basis],
        smem=(0, 1),
        far=(ranks + 5,),
        flops=2 * wide + narrow,
        scratch=[held(basis), held(plane), held(hot), held(hot), dma((1,))],
        order=[same],
    )
    home = exchange(partial_rows, 1)
    back = call(
        functools.partial(return_kernel, ranks),
        pieces,
        home + [same, dhidden],
        flops=2 * slots * slots * width,
    )
    dpartial = exchange(back, -1)
    updated, out_kept, out_away = call(
        functools.partial(update_kernel, ranks, 256),
        [shape((edge_dev, width)), shape((width // 2, width), F32), shape((width // 2, width))],
        [place] + lists + home + [edges, upstream, w_out],
        smem=(0,),
        far=(2 * ranks + 1, 2 * ranks + 2, 2 * ranks + 3),
        far_out=(0,),
        flops=2 * edge_dev * width * (2 * width + slots),
        scratch=[held(edges), held(upstream), held(w_out), held(edges)]
        + [pltpu.VMEM((width, edge_dev), BF16), dma((3,)), dma((edge_dev // 256,))],
        order=[back[0]],
    )
    out_part = joined(out_kept, out_away)
    basis_half = basis_width // 2
    basis_kept, basis_away, *dfetch = call(
        functools.partial(backward_kernel, ranks, step),
        [shape((basis_half, width), F32), shape((basis_half, width))] + pieces,
        [place, block_count] + fetched + dpartial + [src, dst, w_basis, basis],
        smem=(0, 1),
        far=(2 * ranks + 5,),
        flops=3 * wide + 2 * narrow,
        scratch=[held(basis), held(plane), held(plane), held(hot), held(hot)]
        + [pltpu.VMEM((basis_width, width), F32), dma((1,))],
        order=[out_part],
    )
    returned = exchange(dfetch, 1)
    basis_part = joined(basis_kept, basis_away)
    for bit in bits_of("dp")[1:]:
        out_part = halve(out_part, "dp", bit)
        basis_part = summed(basis_part, "dp", bit)
    out_part, basis_part, returned = lax.optimization_barrier((out_part, basis_part, returned))
    grad_w_out, grad_w_basis = finish(out_part, basis_part)
    (grad_edge,) = call(
        functools.partial(final_kernel, ranks, 256),
        [shape((edge_dev, width))],
        [place] + lists + returned + [upstream],
        smem=(0,),
        far=(2 * ranks + 1,),
        far_out=(0,),
        flops=2 * slots * edge_dev * width,
        scratch=[held(upstream), held(upstream), dma((1,)), dma((edge_dev // 256,))],
    )
    out_scale = jnp.sqrt(F32(copies * ranks * edge_dev))
    basis_scale = 2.0 * jnp.sqrt(F32(copies * ranks * blocks * block_rows))
    return (updated[None], grad_edge[None], grad_w_out / out_scale, grad_w_basis / basis_scale)


def solution(mesh):
    placed = (
        P(("groups", "dp"), "graph", None),
        P(("groups", "dp"), "graph", None),
        P(("groups", "dp"), "graph", None, None),
        P(("groups", "dp"), "graph", None, None),
        P(("groups", "dp"), "graph", None),
        P(("groups", "dp"), "graph", None),
        P(("groups", "dp"), "graph", None),
        P(("groups", "dp"), "graph"),
        P(),
        P(),
    )
    return jax.shard_map(
        per_device,
        mesh=mesh,
        in_specs=placed,
        out_specs=(
            P(("groups", "dp"), "graph", None),
            P(("groups", "dp"), "graph", None),
            P("groups", None),
            P("groups", None),
        ),
        check_vma=False,
    )
```

```python
import functools

import jax
import jax.numpy as jnp
from jax import lax
from jax.experimental import pallas as pl
from jax.experimental.pallas import tpu as pltpu
from jax.sharding import PartitionSpec as P

BF16 = jnp.bfloat16
F32 = jnp.float32
VMEM = pl.BlockSpec(memory_space=pltpu.VMEM)
SMEM = pl.BlockSpec(memory_space=pltpu.SMEM)
ANY = pl.BlockSpec(memory_space=pl.ANY)
HBM = pl.BlockSpec(memory_space=pltpu.HBM)
NN = (((1,), (0,)), ((), ()))
NT = (((1,), (1,)), ((), ()))


def dot(a, b, dims=NN):
    return lax.dot_general(a, b, dims, preferred_element_type=F32)


def silu_parts(half):
    tanh = jnp.tanh(half)
    upper = 1.0 + tanh
    act = half * upper
    return act, upper + act * (1.0 - tanh)


def call(body, outs, args, flops=0, scratch=(), smem=(), far=(), far_out=(), order=(), vmem=16):
    args = list(args) + list(order)
    moved = sum(a.size * a.dtype.itemsize for a in args) + sum(
        o.size * o.dtype.itemsize for o in outs
    )
    keep = len(args) - len(order)
    specs = [
        SMEM if i in smem else ANY if i >= keep else HBM if i in far else VMEM
        for i in range(len(args))
    ]

    def inner(*refs):
        body(*refs[:keep], *refs[len(args) :])

    return pl.pallas_call(
        inner if order else body,
        out_shape=tuple(outs),
        in_specs=specs,
        out_specs=tuple(HBM if i in far_out else VMEM for i in range(len(outs))),
        scratch_shapes=list(scratch),
        cost_estimate=pl.CostEstimate(flops=flops, bytes_accessed=moved, transcendentals=0),
        compiler_params=pltpu.CompilerParams(vmem_limit_bytes=vmem << 20),
    )(*args)


def shape(dims, dtype=BF16):
    return jax.ShapeDtypeStruct(dims, dtype)


def held(array):
    return pltpu.VMEM(array.shape, array.dtype)


def started(copies):
    for copy in copies:
        copy.start()
    return copies


def waited(copies):
    for copy in copies:
        copy.wait()


def loads(sources, targets, sems):
    return started(
        [pltpu.make_async_copy(a, b, sems.at[i]) for i, (a, b) in enumerate(zip(sources, targets))]
    )


def hot_lanes(index, first, count, slots, dead=None):
    block = index.shape[1]
    rows = lax.broadcasted_iota(jnp.int32, (slots, block), 0)
    parts = []
    for b in range(first, first + count):
        slot = index[pl.ds(b, 1), :]
        if dead is not None:
            slot = jnp.where(b < dead, slot, -1)
        parts.append(jnp.where(rows == slot, 1.0, 0.0).astype(BF16))
    return jnp.concatenate(parts, axis=1)


def turned(index, per_owner, ranks, me):
    slot = index[...] - me * per_owner
    return jnp.where(slot < 0, slot + ranks * per_owner, slot)


def gathered(pieces):
    return jnp.concatenate([p[...] for p in pieces], axis=0)


def scattered(value, outs):
    per = outs[0].shape[0]
    for s, out in enumerate(outs):
        out[...] = value[s * per : (s + 1) * per]


def columns_of(lists, me, kept, per_owner):
    parts = []
    for ref in lists:
        row = ref[pl.ds(me, 1), :].astype(F32)
        column = jnp.broadcast_to(row, (8, row.shape[1])).T[:, :1]
        parts.append(column[per_owner : 2 * per_owner] if kept else column[:per_owner])
    return jnp.concatenate(parts, axis=0)


def hot_rows(column, edge_dev):
    edges = lax.broadcasted_iota(jnp.int32, (column.shape[0], edge_dev), 1).astype(F32)
    return jnp.where(column == edges, 1.0, 0.0).astype(BF16)


def lend_kernel(ranks, me, *refs):
    lists, edges, outs = refs[:ranks], refs[ranks], refs[ranks + 1 : 2 * ranks + 1]
    edges_v, sems = refs[2 * ranks + 1 :]
    arrive = loads([edges], [edges_v], sems)
    hot = hot_rows(columns_of(lists, me[0], False, outs[0].shape[0]), edges.shape[0])
    waited(arrive)
    scattered(dot(hot, edges_v[...]).astype(BF16), outs)


def owner_kernel(ranks, me, *refs):
    lists, (upstream, w_out, same, dhidden) = refs[:ranks], refs[ranks : ranks + 4]
    upstream_v, w_out_v, sems = refs[ranks + 4 :]
    arrive = loads([upstream, w_out], [upstream_v, w_out_v], sems)
    hot = hot_rows(columns_of(lists, me[0], True, same.shape[0] // ranks), upstream.shape[0])
    same[...] = dot(hot, hot, NT).astype(BF16)
    waited(arrive)
    dhidden[...] = dot(dot(hot, upstream_v[...]).astype(BF16), w_out_v[...], NT)


def forward_kernel(ranks, step, place, count, *refs):
    pieces, (src, dst, weight, basis) = refs[:ranks], refs[ranks : ranks + 4]
    outs = refs[ranks + 4 : 2 * ranks + 4]
    basis_v, message, hot, near_hot, sems = refs[2 * ranks + 4 :]
    arrive = loads([basis], [basis_v], sems)
    per_owner = outs[0].shape[0]
    slots, block = ranks * per_owner, src.shape[1]
    table, weight_t = gathered(pieces).T, (0.5 * weight[...]).T
    src_t = turned(src, per_owner, ranks, place[0])
    dst_t = turned(dst, per_owner, ranks, place[0])
    each = step // block
    spans = [pl.ds(i * step, step) for i in range(basis.shape[0] // step)]
    for i, at in enumerate(spans):
        near_hot[:, at] = hot_lanes(src_t, i * each, each, slots)
        hot[:, at] = hot_lanes(dst_t, i * each, each, slots, count[0, 0])
    waited(arrive)
    for at in spans:
        act = silu_parts(dot(weight_t, basis_v[at, :], NT))[0]
        message[:, at] = (dot(table, near_hot[:, at]) * act).astype(BF16)
    scattered(dot(hot[...], message[...], NT).astype(BF16), outs)


def return_kernel(ranks, *refs):
    pieces, (same, dhidden), outs = refs[:ranks], refs[ranks : ranks + 2], refs[ranks + 2 :]
    agg = dot(same[...], gathered(pieces))
    scattered((dhidden[...] * (0.5 * silu_parts(0.5 * agg)[1])).astype(BF16), outs)


def reverse(value, count):
    bits = count.bit_length() - 1
    return sum(((value >> b) & 1) << (bits - 1 - b) for b in range(bits))


def update_kernel(ranks, step, me, *refs):
    lists, pieces = refs[:ranks], refs[ranks : 2 * ranks]
    edges, upstream, w_out, updated, term = refs[2 * ranks : 2 * ranks + 5]
    edges_v, upstream_v, w_out_v, updated_v, hidden, sems, out_sems = refs[2 * ranks + 5 :]
    arrive = loads([w_out, edges, upstream], [w_out_v, edges_v, upstream_v], sems)
    home = gathered(pieces)
    rows = edges.shape[0]
    hot_t = hot_rows(columns_of(lists, me[0], True, pieces[0].shape[0]), rows).T
    turns = rows // step
    spans = [pl.ds(i * step, step) for i in range(turns)]
    leave = [
        pltpu.make_async_copy(updated_v.at[at, :], updated.at[at, :], out_sems.at[i])
        for i, at in enumerate(spans)
    ]
    fresh = [
        silu_parts(0.5 * dot(hot_t[i * step : (i + 1) * step], home))[0].astype(BF16)
        for i in range(turns)
    ]
    waited(arrive)
    for i, at in enumerate(spans):
        total = edges_v[at, :].astype(F32) + dot(fresh[i], w_out_v[...])
        updated_v[at, :] = total.astype(BF16)
        leave[i].start()
        hidden[:, at] = fresh[i].T
    copies, part = term.shape[0], term.shape[1]
    total = dot(hidden[...], upstream_v[...]).astype(BF16)
    for k in range(copies):
        term[reverse(k, copies)] = total[k * part : (k + 1) * part]
    waited(leave)


def backward_kernel(ranks, step, place, count, *refs):
    fetched, pieces = refs[:ranks], refs[ranks : 2 * ranks]
    src, dst, weight, basis, kept, away = refs[2 * ranks : 2 * ranks + 6]
    outs = refs[2 * ranks + 6 : 3 * ranks + 6]
    basis_v, message, dpre, hot, back_hot, total, sems = refs[3 * ranks + 6 :]
    arrive = loads([basis], [basis_v], sems)
    per_owner = outs[0].shape[0]
    slots, block = ranks * per_owner, src.shape[1]
    src_t = turned(src, per_owner, ranks, place[0])
    dst_t = turned(dst, per_owner, ranks, place[0])
    near, back = gathered(fetched).T, gathered(pieces).T
    weight_t = (0.5 * weight[...]).T
    each = step // block
    spans = [pl.ds(i * step, step) for i in range(basis.shape[0] // step)]
    for i, at in enumerate(spans):
        hot[:, at] = hot_lanes(src_t, i * each, each, slots)
        back_hot[:, at] = hot_lanes(dst_t, i * each, each, slots, count[0, 0])
    waited(arrive)
    for at in spans:
        act, slope = silu_parts(dot(weight_t, basis_v[at, :], NT))
        rows = dot(back, back_hot[:, at]).astype(BF16)
        message[:, at] = rows * act.astype(BF16)
        dpre[:, at] = rows * dot(near, hot[:, at]).astype(BF16) * slope.astype(BF16)
    total[...] = dot(dpre[...], basis_v[...]).T
    half = kept.shape[0]
    kept[...] = total[pl.ds(pl.multiple_of(place[1] * half, half), half), :]
    away[...] = total[pl.ds(pl.multiple_of((1 - place[1]) * half, half), half), :].astype(BF16)
    scattered(dot(hot[...], message[...], NT).astype(BF16), outs)


def final_kernel(ranks, step, me, *refs):
    lists, pieces = refs[:ranks], refs[ranks : 2 * ranks]
    upstream, out, upstream_v, out_v, sems, out_sems = refs[2 * ranks :]
    arrive = loads([upstream], [upstream_v], sems)
    back = gathered(pieces)
    rows = upstream.shape[0]
    hot_t = hot_rows(columns_of(lists, me[0], False, pieces[0].shape[0]), rows).T
    waited(arrive)
    leave = []
    for i in range(rows // step):
        at = pl.ds(i * step, step)
        total = upstream_v[at, :].astype(F32) + dot(hot_t[i * step : (i + 1) * step], back)
        out_v[at, :] = total.astype(BF16)
        leave.append(pltpu.make_async_copy(out_v.at[at, :], out.at[at, :], out_sems.at[i]))
        leave[i].start()
    waited(leave)


def swap(value, axis, mask):
    return lax.ppermute(value, axis, [(k, k ^ mask) for k in range(lax.axis_size(axis))])


def shift(value, axis, by):
    count = lax.axis_size(axis)
    return lax.ppermute(value, axis, [(k, (k + by) % count) for k in range(count)])


def exchange(pieces, sign):
    return [pieces[0]] + [shift(pieces[s], "graph", sign * s) for s in range(1, len(pieces))]


def halve(value, axis, bit):
    half = value.reshape(2, value.shape[0] // 2, value.shape[1])
    own = (lax.axis_index(axis) >> bit) & 1
    away = lax.dynamic_index_in_dim(half, 1 - own, 0, keepdims=False).astype(BF16)
    kept = lax.dynamic_index_in_dim(half, own, 0, keepdims=False)
    return kept.astype(F32) + swap(away, axis, 1 << bit).astype(F32)


def double(value, got, axis, bit):
    low = ((lax.axis_index(axis) >> bit) & 1) == 0
    return jnp.where(low, jnp.concatenate([value, got]), jnp.concatenate([got, value]))


def bits_of(axis):
    return range(lax.axis_size(axis).bit_length() - 1)


def joined(kept, away):
    return kept + swap(away, "dp", 1).astype(F32)


def doubled(out, basis, axis, bit):
    rows = basis.shape[0]
    got = swap(jnp.concatenate([basis, out]), axis, 1 << bit)
    return got[:rows], double(out, got[rows:], axis, bit)


def per_device(
    edge_emb,
    cotangent,
    fetch_rows,
    store_rows,
    trip_src,
    trip_dst,
    trip_basis,
    block_count,
    w_basis,
    w_out,
):
    edges, upstream, basis = edge_emb[0], cotangent[0], trip_basis[0]
    ranks, copies = lax.axis_size("graph"), lax.axis_size("dp")
    place = jnp.stack([lax.axis_index("graph"), lax.axis_index("dp") & 1]).astype(jnp.int32)
    edge_dev, width = edges.shape
    per_owner = fetch_rows.shape[3]
    slots = ranks * per_owner
    blocks, block_rows = trip_src.shape[1:]
    triplets, basis_width = basis.shape
    src, dst = trip_src[0], trip_dst[0]
    pieces = [shape((per_owner, width))] * ranks
    plane, hot = shape((width, triplets)), shape((slots, triplets))
    step = 256
    wide = 2 * triplets * slots * width
    narrow = 2 * triplets * basis_width * width
    dma = pltpu.SemaphoreType.DMA

    both = jnp.concatenate([fetch_rows[0, 0], store_rows[0, 0]], axis=1)
    lists = exchange([both] * ranks, 1)
    lend = call(
        functools.partial(lend_kernel, ranks),
        pieces,
        [place] + lists + [edges],
        smem=(0,),
        far=(ranks + 1,),
        flops=2 * slots * edge_dev * width,
        scratch=[held(edges), dma((1,))],
    )
    fetched = exchange(lend, -1)
    same, dhidden = call(
        functools.partial(owner_kernel, ranks),
        [shape((slots, slots)), shape((slots, width), F32)],
        [place] + lists + [upstream, w_out],
        smem=(0,),
        far=(ranks + 1, ranks + 2),
        flops=4 * slots * edge_dev * width,
        scratch=[held(upstream), held(w_out), dma((2,))],
        order=[lend[0]],
    )
    partial_rows = call(
        functools.partial(forward_kernel, ranks, step),
        pieces,
        [place, block_count] + fetched + [src, dst, w_basis, basis],
        smem=(0, 1),
        far=(ranks + 5,),
        flops=2 * wide + narrow,
        scratch=[held(basis), held(plane), held(hot), held(hot), dma((1,))],
        order=[same],
        vmem=30,
    )
    home = exchange(partial_rows, 1)
    back = call(
        functools.partial(return_kernel, ranks),
        pieces,
        home + [same, dhidden],
        flops=2 * slots * slots * width,
    )
    dpartial = exchange(back, -1)
    updated, out_term = call(
        functools.partial(update_kernel, ranks, 256),
        [shape((edge_dev, width)), shape((copies, width // copies, width))],
        [place] + lists + home + [edges, upstream, w_out],
        smem=(0,),
        far=(2 * ranks + 1, 2 * ranks + 2, 2 * ranks + 3),
        far_out=(0,),
        flops=2 * edge_dev * width * (2 * width + slots),
        scratch=[held(edges), held(upstream), held(w_out), held(edges)]
        + [pltpu.VMEM((width, edge_dev), BF16), dma((3,)), dma((edge_dev // 256,))],
        order=[back[0]],
    )
    out_parts = lax.all_to_all(out_term, "dp", split_axis=0, concat_axis=0, tiled=True)
    basis_half = basis_width // 2
    basis_kept, basis_away, *dfetch = call(
        functools.partial(backward_kernel, ranks, step),
        [shape((basis_half, width), F32), shape((basis_half, width))] + pieces,
        [place, block_count] + fetched + dpartial + [src, dst, w_basis, basis],
        smem=(0, 1),
        far=(2 * ranks + 5,),
        flops=3 * wide + 2 * narrow,
        scratch=[held(basis), held(plane), held(plane), held(hot), held(hot)]
        + [pltpu.VMEM((basis_width, width), F32), dma((1,))],
        order=[out_term],
        vmem=36,
    )
    returned = exchange(dfetch, 1)
    basis_part = joined(basis_kept, basis_away)
    for bit in bits_of("dp")[1:]:
        basis_part = halve(basis_part, "dp", bit)
    out_part = jnp.sum(out_parts.astype(F32), axis=0)
    for bit in reversed(bits_of("graph")):
        out_part = halve(out_part, "graph", bit)
    out, total = out_part.astype(BF16), basis_part.astype(BF16)
    out, total, returned = lax.optimization_barrier((out, total, returned))
    for bit in bits_of("graph"):
        got, out = doubled(out, total, "graph", bit)
        total = (total.astype(F32) + got.astype(F32)).astype(BF16)
    (grad_edge,) = call(
        functools.partial(final_kernel, ranks, 256),
        [shape((edge_dev, width))],
        [place] + lists + returned + [upstream],
        smem=(0,),
        far=(2 * ranks + 1,),
        far_out=(0,),
        flops=2 * slots * edge_dev * width,
        scratch=[held(upstream), held(upstream), dma((1,)), dma((edge_dev // 256,))],
    )
    out, total, grad_edge = lax.optimization_barrier((out, total, grad_edge))
    for bit in reversed(bits_of("dp")):
        got, out = doubled(out, total, "dp", bit)
        total = double(total, got, "dp", bit)
    out_scale = jnp.sqrt(F32(copies * ranks * edge_dev))
    basis_scale = 2.0 * jnp.sqrt(F32(copies * ranks * blocks * block_rows))
    return (updated[None], grad_edge[None], out.astype(F32) / out_scale, total.astype(F32) / basis_scale)


def solution(mesh):
    placed = (
        P(("groups", "dp"), "graph", None),
        P(("groups", "dp"), "graph", None),
        P(("groups", "dp"), "graph", None, None),
        P(("groups", "dp"), "graph", None, None),
        P(("groups", "dp"), "graph", None),
        P(("groups", "dp"), "graph", None),
        P(("groups", "dp"), "graph", None),
        P(("groups", "dp"), "graph"),
        P(),
        P(),
    )
    return jax.shard_map(
        per_device,
        mesh=mesh,
        in_specs=placed,
        out_specs=(
            P(("groups", "dp"), "graph", None),
            P(("groups", "dp"), "graph", None),
            P("groups", None),
            P("groups", None),
        ),
        check_vma=False,
    )
```

```python
import functools

import jax
import jax.numpy as jnp
from jax import lax
from jax.experimental import pallas as pl
from jax.experimental.pallas import tpu as pltpu
from jax.sharding import PartitionSpec as P

BF16 = jnp.bfloat16
F32 = jnp.float32
VMEM = pl.BlockSpec(memory_space=pltpu.VMEM)
SMEM = pl.BlockSpec(memory_space=pltpu.SMEM)
ANY = pl.BlockSpec(memory_space=pl.ANY)
HBM = pl.BlockSpec(memory_space=pltpu.HBM)
NN = (((1,), (0,)), ((), ()))
NT = (((1,), (1,)), ((), ()))


def dot(a, b, dims=NN):
    return lax.dot_general(a, b, dims, preferred_element_type=F32)


def silu_parts(half):
    tanh = jnp.tanh(half)
    upper = 1.0 + tanh
    act = half * upper
    return act, upper + act * (1.0 - tanh)


def call(body, outs, args, flops=0, scratch=(), smem=(), far=(), far_out=(), order=(), vmem=16, pin=False):
    args = [
        pltpu.with_memory_space_constraint(a, pltpu.HBM) if pin and i in far else a
        for i, a in enumerate(args)
    ] + list(order)
    moved = sum(a.size * a.dtype.itemsize for a in args) + sum(
        o.size * o.dtype.itemsize for o in outs
    )
    keep = len(args) - len(order)
    specs = [
        SMEM if i in smem else ANY if i >= keep else HBM if i in far else VMEM
        for i in range(len(args))
    ]

    def inner(*refs):
        body(*refs[:keep], *refs[len(args) :])

    return pl.pallas_call(
        inner if order else body,
        out_shape=tuple(outs),
        in_specs=specs,
        out_specs=tuple(HBM if i in far_out else VMEM for i in range(len(outs))),
        scratch_shapes=list(scratch),
        cost_estimate=pl.CostEstimate(flops=flops, bytes_accessed=moved, transcendentals=0),
        compiler_params=pltpu.CompilerParams(vmem_limit_bytes=vmem << 20),
    )(*args)


def shape(dims, dtype=BF16):
    return jax.ShapeDtypeStruct(dims, dtype)


def held(array):
    return pltpu.VMEM(array.shape, array.dtype)


def started(copies):
    for copy in copies:
        copy.start()
    return copies


def waited(copies):
    for copy in copies:
        copy.wait()


def loads(sources, targets, sems):
    return started(
        [pltpu.make_async_copy(a, b, sems.at[i]) for i, (a, b) in enumerate(zip(sources, targets))]
    )


def hot_lanes(index, first, count, slots, dead=None):
    block = index.shape[1]
    rows = lax.broadcasted_iota(jnp.int32, (slots, block), 0)
    parts = []
    for b in range(first, first + count):
        slot = index[pl.ds(b, 1), :]
        if dead is not None:
            slot = jnp.where(b < dead, slot, -1)
        parts.append(jnp.where(rows == slot, 1.0, 0.0).astype(BF16))
    return jnp.concatenate(parts, axis=1)


def turned(index, per_owner, ranks, me):
    slot = index[...] - me * per_owner
    return jnp.where(slot < 0, slot + ranks * per_owner, slot)


def gathered(pieces):
    return jnp.concatenate([p[...] for p in pieces], axis=0)


def scattered(value, outs):
    per = outs[0].shape[0]
    for s, out in enumerate(outs):
        out[...] = value[s * per : (s + 1) * per]


def columns_of(lists, me, kept, per_owner):
    parts = []
    for ref in lists:
        row = ref[pl.ds(me, 1), :].astype(F32)
        column = jnp.broadcast_to(row, (8, row.shape[1])).T[:, :1]
        parts.append(column[per_owner : 2 * per_owner] if kept else column[:per_owner])
    return jnp.concatenate(parts, axis=0)


def hot_rows(column, edge_dev):
    edges = lax.broadcasted_iota(jnp.int32, (column.shape[0], edge_dev), 1).astype(F32)
    return jnp.where(column == edges, 1.0, 0.0).astype(BF16)


def pair_kernel(fetch, store, out, fetch_v, store_v, sems):
    waited(loads([fetch, store], [fetch_v, store_v], sems))
    out[...] = jnp.concatenate([fetch_v[...], store_v[...]], axis=1)


def lend_kernel(ranks, me, *refs):
    lists, edges, outs = refs[:ranks], refs[ranks], refs[ranks + 1 : 2 * ranks + 1]
    edges_v, sems = refs[2 * ranks + 1 :]
    arrive = loads([edges], [edges_v], sems)
    hot = hot_rows(columns_of(lists, me[0], False, outs[0].shape[0]), edges.shape[0])
    waited(arrive)
    scattered(dot(hot, edges_v[...]).astype(BF16), outs)


def owner_kernel(ranks, me, *refs):
    lists, (upstream, w_out, same, dhidden) = refs[:ranks], refs[ranks : ranks + 4]
    upstream_v, w_out_v, sems = refs[ranks + 4 :]
    arrive = loads([upstream, w_out], [upstream_v, w_out_v], sems)
    hot = hot_rows(columns_of(lists, me[0], True, same.shape[0] // ranks), upstream.shape[0])
    same[...] = dot(hot, hot, NT).astype(BF16)
    waited(arrive)
    dhidden[...] = dot(dot(hot, upstream_v[...]).astype(BF16), w_out_v[...], NT)


def forward_kernel(ranks, step, place, count, *refs):
    pieces, (src, dst, weight, basis) = refs[:ranks], refs[ranks : ranks + 4]
    outs = refs[ranks + 4 : 2 * ranks + 4]
    basis_v, message, hot, near_hot, sems = refs[2 * ranks + 4 :]
    arrive = loads([basis], [basis_v], sems)
    per_owner = outs[0].shape[0]
    slots, block = ranks * per_owner, src.shape[1]
    table, weight_t = gathered(pieces).T, (0.5 * weight[...]).T
    src_t = turned(src, per_owner, ranks, place[0])
    dst_t = turned(dst, per_owner, ranks, place[0])
    each = step // block
    spans = [pl.ds(i * step, step) for i in range(basis.shape[0] // step)]
    for i, at in enumerate(spans):
        near_hot[:, at] = hot_lanes(src_t, i * each, each, slots)
        hot[:, at] = hot_lanes(dst_t, i * each, each, slots, count[0, 0])
    waited(arrive)
    for at in spans:
        act = silu_parts(dot(weight_t, basis_v[at, :], NT))[0]
        message[:, at] = (dot(table, near_hot[:, at]) * act).astype(BF16)
    scattered(dot(hot[...], message[...], NT).astype(BF16), outs)


def return_kernel(ranks, *refs):
    pieces, (same, dhidden), outs = refs[:ranks], refs[ranks : ranks + 2], refs[ranks + 2 :]
    agg = dot(same[...], gathered(pieces))
    scattered((dhidden[...] * (0.5 * silu_parts(0.5 * agg)[1])).astype(BF16), outs)


def reverse(value, count):
    bits = count.bit_length() - 1
    return sum(((value >> b) & 1) << (bits - 1 - b) for b in range(bits))


def update_kernel(ranks, step, me, *refs):
    lists, pieces = refs[:ranks], refs[ranks : 2 * ranks]
    edges, upstream, w_out, updated, term = refs[2 * ranks : 2 * ranks + 5]
    edges_v, upstream_v, w_out_v, updated_v, hidden, sems, out_sems = refs[2 * ranks + 5 :]
    arrive = loads([w_out, edges, upstream], [w_out_v, edges_v, upstream_v], sems)
    home = gathered(pieces)
    rows = edges.shape[0]
    hot_t = hot_rows(columns_of(lists, me[0], True, pieces[0].shape[0]), rows).T
    turns = rows // step
    spans = [pl.ds(i * step, step) for i in range(turns)]
    leave = [
        pltpu.make_async_copy(updated_v.at[at, :], updated.at[at, :], out_sems.at[i])
        for i, at in enumerate(spans)
    ]
    fresh = [
        silu_parts(0.5 * dot(hot_t[i * step : (i + 1) * step], home))[0].astype(BF16)
        for i in range(turns)
    ]
    waited(arrive)
    for i, at in enumerate(spans):
        total = edges_v[at, :].astype(F32) + dot(fresh[i], w_out_v[...])
        updated_v[at, :] = total.astype(BF16)
        leave[i].start()
        hidden[:, at] = fresh[i].T
    total = dot(hidden[...], upstream_v[...]).astype(BF16)
    if len(term.shape) == 2:
        term[...] = total
    else:
        parts, part = term.shape[0], term.shape[1]
        copies = parts // ranks
        for k in range(parts):
            block = reverse(k % copies, copies) * ranks + k // copies
            term[k] = total[block * part : (block + 1) * part]
    waited(leave)


def backward_kernel(ranks, step, place, count, *refs):
    fetched, pieces = refs[:ranks], refs[ranks : 2 * ranks]
    src, dst, weight, basis, kept, away = refs[2 * ranks : 2 * ranks + 6]
    outs = refs[2 * ranks + 6 : 3 * ranks + 6]
    basis_v, message, dpre, hot, back_hot, total, sems = refs[3 * ranks + 6 :]
    arrive = loads([basis], [basis_v], sems)
    per_owner = outs[0].shape[0]
    slots, block = ranks * per_owner, src.shape[1]
    src_t = turned(src, per_owner, ranks, place[0])
    dst_t = turned(dst, per_owner, ranks, place[0])
    near, back = gathered(fetched).T, gathered(pieces).T
    weight_t = (0.5 * weight[...]).T
    each = step // block
    spans = [pl.ds(i * step, step) for i in range(basis.shape[0] // step)]
    for i, at in enumerate(spans):
        hot[:, at] = hot_lanes(src_t, i * each, each, slots)
        back_hot[:, at] = hot_lanes(dst_t, i * each, each, slots, count[0, 0])
    waited(arrive)
    for at in spans:
        act, slope = silu_parts(dot(weight_t, basis_v[at, :], NT))
        rows = dot(back, back_hot[:, at]).astype(BF16)
        message[:, at] = rows * act.astype(BF16)
        dpre[:, at] = rows * dot(near, hot[:, at]).astype(BF16) * slope.astype(BF16)
    total[...] = dot(dpre[...], basis_v[...]).T
    half = kept.shape[0]
    kept[...] = total[pl.ds(pl.multiple_of(place[1] * half, half), half), :]
    away[...] = total[pl.ds(pl.multiple_of((1 - place[1]) * half, half), half), :].astype(BF16)
    scattered(dot(hot[...], message[...], NT).astype(BF16), outs)


def final_kernel(ranks, step, me, *refs):
    lists, pieces = refs[:ranks], refs[ranks : 2 * ranks]
    upstream, out, upstream_v, out_v, sems, out_sems = refs[2 * ranks :]
    arrive = loads([upstream], [upstream_v], sems)
    back = gathered(pieces)
    rows = upstream.shape[0]
    hot_t = hot_rows(columns_of(lists, me[0], False, pieces[0].shape[0]), rows).T
    waited(arrive)
    leave = []
    for i in range(rows // step):
        at = pl.ds(i * step, step)
        total = upstream_v[at, :].astype(F32) + dot(hot_t[i * step : (i + 1) * step], back)
        out_v[at, :] = total.astype(BF16)
        leave.append(pltpu.make_async_copy(out_v.at[at, :], out.at[at, :], out_sems.at[i]))
        leave[i].start()
    waited(leave)


def swap(value, axis, mask):
    return lax.ppermute(value, axis, [(k, k ^ mask) for k in range(lax.axis_size(axis))])


def shift(value, axis, by):
    count = lax.axis_size(axis)
    return lax.ppermute(value, axis, [(k, (k + by) % count) for k in range(count)])


def exchange(pieces, sign):
    return [pieces[0]] + [shift(pieces[s], "graph", sign * s) for s in range(1, len(pieces))]


def halve(value, axis, bit):
    half = value.reshape(2, value.shape[0] // 2, value.shape[1])
    own = (lax.axis_index(axis) >> bit) & 1
    away = lax.dynamic_index_in_dim(half, 1 - own, 0, keepdims=False).astype(BF16)
    kept = lax.dynamic_index_in_dim(half, own, 0, keepdims=False)
    return kept.astype(F32) + swap(away, axis, 1 << bit).astype(F32)


def double(value, got, axis, bit):
    low = ((lax.axis_index(axis) >> bit) & 1) == 0
    return jnp.where(low, jnp.concatenate([value, got]), jnp.concatenate([got, value]))


def bits_of(axis):
    return range(lax.axis_size(axis).bit_length() - 1)


def joined(kept, away):
    return kept + swap(away, "dp", 1).astype(F32)


def doubled(out, basis, axis, bit):
    rows = basis.shape[0]
    got = swap(jnp.concatenate([basis, out]), axis, 1 << bit)
    return got[:rows], double(out, got[rows:], axis, bit)


def per_device(
    edge_emb,
    cotangent,
    fetch_rows,
    store_rows,
    trip_src,
    trip_dst,
    trip_basis,
    block_count,
    w_basis,
    w_out,
):
    edges, upstream, basis = edge_emb[0], cotangent[0], trip_basis[0]
    ranks, copies = lax.axis_size("graph"), lax.axis_size("dp")
    place = jnp.stack([lax.axis_index("graph"), lax.axis_index("dp") & 1]).astype(jnp.int32)
    edge_dev, width = edges.shape
    per_owner = fetch_rows.shape[3]
    slots = ranks * per_owner
    blocks, block_rows = trip_src.shape[1:]
    triplets, basis_width = basis.shape
    src, dst = trip_src[0], trip_dst[0]
    pieces = [shape((per_owner, width))] * ranks
    plane, hot = shape((width, triplets)), shape((slots, triplets))
    step = 256
    wide = 2 * triplets * slots * width
    narrow = 2 * triplets * basis_width * width
    dma = pltpu.SemaphoreType.DMA

    (both,) = call(
        pair_kernel,
        [shape((ranks, 2 * per_owner), jnp.int32)],
        [fetch_rows[0, 0], store_rows[0, 0]],
        far=(0, 1),
        scratch=[pltpu.VMEM((ranks, per_owner), jnp.int32)] * 2 + [dma((2,))],
        pin=True,
    )
    lists = exchange([both] * ranks, 1)
    lend = call(
        functools.partial(lend_kernel, ranks),
        pieces,
        [place] + lists + [edges],
        smem=(0,),
        far=(ranks + 1,),
        flops=2 * slots * edge_dev * width,
        scratch=[held(edges), dma((1,))],
        pin=True,
    )
    fetched = exchange(lend, -1)
    same, dhidden = call(
        functools.partial(owner_kernel, ranks),
        [shape((slots, slots)), shape((slots, width), F32)],
        [place] + lists + [upstream, w_out],
        smem=(0,),
        far=(ranks + 1, ranks + 2),
        flops=4 * slots * edge_dev * width,
        scratch=[held(upstream), held(w_out), dma((2,))],
        order=[lend[0]],
        pin=True,
    )
    partial_rows = call(
        functools.partial(forward_kernel, ranks, step),
        pieces,
        [place, block_count] + fetched + [src, dst, w_basis, basis],
        smem=(0, 1),
        far=(ranks + 5,),
        flops=2 * wide + narrow,
        scratch=[held(basis), held(plane), held(hot), held(hot), dma((1,))],
        order=[same],
        vmem=30,
        pin=True,
    )
    home = exchange(partial_rows, 1)
    back = call(
        functools.partial(return_kernel, ranks),
        pieces,
        home + [same, dhidden],
        flops=2 * slots * slots * width,
    )
    dpartial = exchange(back, -1)
    parts = ranks * copies
    part = width // parts
    term_dims = (width, width) if part % 16 else (parts, part, width)
    updated, out_term = call(
        functools.partial(update_kernel, ranks, 256),
        [shape((edge_dev, width)), shape(term_dims)],
        [place] + lists + home + [edges, upstream, w_out],
        smem=(0,),
        far=(2 * ranks + 1, 2 * ranks + 2, 2 * ranks + 3),
        far_out=(0,),
        flops=2 * edge_dev * width * (2 * width + slots),
        scratch=[held(edges), held(upstream), held(w_out), held(edges)]
        + [pltpu.VMEM((width, edge_dev), BF16), dma((3,)), dma((edge_dev // 256,))],
        order=[back[0]],
    )
    sent = out_term
    if part % 16:
        blocks_of = [reverse(k % copies, copies) * ranks + k // copies for k in range(parts)]
        split = out_term.reshape(parts, part, width)
        sent = jnp.stack([split[block] for block in blocks_of])
    out_parts = lax.all_to_all(sent, ("graph", "dp"), split_axis=0, concat_axis=0, tiled=True)
    basis_half = basis_width // 2
    basis_kept, basis_away, *dfetch = call(
        functools.partial(backward_kernel, ranks, step),
        [shape((basis_half, width), F32), shape((basis_half, width))] + pieces,
        [place, block_count] + fetched + dpartial + [src, dst, w_basis, basis],
        smem=(0, 1),
        far=(2 * ranks + 5,),
        flops=3 * wide + 2 * narrow,
        scratch=[held(basis), held(plane), held(plane), held(hot), held(hot)]
        + [pltpu.VMEM((basis_width, width), F32), dma((1,))],
        order=[out_term],
        vmem=36,
        pin=True,
    )
    returned = exchange(dfetch, 1)
    basis_part = joined(basis_kept, basis_away)
    for bit in bits_of("dp")[1:]:
        basis_part = halve(basis_part, "dp", bit)
    out_part = jnp.sum(out_parts.astype(F32), axis=0)
    out, total = out_part.astype(BF16), basis_part.astype(BF16)
    for bit in bits_of("graph"):
        early, late = (1, 2) if bit == 0 else (2, ranks)
        if bit < 2:
            tied = (out, total, returned[early:late])
            out, total, returned[early:late] = lax.optimization_barrier(tied)
        got, out = doubled(out, total, "graph", bit)
        total = (total.astype(F32) + got.astype(F32)).astype(BF16)
    (grad_edge,) = call(
        functools.partial(final_kernel, ranks, 256),
        [shape((edge_dev, width))],
        [place] + lists + returned + [upstream],
        smem=(0,),
        far=(2 * ranks + 1,),
        far_out=(0,),
        flops=2 * slots * edge_dev * width,
        scratch=[held(upstream), held(upstream), dma((1,)), dma((edge_dev // 256,))],
    )
    out, total, grad_edge = lax.optimization_barrier((out, total, grad_edge))
    for bit in reversed(bits_of("dp")):
        got, out = doubled(out, total, "dp", bit)
        total = double(total, got, "dp", bit)
    out_scale = jnp.sqrt(F32(copies * ranks * edge_dev))
    basis_scale = 2.0 * jnp.sqrt(F32(copies * ranks * blocks * block_rows))
    return (updated[None], grad_edge[None], out.astype(F32) / out_scale, total.astype(F32) / basis_scale)


def solution(mesh):
    placed = (
        P(("groups", "dp"), "graph", None),
        P(("groups", "dp"), "graph", None),
        P(("groups", "dp"), "graph", None, None),
        P(("groups", "dp"), "graph", None, None),
        P(("groups", "dp"), "graph", None),
        P(("groups", "dp"), "graph", None),
        P(("groups", "dp"), "graph", None),
        P(("groups", "dp"), "graph"),
        P(),
        P(),
    )
    return jax.shard_map(
        per_device,
        mesh=mesh,
        in_specs=placed,
        out_specs=(
            P(("groups", "dp"), "graph", None),
            P(("groups", "dp"), "graph", None),
            P("groups", None),
            P("groups", None),
        ),
        check_vma=False,
    )
```

```python
import functools
import math

import jax
import jax.numpy as jnp
from jax import lax
from jax.experimental import pallas as pl
from jax.experimental.pallas import tpu as pltpu
from jax.sharding import PartitionSpec as P

BF16 = jnp.bfloat16
F32 = jnp.float32
VMEM = pl.BlockSpec(memory_space=pltpu.VMEM)
SMEM = pl.BlockSpec(memory_space=pltpu.SMEM)
ANY = pl.BlockSpec(memory_space=pl.ANY)
HBM = pl.BlockSpec(memory_space=pltpu.HBM)
NN = (((1,), (0,)), ((), ()))
NT = (((1,), (1,)), ((), ()))


def dot(a, b, dims=NN):
    return lax.dot_general(a, b, dims, preferred_element_type=F32)


def silu_parts(half):
    tanh = jnp.tanh(half)
    upper = 1.0 + tanh
    act = half * upper
    return act, upper + act * (1.0 - tanh)


def call(body, outs, args, flops=0, scratch=(), smem=(), far=(), far_out=(), order=(), vmem=16, pin=False):
    args = [
        pltpu.with_memory_space_constraint(a, pltpu.HBM) if pin and i in far else a
        for i, a in enumerate(args)
    ] + list(order)
    moved = sum(a.size * a.dtype.itemsize for a in args) + sum(
        o.size * o.dtype.itemsize for o in outs
    )
    keep = len(args) - len(order)
    specs = [
        SMEM if i in smem else ANY if i >= keep else HBM if i in far else VMEM
        for i in range(len(args))
    ]

    def inner(*refs):
        body(*refs[:keep], *refs[len(args) :])

    return pl.pallas_call(
        inner if order else body,
        out_shape=tuple(outs),
        in_specs=specs,
        out_specs=tuple(HBM if i in far_out else VMEM for i in range(len(outs))),
        scratch_shapes=list(scratch),
        cost_estimate=pl.CostEstimate(flops=flops, bytes_accessed=moved, transcendentals=0),
        compiler_params=pltpu.CompilerParams(vmem_limit_bytes=vmem << 20),
    )(*args)


def shape(dims, dtype=BF16):
    return jax.ShapeDtypeStruct(dims, dtype)


def held(array):
    return pltpu.VMEM(array.shape, array.dtype)


def started(copies):
    for copy in copies:
        copy.start()
    return copies


def waited(copies):
    for copy in copies:
        copy.wait()


def loads(sources, targets, sems):
    return started(
        [pltpu.make_async_copy(a, b, sems.at[i]) for i, (a, b) in enumerate(zip(sources, targets))]
    )


def hot_lanes(index, first, count, slots, dead=None):
    block = index.shape[1]
    rows = lax.broadcasted_iota(jnp.int32, (slots, block), 0)
    parts = []
    for b in range(first, first + count):
        slot = index[pl.ds(b, 1), :]
        if dead is not None:
            slot = jnp.where(b < dead, slot, -1)
        parts.append(jnp.where(rows == slot, 1.0, 0.0).astype(BF16))
    return jnp.concatenate(parts, axis=1)


def turned(index, per_owner, ranks, me):
    slot = index[...] - me * per_owner
    return jnp.where(slot < 0, slot + ranks * per_owner, slot)


def gathered(pieces):
    return jnp.concatenate([p[...] for p in pieces], axis=0)


def scattered(value, outs):
    per = outs[0].shape[0]
    for s, out in enumerate(outs):
        out[...] = value[s * per : (s + 1) * per]


def columns_of(lists, me, kept, per_owner):
    parts = []
    for ref in lists:
        row = ref[pl.ds(me, 1), :].astype(F32)
        column = jnp.broadcast_to(row, (8, row.shape[1])).T[:, :1]
        parts.append(column[per_owner : 2 * per_owner] if kept else column[:per_owner])
    return jnp.concatenate(parts, axis=0)


def hot_rows(column, edge_dev):
    edges = lax.broadcasted_iota(jnp.int32, (column.shape[0], edge_dev), 1).astype(F32)
    return jnp.where(column == edges, 1.0, 0.0).astype(BF16)


def pair_kernel(fetch, store, out, fetch_v, store_v, sems):
    waited(loads([fetch, store], [fetch_v, store_v], sems))
    out[...] = jnp.concatenate([fetch_v[...], store_v[...]], axis=1)


def near_kernel(edges, out, sems):
    waited(loads([edges], [out], sems))


def lend_kernel(ranks, me, *refs):
    lists, edges, outs = refs[:ranks], refs[ranks], refs[ranks + 1 :]
    hot = hot_rows(columns_of(lists, me[0], False, outs[0].shape[0]), edges.shape[0])
    scattered(dot(hot, edges[...]).astype(BF16), outs)


def owner_kernel(ranks, me, *refs):
    lists, (upstream, w_out, same, dhidden) = refs[:ranks], refs[ranks : ranks + 4]
    upstream_v, w_out_v, sems = refs[ranks + 4 :]
    arrive = loads([upstream, w_out], [upstream_v, w_out_v], sems)
    hot = hot_rows(columns_of(lists, me[0], True, same.shape[0] // ranks), upstream.shape[0])
    same[...] = dot(hot, hot, NT).astype(BF16)
    waited(arrive)
    dhidden[...] = dot(dot(hot, upstream_v[...]).astype(BF16), w_out_v[...], NT)


def forward_kernel(ranks, step, place, count, *refs):
    pieces, (src, dst, weight, basis) = refs[:ranks], refs[ranks : ranks + 4]
    outs = refs[ranks + 4 : 2 * ranks + 4]
    basis_v, message, hot, near_hot, sems = refs[2 * ranks + 4 :]
    arrive = loads([basis], [basis_v], sems)
    per_owner = outs[0].shape[0]
    slots, block = ranks * per_owner, src.shape[1]
    table, weight_t = gathered(pieces).T, (0.5 * weight[...]).T
    src_t = turned(src, per_owner, ranks, place[0])
    dst_t = turned(dst, per_owner, ranks, place[0])
    each = step // block
    spans = [pl.ds(i * step, step) for i in range(basis.shape[0] // step)]
    for i, at in enumerate(spans):
        near_hot[:, at] = hot_lanes(src_t, i * each, each, slots)
        hot[:, at] = hot_lanes(dst_t, i * each, each, slots, count[0, 0])
    waited(arrive)
    for at in spans:
        act = silu_parts(dot(weight_t, basis_v[at, :], NT))[0]
        message[:, at] = (dot(table, near_hot[:, at]) * act).astype(BF16)
    scattered(dot(hot[...], message[...], NT).astype(BF16), outs)


def return_kernel(ranks, *refs):
    pieces, (same, dhidden), outs = refs[:ranks], refs[ranks : ranks + 2], refs[ranks + 2 :]
    agg = dot(same[...], gathered(pieces))
    scattered((dhidden[...] * (0.5 * silu_parts(0.5 * agg)[1])).astype(BF16), outs)


def reverse(value, count):
    bits = count.bit_length() - 1
    return sum(((value >> b) & 1) << (bits - 1 - b) for b in range(bits))


def update_kernel(ranks, step, me, *refs):
    lists, pieces = refs[:ranks], refs[ranks : 2 * ranks]
    edges, upstream, w_out, updated, term = refs[2 * ranks : 2 * ranks + 5]
    edges_v, upstream_v, w_out_v, updated_v, hidden, sems, out_sems = refs[2 * ranks + 5 :]
    arrive = loads([w_out, edges, upstream], [w_out_v, edges_v, upstream_v], sems)
    home = gathered(pieces)
    rows = edges.shape[0]
    hot_t = hot_rows(columns_of(lists, me[0], True, pieces[0].shape[0]), rows).T
    turns = rows // step
    spans = [pl.ds(i * step, step) for i in range(turns)]
    leave = [
        pltpu.make_async_copy(updated_v.at[at, :], updated.at[at, :], out_sems.at[i])
        for i, at in enumerate(spans)
    ]
    fresh = [
        silu_parts(0.5 * dot(hot_t[i * step : (i + 1) * step], home))[0].astype(BF16)
        for i in range(turns)
    ]
    waited(arrive)
    for i, at in enumerate(spans):
        total = edges_v[at, :].astype(F32) + dot(fresh[i], w_out_v[...])
        updated_v[at, :] = total.astype(BF16)
        leave[i].start()
        hidden[:, at] = fresh[i].T
    total = dot(hidden[...], upstream_v[...]).astype(BF16)
    if len(term.shape) == 2:
        term[...] = total
    else:
        parts, part = term.shape[0], term.shape[1]
        copies = parts // ranks
        for k in range(parts):
            block = reverse(k % copies, copies) * ranks + reverse(k // copies, ranks)
            term[k] = total[block * part : (block + 1) * part]
    waited(leave)


def backward_kernel(ranks, step, place, count, *refs):
    fetched, pieces = refs[:ranks], refs[ranks : 2 * ranks]
    src, dst, weight, basis, kept, away = refs[2 * ranks : 2 * ranks + 6]
    outs = refs[2 * ranks + 6 : 3 * ranks + 6]
    basis_v, message, dpre, hot, back_hot, total, sems = refs[3 * ranks + 6 :]
    arrive = loads([basis], [basis_v], sems)
    per_owner = outs[0].shape[0]
    slots, block = ranks * per_owner, src.shape[1]
    src_t = turned(src, per_owner, ranks, place[0])
    dst_t = turned(dst, per_owner, ranks, place[0])
    near, back = gathered(fetched).T, gathered(pieces).T
    weight_t = (0.5 * weight[...]).T
    each = step // block
    spans = [pl.ds(i * step, step) for i in range(basis.shape[0] // step)]
    for i, at in enumerate(spans):
        hot[:, at] = hot_lanes(src_t, i * each, each, slots)
        back_hot[:, at] = hot_lanes(dst_t, i * each, each, slots, count[0, 0])
    waited(arrive)
    for at in spans:
        act, slope = silu_parts(dot(weight_t, basis_v[at, :], NT))
        rows = dot(back, back_hot[:, at]).astype(BF16)
        message[:, at] = rows * act.astype(BF16)
        dpre[:, at] = rows * dot(near, hot[:, at]).astype(BF16) * slope.astype(BF16)
    total[...] = dot(dpre[...], basis_v[...]).T
    half = kept.shape[0]
    kept[...] = total[pl.ds(pl.multiple_of(place[1] * half, half), half), :]
    away[...] = total[pl.ds(pl.multiple_of((1 - place[1]) * half, half), half), :].astype(BF16)
    scattered(dot(hot[...], message[...], NT).astype(BF16), outs)


def final_kernel(ranks, step, me, *refs):
    lists, pieces = refs[:ranks], refs[ranks : 2 * ranks]
    upstream, out, upstream_v, out_v, sems, out_sems = refs[2 * ranks :]
    arrive = loads([upstream], [upstream_v], sems)
    back = gathered(pieces)
    rows = upstream.shape[0]
    hot_t = hot_rows(columns_of(lists, me[0], False, pieces[0].shape[0]), rows).T
    waited(arrive)
    leave = []
    for i in range(rows // step):
        at = pl.ds(i * step, step)
        total = upstream_v[at, :].astype(F32) + dot(hot_t[i * step : (i + 1) * step], back)
        out_v[at, :] = total.astype(BF16)
        leave.append(pltpu.make_async_copy(out_v.at[at, :], out.at[at, :], out_sems.at[i]))
        leave[i].start()
    waited(leave)


def finish_kernel(scales, low, out, out_got, basis, basis_got, out_full, basis_full):
    for own, got, full, scale in (
        (out, out_got, out_full, scales[0]),
        (basis, basis_got, basis_full, scales[1]),
    ):
        rows = own.shape[0]
        mine = pl.multiple_of(low[1] * rows, rows)
        other = pl.multiple_of((1 - low[1]) * rows, rows)
        full[pl.ds(mine, rows), :] = own[...].astype(F32) * scale
        full[pl.ds(other, rows), :] = got[...].astype(F32) * scale


def swap(value, axis, mask):
    return lax.ppermute(value, axis, [(k, k ^ mask) for k in range(lax.axis_size(axis))])


def shift(value, axis, by):
    count = lax.axis_size(axis)
    return lax.ppermute(value, axis, [(k, (k + by) % count) for k in range(count)])


def exchange(pieces, sign):
    return [pieces[0]] + [shift(pieces[s], "graph", sign * s) for s in range(1, len(pieces))]


def halve(value, axis, bit):
    half = value.reshape(2, value.shape[0] // 2, value.shape[1])
    own = (lax.axis_index(axis) >> bit) & 1
    away = lax.dynamic_index_in_dim(half, 1 - own, 0, keepdims=False).astype(BF16)
    kept = lax.dynamic_index_in_dim(half, own, 0, keepdims=False)
    return kept.astype(F32) + swap(away, axis, 1 << bit).astype(F32)


def double(value, got, axis, bit):
    low = ((lax.axis_index(axis) >> bit) & 1) == 0
    return jnp.where(low, jnp.concatenate([value, got]), jnp.concatenate([got, value]))


def bits_of(axis):
    return range(lax.axis_size(axis).bit_length() - 1)


def joined(kept, away):
    return kept + swap(away, "dp", 1).astype(F32)


def doubled(out, basis, axis, bit):
    rows = basis.shape[0]
    got = swap(jnp.concatenate([basis, out]), axis, 1 << bit)
    return got[:rows], double(out, got[rows:], axis, bit)


def per_device(
    edge_emb,
    cotangent,
    fetch_rows,
    store_rows,
    trip_src,
    trip_dst,
    trip_basis,
    block_count,
    w_basis,
    w_out,
):
    edges, upstream, basis = edge_emb[0], cotangent[0], trip_basis[0]
    ranks, copies = lax.axis_size("graph"), lax.axis_size("dp")
    place = jnp.stack([lax.axis_index("graph"), lax.axis_index("dp") & 1]).astype(jnp.int32)
    edge_dev, width = edges.shape
    per_owner = fetch_rows.shape[3]
    slots = ranks * per_owner
    blocks, block_rows = trip_src.shape[1:]
    triplets, basis_width = basis.shape
    src, dst = trip_src[0], trip_dst[0]
    pieces = [shape((per_owner, width))] * ranks
    plane, hot = shape((width, triplets)), shape((slots, triplets))
    step = 256
    wide = 2 * triplets * slots * width
    narrow = 2 * triplets * basis_width * width
    dma = pltpu.SemaphoreType.DMA

    (both,) = call(
        pair_kernel,
        [shape((ranks, 2 * per_owner), jnp.int32)],
        [fetch_rows[0, 0], store_rows[0, 0]],
        far=(0, 1),
        scratch=[pltpu.VMEM((ranks, per_owner), jnp.int32)] * 2 + [dma((2,))],
        pin=True,
    )
    lists = exchange([both] * ranks, 1)
    (near,) = call(
        near_kernel,
        [shape(edges.shape)],
        [edges],
        far=(0,),
        flops=wide,
        scratch=[dma((1,))],
        order=[both],
        pin=True,
    )
    lend = call(
        functools.partial(lend_kernel, ranks),
        pieces,
        [place] + lists + [near],
        smem=(0,),
        flops=2 * slots * edge_dev * width,
    )
    fetched = exchange(lend, -1)
    same, dhidden = call(
        functools.partial(owner_kernel, ranks),
        [shape((slots, slots)), shape((slots, width), F32)],
        [place] + lists + [upstream, w_out],
        smem=(0,),
        far=(ranks + 1, ranks + 2),
        flops=4 * slots * edge_dev * width,
        scratch=[held(upstream), held(w_out), dma((2,))],
        order=[lend[0]],
        pin=True,
    )
    partial_rows = call(
        functools.partial(forward_kernel, ranks, step),
        pieces,
        [place, block_count] + fetched + [src, dst, w_basis, basis],
        smem=(0, 1),
        far=(ranks + 5,),
        flops=2 * wide + narrow,
        scratch=[held(basis), held(plane), held(hot), held(hot), dma((1,))],
        order=[same],
        vmem=30,
        pin=True,
    )
    home = exchange(partial_rows, 1)
    back = call(
        functools.partial(return_kernel, ranks),
        pieces,
        home + [same, dhidden],
        flops=2 * slots * slots * width,
    )
    dpartial = exchange(back, -1)
    parts = ranks * copies
    part = width // parts
    term_dims = (width, width) if part % 16 else (parts, part, width)
    updated, out_term = call(
        functools.partial(update_kernel, ranks, 256),
        [shape((edge_dev, width)), shape(term_dims)],
        [place] + lists + home + [edges, upstream, w_out],
        smem=(0,),
        far=(2 * ranks + 1, 2 * ranks + 2, 2 * ranks + 3),
        far_out=(0,),
        flops=2 * edge_dev * width * (2 * width + slots),
        scratch=[held(edges), held(upstream), held(w_out), held(edges)]
        + [pltpu.VMEM((width, edge_dev), BF16), dma((3,)), dma((edge_dev // 256,))],
        order=[back[0]],
    )
    sent = out_term
    if part % 16:
        blocks_of = [
            reverse(k % copies, copies) * ranks + reverse(k // copies, ranks) for k in range(parts)
        ]
        split = out_term.reshape(parts, part, width)
        sent = jnp.stack([split[block] for block in blocks_of])
    out_parts = lax.all_to_all(sent, ("graph", "dp"), split_axis=0, concat_axis=0, tiled=True)
    basis_half = basis_width // 2
    basis_kept, basis_away, *dfetch = call(
        functools.partial(backward_kernel, ranks, step),
        [shape((basis_half, width), F32), shape((basis_half, width))] + pieces,
        [place, block_count] + fetched + dpartial + [src, dst, w_basis, basis],
        smem=(0, 1),
        far=(2 * ranks + 5,),
        flops=3 * wide + 2 * narrow,
        scratch=[held(basis), held(plane), held(plane), held(hot), held(hot)]
        + [pltpu.VMEM((basis_width, width), F32), dma((1,))],
        order=[out_term],
        vmem=36,
        pin=True,
    )
    returned = exchange(dfetch, 1)
    basis_part = joined(basis_kept, basis_away)
    for bit in bits_of("dp")[1:]:
        basis_part = halve(basis_part, "dp", bit)
    out_part = jnp.sum(out_parts.astype(F32), axis=0)
    out, total = out_part.astype(BF16), basis_part.astype(BF16)
    for bit in reversed(bits_of("graph")):
        if bit == 0:
            out, total, returned = lax.optimization_barrier((out, total, returned))
        got, out = doubled(out, total, "graph", bit)
        total = (total.astype(F32) + got.astype(F32)).astype(BF16)
    (grad_edge,) = call(
        functools.partial(final_kernel, ranks, 256),
        [shape((edge_dev, width))],
        [place] + lists + returned + [upstream],
        smem=(0,),
        far=(2 * ranks + 1,),
        far_out=(0,),
        flops=2 * slots * edge_dev * width,
        scratch=[held(upstream), held(upstream), dma((1,)), dma((edge_dev // 256,))],
    )
    out, total, grad_edge = lax.optimization_barrier((out, total, grad_edge))
    for bit in reversed(bits_of("dp")[1:]):
        got, out = doubled(out, total, "dp", bit)
        total = double(total, got, "dp", bit)
    rows = total.shape[0]
    got = swap(jnp.concatenate([total, out]), "dp", 1)
    out_scale = 1.0 / math.sqrt(copies * ranks * edge_dev)
    basis_scale = 0.5 / math.sqrt(copies * ranks * blocks * block_rows)
    grad_w_out, grad_w_basis = call(
        functools.partial(finish_kernel, (out_scale, basis_scale)),
        [shape((width, width), F32), shape((basis_width, width), F32)],
        [place, out, got[rows:], total, got[:rows]],
        smem=(0,),
    )
    return (updated[None], grad_edge[None], grad_w_out, grad_w_basis)


def solution(mesh):
    placed = (
        P(("groups", "dp"), "graph", None),
        P(("groups", "dp"), "graph", None),
        P(("groups", "dp"), "graph", None, None),
        P(("groups", "dp"), "graph", None, None),
        P(("groups", "dp"), "graph", None),
        P(("groups", "dp"), "graph", None),
        P(("groups", "dp"), "graph", None),
        P(("groups", "dp"), "graph"),
        P(),
        P(),
    )
    return jax.shard_map(
        per_device,
        mesh=mesh,
        in_specs=placed,
        out_specs=(
            P(("groups", "dp"), "graph", None),
            P(("groups", "dp"), "graph", None),
            P("groups", None),
            P("groups", None),
        ),
        check_vma=False,
    )
```

```python
import functools
import math

import jax
import jax.numpy as jnp
from jax import lax
from jax.experimental import pallas as pl
from jax.experimental.pallas import tpu as pltpu
from jax.sharding import PartitionSpec as P

BF16 = jnp.bfloat16
F32 = jnp.float32
VMEM = pl.BlockSpec(memory_space=pltpu.VMEM)
SMEM = pl.BlockSpec(memory_space=pltpu.SMEM)
ANY = pl.BlockSpec(memory_space=pl.ANY)
HBM = pl.BlockSpec(memory_space=pltpu.HBM)
NN = (((1,), (0,)), ((), ()))
NT = (((1,), (1,)), ((), ()))


def dot(a, b, dims=NN):
    return lax.dot_general(a, b, dims, preferred_element_type=F32)


def silu_parts(half):
    tanh = jnp.tanh(half)
    upper = 1.0 + tanh
    act = half * upper
    return act, upper + act * (1.0 - tanh)


def call(body, outs, args, flops=0, scratch=(), smem=(), far=(), far_out=(), order=(), vmem=16, pin=False):
    args = [
        pltpu.with_memory_space_constraint(a, pltpu.HBM) if pin and i in far else a
        for i, a in enumerate(args)
    ] + list(order)
    moved = sum(a.size * a.dtype.itemsize for a in args) + sum(
        o.size * o.dtype.itemsize for o in outs
    )
    keep = len(args) - len(order)
    specs = [
        SMEM if i in smem else ANY if i >= keep else HBM if i in far else VMEM
        for i in range(len(args))
    ]

    def inner(*refs):
        body(*refs[:keep], *refs[len(args) :])

    return pl.pallas_call(
        inner if order else body,
        out_shape=tuple(outs),
        in_specs=specs,
        out_specs=tuple(HBM if i in far_out else VMEM for i in range(len(outs))),
        scratch_shapes=list(scratch),
        cost_estimate=pl.CostEstimate(flops=flops, bytes_accessed=moved, transcendentals=0),
        compiler_params=pltpu.CompilerParams(vmem_limit_bytes=vmem << 20),
    )(*args)


def shape(dims, dtype=BF16):
    return jax.ShapeDtypeStruct(dims, dtype)


def held(array):
    return pltpu.VMEM(array.shape, array.dtype)


def started(copies):
    for copy in copies:
        copy.start()
    return copies


def waited(copies):
    for copy in copies:
        copy.wait()


def loads(sources, targets, sems):
    return started(
        [pltpu.make_async_copy(a, b, sems.at[i]) for i, (a, b) in enumerate(zip(sources, targets))]
    )


def hot_lanes(index, first, count, slots, dead=None):
    block = index.shape[1]
    rows = lax.broadcasted_iota(jnp.int32, (slots, block), 0)
    parts = []
    for b in range(first, first + count):
        slot = index[pl.ds(b, 1), :]
        if dead is not None:
            slot = jnp.where(b < dead, slot, -1)
        parts.append(jnp.where(rows == slot, 1.0, 0.0).astype(BF16))
    return jnp.concatenate(parts, axis=1)


def turned(index, per_owner, ranks, me):
    slot = index[...] - me * per_owner
    return jnp.where(slot < 0, slot + ranks * per_owner, slot)


def gathered(pieces):
    return jnp.concatenate([p[...] for p in pieces], axis=0)


def scattered(value, outs):
    per = outs[0].shape[0]
    for s, out in enumerate(outs):
        out[...] = value[s * per : (s + 1) * per]


def columns_of(lists, me, kept, per_owner):
    parts = []
    for ref in lists:
        row = ref[pl.ds(me, 1), :].astype(F32)
        column = jnp.broadcast_to(row, (8, row.shape[1])).T[:, :1]
        parts.append(column[per_owner : 2 * per_owner] if kept else column[:per_owner])
    return jnp.concatenate(parts, axis=0)


def hot_edges(lists, me, kept, per_owner, edge_dev):
    first = per_owner if kept else 0
    row = jnp.concatenate(
        [ref[pl.ds(me, 1), :][:, first : first + per_owner] for ref in lists], axis=1
    )
    edges = lax.broadcasted_iota(jnp.int32, (edge_dev, row.shape[1]), 0)
    return jnp.where(edges == row, 1.0, 0.0).astype(BF16)


def hot_rows(column, edge_dev):
    edges = lax.broadcasted_iota(jnp.int32, (column.shape[0], edge_dev), 1).astype(F32)
    return jnp.where(column == edges, 1.0, 0.0).astype(BF16)


def pair_kernel(fetch, store, out, fetch_v, store_v, sems):
    waited(loads([fetch, store], [fetch_v, store_v], sems))
    out[...] = jnp.concatenate([fetch_v[...], store_v[...]], axis=1)


def near_kernel(edges, out, sems):
    waited(loads([edges], [out], sems))


def lend_kernel(ranks, me, *refs):
    lists, edges, outs = refs[:ranks], refs[ranks], refs[ranks + 1 :]
    hot = hot_rows(columns_of(lists, me[0], False, outs[0].shape[0]), edges.shape[0])
    scattered(dot(hot, edges[...]).astype(BF16), outs)


def owner_kernel(ranks, me, *refs):
    lists, (upstream, w_out, same, dhidden) = refs[:ranks], refs[ranks : ranks + 4]
    upstream_v, w_out_v, sems = refs[ranks + 4 :]
    arrive = loads([upstream, w_out], [upstream_v, w_out_v], sems)
    hot = hot_rows(columns_of(lists, me[0], True, same.shape[0] // ranks), upstream.shape[0])
    same[...] = dot(hot, hot, NT).astype(BF16)
    waited(arrive)
    dhidden[...] = dot(dot(hot, upstream_v[...]).astype(BF16), w_out_v[...], NT)


def forward_kernel(ranks, step, place, count, *refs):
    pieces, (src, dst, weight, basis) = refs[:ranks], refs[ranks : ranks + 4]
    outs = refs[ranks + 4 : 2 * ranks + 4]
    basis_v, message, hot, near_hot, sems = refs[2 * ranks + 4 :]
    arrive = loads([basis], [basis_v], sems)
    per_owner = outs[0].shape[0]
    slots, block = ranks * per_owner, src.shape[1]
    table, weight_t = gathered(pieces).T, (0.5 * weight[...]).T
    src_t = turned(src, per_owner, ranks, place[0])
    dst_t = turned(dst, per_owner, ranks, place[0])
    each = step // block
    spans = [pl.ds(i * step, step) for i in range(basis.shape[0] // step)]
    for i, at in enumerate(spans):
        near_hot[:, at] = hot_lanes(src_t, i * each, each, slots)
        hot[:, at] = hot_lanes(dst_t, i * each, each, slots, count[0, 0])
    waited(arrive)
    for at in spans:
        act = silu_parts(dot(weight_t, basis_v[at, :], NT))[0]
        message[:, at] = (dot(table, near_hot[:, at]) * act).astype(BF16)
    scattered(dot(hot[...], message[...], NT).astype(BF16), outs)


def return_kernel(ranks, *refs):
    pieces, (same, dhidden), outs = refs[:ranks], refs[ranks : ranks + 2], refs[ranks + 2 :]
    agg = dot(same[...], gathered(pieces))
    scattered((dhidden[...] * (0.5 * silu_parts(0.5 * agg)[1])).astype(BF16), outs)


def reverse(value, count):
    bits = count.bit_length() - 1
    return sum(((value >> b) & 1) << (bits - 1 - b) for b in range(bits))


def update_kernel(ranks, step, me, *refs):
    lists, pieces = refs[:ranks], refs[ranks : 2 * ranks]
    edges, upstream, w_out, updated, term = refs[2 * ranks : 2 * ranks + 5]
    edges_v, upstream_v, w_out_v, updated_v, hidden, sems, out_sems = refs[2 * ranks + 5 :]
    arrive = loads([w_out, edges, upstream], [w_out_v, edges_v, upstream_v], sems)
    home = gathered(pieces)
    rows = edges.shape[0]
    hot_t = hot_edges(lists, me[0], True, pieces[0].shape[0], rows)
    turns = rows // step
    spans = [pl.ds(i * step, step) for i in range(turns)]
    leave = [
        pltpu.make_async_copy(updated_v.at[at, :], updated.at[at, :], out_sems.at[i])
        for i, at in enumerate(spans)
    ]
    fresh = [
        silu_parts(0.5 * dot(hot_t[i * step : (i + 1) * step], home))[0].astype(BF16)
        for i in range(turns)
    ]
    waited(arrive)
    for i, at in enumerate(spans):
        total = edges_v[at, :].astype(F32) + dot(fresh[i], w_out_v[...])
        updated_v[at, :] = total.astype(BF16)
        leave[i].start()
        hidden[:, at] = fresh[i].T
    total = dot(hidden[...], upstream_v[...]).astype(BF16)
    if len(term.shape) == 2:
        term[...] = total
    else:
        parts, part = term.shape[0], term.shape[1]
        copies = parts // ranks
        for k in range(parts):
            block = reverse(k % copies, copies) * ranks + reverse(k // copies, ranks)
            term[k] = total[block * part : (block + 1) * part]
    waited(leave)


def backward_kernel(ranks, step, place, count, *refs):
    fetched, pieces = refs[:ranks], refs[ranks : 2 * ranks]
    src, dst, weight, basis, kept, away = refs[2 * ranks : 2 * ranks + 6]
    outs = refs[2 * ranks + 6 : 3 * ranks + 6]
    basis_v, message, dpre, hot, back_hot, total, sems = refs[3 * ranks + 6 :]
    arrive = loads([basis], [basis_v], sems)
    per_owner = outs[0].shape[0]
    slots, block = ranks * per_owner, src.shape[1]
    src_t = turned(src, per_owner, ranks, place[0])
    dst_t = turned(dst, per_owner, ranks, place[0])
    near, back = gathered(fetched).T, gathered(pieces).T
    weight_t = (0.5 * weight[...]).T
    each = step // block
    spans = [pl.ds(i * step, step) for i in range(basis.shape[0] // step)]
    for i, at in enumerate(spans):
        hot[:, at] = hot_lanes(src_t, i * each, each, slots)
        back_hot[:, at] = hot_lanes(dst_t, i * each, each, slots, count[0, 0])
    waited(arrive)
    for at in spans:
        act, slope = silu_parts(dot(weight_t, basis_v[at, :], NT))
        rows = dot(back, back_hot[:, at]).astype(BF16)
        message[:, at] = rows * act.astype(BF16)
        dpre[:, at] = rows * dot(near, hot[:, at]).astype(BF16) * slope.astype(BF16)
    total[...] = dot(dpre[...], basis_v[...]).T
    half = kept.shape[0]
    kept[...] = total[pl.ds(pl.multiple_of(place[1] * half, half), half), :]
    away[...] = total[pl.ds(pl.multiple_of((1 - place[1]) * half, half), half), :].astype(BF16)
    scattered(dot(hot[...], message[...], NT).astype(BF16), outs)


def final_kernel(ranks, step, me, *refs):
    lists, pieces = refs[:ranks], refs[ranks : 2 * ranks]
    upstream, out, upstream_v, out_v, sems, out_sems = refs[2 * ranks :]
    arrive = loads([upstream], [upstream_v], sems)
    back = gathered(pieces)
    rows = upstream.shape[0]
    hot_t = hot_edges(lists, me[0], False, pieces[0].shape[0], rows)
    waited(arrive)
    leave = []
    for i in range(rows // step):
        at = pl.ds(i * step, step)
        total = upstream_v[at, :].astype(F32) + dot(hot_t[i * step : (i + 1) * step], back)
        out_v[at, :] = total.astype(BF16)
        leave.append(pltpu.make_async_copy(out_v.at[at, :], out.at[at, :], out_sems.at[i]))
        leave[i].start()
    waited(leave)


def finish_kernel(scales, low, out, out_got, basis, basis_got, out_full, basis_full):
    for own, got, full, scale in (
        (out, out_got, out_full, scales[0]),
        (basis, basis_got, basis_full, scales[1]),
    ):
        rows = own.shape[0]
        mine = pl.multiple_of(low[1] * rows, rows)
        other = pl.multiple_of((1 - low[1]) * rows, rows)
        full[pl.ds(mine, rows), :] = own[...].astype(F32) * scale
        full[pl.ds(other, rows), :] = got[...].astype(F32) * scale


def swap(value, axis, mask):
    return lax.ppermute(value, axis, [(k, k ^ mask) for k in range(lax.axis_size(axis))])


def shift(value, axis, by):
    count = lax.axis_size(axis)
    return lax.ppermute(value, axis, [(k, (k + by) % count) for k in range(count)])


def exchange(pieces, sign):
    return [pieces[0]] + [shift(pieces[s], "graph", sign * s) for s in range(1, len(pieces))]


def halve(value, axis, bit):
    half = value.reshape(2, value.shape[0] // 2, value.shape[1])
    own = (lax.axis_index(axis) >> bit) & 1
    away = lax.dynamic_index_in_dim(half, 1 - own, 0, keepdims=False).astype(BF16)
    kept = lax.dynamic_index_in_dim(half, own, 0, keepdims=False)
    return kept.astype(F32) + swap(away, axis, 1 << bit).astype(F32)


def double(value, got, axis, bit):
    low = ((lax.axis_index(axis) >> bit) & 1) == 0
    return jnp.where(low, jnp.concatenate([value, got]), jnp.concatenate([got, value]))


def bits_of(axis):
    return range(lax.axis_size(axis).bit_length() - 1)


def joined(kept, away):
    return kept + swap(away, "dp", 1).astype(F32)


def doubled(out, basis, axis, bit):
    rows = basis.shape[0]
    got = swap(jnp.concatenate([basis, out]), axis, 1 << bit)
    return got[:rows], double(out, got[rows:], axis, bit)


def per_device(
    edge_emb,
    cotangent,
    fetch_rows,
    store_rows,
    trip_src,
    trip_dst,
    trip_basis,
    block_count,
    w_basis,
    w_out,
):
    edges, upstream, basis = edge_emb[0], cotangent[0], trip_basis[0]
    ranks, copies = lax.axis_size("graph"), lax.axis_size("dp")
    place = jnp.stack([lax.axis_index("graph"), lax.axis_index("dp") & 1]).astype(jnp.int32)
    edge_dev, width = edges.shape
    per_owner = fetch_rows.shape[3]
    slots = ranks * per_owner
    blocks, block_rows = trip_src.shape[1:]
    triplets, basis_width = basis.shape
    src, dst = trip_src[0], trip_dst[0]
    pieces = [shape((per_owner, width))] * ranks
    plane, hot = shape((width, triplets)), shape((slots, triplets))
    step = 256
    wide = 2 * triplets * slots * width
    narrow = 2 * triplets * basis_width * width
    dma = pltpu.SemaphoreType.DMA

    (both,) = call(
        pair_kernel,
        [shape((ranks, 2 * per_owner), jnp.int32)],
        [fetch_rows[0, 0], store_rows[0, 0]],
        far=(0, 1),
        scratch=[pltpu.VMEM((ranks, per_owner), jnp.int32)] * 2 + [dma((2,))],
        pin=True,
    )
    lists = exchange([both] * ranks, 1)
    (near,) = call(
        near_kernel,
        [shape(edges.shape)],
        [edges],
        far=(0,),
        flops=wide,
        scratch=[dma((1,))],
        order=[both],
        pin=True,
    )
    lend = call(
        functools.partial(lend_kernel, ranks),
        pieces,
        [place] + lists + [near],
        smem=(0,),
        flops=2 * slots * edge_dev * width,
    )
    fetched = exchange(lend, -1)
    same, dhidden = call(
        functools.partial(owner_kernel, ranks),
        [shape((slots, slots)), shape((slots, width), F32)],
        [place] + lists + [upstream, w_out],
        smem=(0,),
        far=(ranks + 1, ranks + 2),
        flops=4 * slots * edge_dev * width,
        scratch=[held(upstream), held(w_out), dma((2,))],
        order=[lend[0]],
        pin=True,
    )
    partial_rows = call(
        functools.partial(forward_kernel, ranks, step),
        pieces,
        [place, block_count] + fetched + [src, dst, w_basis, basis],
        smem=(0, 1),
        far=(ranks + 5,),
        flops=2 * wide + narrow,
        scratch=[held(basis), held(plane), held(hot), held(hot), dma((1,))],
        order=[same],
        vmem=30,
        pin=True,
    )
    home = exchange(partial_rows, 1)
    back = call(
        functools.partial(return_kernel, ranks),
        pieces,
        home + [same, dhidden],
        flops=2 * slots * slots * width,
    )
    dpartial = exchange(back, -1)
    parts = ranks * copies
    part = width // parts
    term_dims = (width, width) if part % 16 else (parts, part, width)
    updated, out_term = call(
        functools.partial(update_kernel, ranks, 256),
        [shape((edge_dev, width)), shape(term_dims)],
        [place] + lists + home + [edges, upstream, w_out],
        smem=(0,),
        far=(2 * ranks + 1, 2 * ranks + 2, 2 * ranks + 3),
        far_out=(0,),
        flops=2 * edge_dev * width * (2 * width + slots),
        scratch=[held(edges), held(upstream), held(w_out), held(edges)]
        + [pltpu.VMEM((width, edge_dev), BF16), dma((3,)), dma((edge_dev // 256,))],
        order=[back[0]],
    )
    sent = out_term
    if part % 16:
        blocks_of = [
            reverse(k % copies, copies) * ranks + reverse(k // copies, ranks) for k in range(parts)
        ]
        split = out_term.reshape(parts, part, width)
        sent = jnp.stack([split[block] for block in blocks_of])
    out_parts = lax.all_to_all(sent, ("graph", "dp"), split_axis=0, concat_axis=0, tiled=True)
    basis_half = basis_width // 2
    basis_kept, basis_away, *dfetch = call(
        functools.partial(backward_kernel, ranks, step),
        [shape((basis_half, width), F32), shape((basis_half, width))] + pieces,
        [place, block_count] + fetched + dpartial + [src, dst, w_basis, basis],
        smem=(0, 1),
        far=(2 * ranks + 5,),
        flops=3 * wide + 2 * narrow,
        scratch=[held(basis), held(plane), held(plane), held(hot), held(hot)]
        + [pltpu.VMEM((basis_width, width), F32), dma((1,))],
        order=[out_term],
        vmem=36,
        pin=True,
    )
    returned = exchange(dfetch, 1)
    basis_part = joined(basis_kept, basis_away)
    for bit in bits_of("dp")[1:]:
        basis_part = halve(basis_part, "dp", bit)
    out_part = jnp.sum(out_parts.astype(F32), axis=0)
    out, total = out_part.astype(BF16), basis_part.astype(BF16)
    for bit in reversed(bits_of("graph")):
        if bit == 0:
            out, total, returned = lax.optimization_barrier((out, total, returned))
        got, out = doubled(out, total, "graph", bit)
        total = (total.astype(F32) + got.astype(F32)).astype(BF16)
    (grad_edge,) = call(
        functools.partial(final_kernel, ranks, 256),
        [shape((edge_dev, width))],
        [place] + lists + returned + [upstream],
        smem=(0,),
        far=(2 * ranks + 1,),
        far_out=(0,),
        flops=2 * slots * edge_dev * width,
        scratch=[held(upstream), held(upstream), dma((1,)), dma((edge_dev // 256,))],
    )
    out, total, grad_edge = lax.optimization_barrier((out, total, grad_edge))
    for bit in reversed(bits_of("dp")[1:]):
        got, out = doubled(out, total, "dp", bit)
        total = double(total, got, "dp", bit)
    rows = total.shape[0]
    got = swap(jnp.concatenate([total, out]), "dp", 1)
    out_scale = 1.0 / math.sqrt(copies * ranks * edge_dev)
    basis_scale = 0.5 / math.sqrt(copies * ranks * blocks * block_rows)
    grad_w_out, grad_w_basis = call(
        functools.partial(finish_kernel, (out_scale, basis_scale)),
        [shape((width, width), F32), shape((basis_width, width), F32)],
        [place, out, got[rows:], total, got[:rows]],
        smem=(0,),
    )
    return (updated[None], grad_edge[None], grad_w_out, grad_w_basis)


def solution(mesh):
    placed = (
        P(("groups", "dp"), "graph", None),
        P(("groups", "dp"), "graph", None),
        P(("groups", "dp"), "graph", None, None),
        P(("groups", "dp"), "graph", None, None),
        P(("groups", "dp"), "graph", None),
        P(("groups", "dp"), "graph", None),
        P(("groups", "dp"), "graph", None),
        P(("groups", "dp"), "graph"),
        P(),
        P(),
    )
    return jax.shard_map(
        per_device,
        mesh=mesh,
        in_specs=placed,
        out_specs=(
            P(("groups", "dp"), "graph", None),
            P(("groups", "dp"), "graph", None),
            P("groups", None),
            P("groups", None),
        ),
        check_vma=False,
    )
```

```python
import functools
import math

import jax
import jax.numpy as jnp
from jax import lax
from jax.experimental import pallas as pl
from jax.experimental.pallas import tpu as pltpu
from jax.sharding import PartitionSpec as P

BF16 = jnp.bfloat16
F32 = jnp.float32
VMEM = pl.BlockSpec(memory_space=pltpu.VMEM)
SMEM = pl.BlockSpec(memory_space=pltpu.SMEM)
ANY = pl.BlockSpec(memory_space=pl.ANY)
HBM = pl.BlockSpec(memory_space=pltpu.HBM)
NN = (((1,), (0,)), ((), ()))
NT = (((1,), (1,)), ((), ()))


def dot(a, b, dims=NN):
    return lax.dot_general(a, b, dims, preferred_element_type=F32)


def silu_parts(half):
    tanh = jnp.tanh(half)
    upper = 1.0 + tanh
    act = half * upper
    return act, upper + act * (1.0 - tanh)


def call(body, outs, args, flops=0, scratch=(), smem=(), far=(), far_out=(), order=(), vmem=16, pin=False):
    args = [
        pltpu.with_memory_space_constraint(a, pltpu.HBM) if pin and i in far else a
        for i, a in enumerate(args)
    ] + list(order)
    moved = sum(a.size * a.dtype.itemsize for a in args) + sum(
        o.size * o.dtype.itemsize for o in outs
    )
    keep = len(args) - len(order)
    specs = [
        SMEM if i in smem else ANY if i >= keep else HBM if i in far else VMEM
        for i in range(len(args))
    ]

    def inner(*refs):
        body(*refs[:keep], *refs[len(args) :])

    return pl.pallas_call(
        inner if order else body,
        out_shape=tuple(outs),
        in_specs=specs,
        out_specs=tuple(HBM if i in far_out else VMEM for i in range(len(outs))),
        scratch_shapes=list(scratch),
        cost_estimate=pl.CostEstimate(flops=flops, bytes_accessed=moved, transcendentals=0),
        compiler_params=pltpu.CompilerParams(vmem_limit_bytes=vmem << 20),
    )(*args)


def shape(dims, dtype=BF16):
    return jax.ShapeDtypeStruct(dims, dtype)


def held(array):
    return pltpu.VMEM(array.shape, array.dtype)


def started(copies):
    for copy in copies:
        copy.start()
    return copies


def waited(copies):
    for copy in copies:
        copy.wait()


def loads(sources, targets, sems):
    return started(
        [pltpu.make_async_copy(a, b, sems.at[i]) for i, (a, b) in enumerate(zip(sources, targets))]
    )


def hot_lanes(index, first, count, slots, dead=None):
    block = index.shape[1]
    rows = lax.broadcasted_iota(jnp.int32, (slots, block), 0)
    parts = []
    for b in range(first, first + count):
        slot = index[pl.ds(b, 1), :]
        if dead is not None:
            slot = jnp.where(b < dead, slot, -1)
        parts.append(jnp.where(rows == slot, 1.0, 0.0).astype(BF16))
    return jnp.concatenate(parts, axis=1)


def turned(index, per_owner, ranks, me):
    slot = index[...] - me * per_owner
    return jnp.where(slot < 0, slot + ranks * per_owner, slot)


def gathered(pieces):
    return jnp.concatenate([p[...] for p in pieces], axis=0)


def scattered(value, outs):
    per = outs[0].shape[0]
    for s, out in enumerate(outs):
        out[...] = value[s * per : (s + 1) * per]


def columns_of(lists, me, kept, per_owner):
    parts = []
    for ref in lists:
        row = ref[pl.ds(me, 1), :].astype(F32)
        column = jnp.broadcast_to(row, (8, row.shape[1])).T[:, :1]
        parts.append(column[per_owner : 2 * per_owner] if kept else column[:per_owner])
    return jnp.concatenate(parts, axis=0)


def hot_edges(lists, me, kept, per_owner, edge_dev):
    first = per_owner if kept else 0
    row = jnp.concatenate(
        [ref[pl.ds(me, 1), :][:, first : first + per_owner] for ref in lists], axis=1
    )
    edges = lax.broadcasted_iota(jnp.int32, (edge_dev, row.shape[1]), 0)
    return jnp.where(edges == row, 1.0, 0.0).astype(BF16)


def hot_rows(column, edge_dev):
    edges = lax.broadcasted_iota(jnp.int32, (column.shape[0], edge_dev), 1).astype(F32)
    return jnp.where(column == edges, 1.0, 0.0).astype(BF16)


def pair_kernel(fetch, store, out, fetch_v, store_v, sems):
    waited(loads([fetch, store], [fetch_v, store_v], sems))
    out[...] = jnp.concatenate([fetch_v[...], store_v[...]], axis=1)


def near_kernel(edges, out, sems):
    waited(loads([edges], [out], sems))


def lend_kernel(ranks, me, *refs):
    lists, edges, outs = refs[:ranks], refs[ranks], refs[ranks + 1 :]
    hot = hot_rows(columns_of(lists, me[0], False, outs[0].shape[0]), edges.shape[0])
    scattered(dot(hot, edges[...]).astype(BF16), outs)


def owner_kernel(ranks, me, *refs):
    lists, (upstream, w_out, same, dhidden) = refs[:ranks], refs[ranks : ranks + 4]
    upstream_v, w_out_v, sems = refs[ranks + 4 :]
    arrive = loads([upstream, w_out], [upstream_v, w_out_v], sems)
    hot = hot_rows(columns_of(lists, me[0], True, same.shape[0] // ranks), upstream.shape[0])
    same[...] = dot(hot, hot, NT).astype(BF16)
    waited(arrive)
    dhidden[...] = dot(dot(hot, upstream_v[...]).astype(BF16), w_out_v[...], NT)


def forward_kernel(ranks, step, place, count, *refs):
    pieces, (src, dst, weight, basis) = refs[:ranks], refs[ranks : ranks + 4]
    outs = refs[ranks + 4 : 2 * ranks + 4]
    basis_v, message, hot, near_hot, sems = refs[2 * ranks + 4 :]
    arrive = loads([basis], [basis_v], sems)
    per_owner = outs[0].shape[0]
    slots, block = ranks * per_owner, src.shape[1]
    table, weight_t = gathered(pieces).T, (0.5 * weight[...]).T
    src_t = turned(src, per_owner, ranks, place[0])
    dst_t = turned(dst, per_owner, ranks, place[0])
    each = step // block
    spans = [pl.ds(i * step, step) for i in range(basis.shape[0] // step)]
    for i, at in enumerate(spans):
        near_hot[:, at] = hot_lanes(src_t, i * each, each, slots)
        hot[:, at] = hot_lanes(dst_t, i * each, each, slots, count[0, 0])
    waited(arrive)
    for at in spans:
        act = silu_parts(dot(weight_t, basis_v[at, :], NT))[0]
        message[:, at] = (dot(table, near_hot[:, at]) * act).astype(BF16)
    scattered(dot(hot[...], message[...], NT).astype(BF16), outs)


def return_kernel(ranks, *refs):
    pieces, (same, dhidden), outs = refs[:ranks], refs[ranks : ranks + 2], refs[ranks + 2 :]
    agg = dot(same[...], gathered(pieces))
    scattered((dhidden[...] * (0.5 * silu_parts(0.5 * agg)[1])).astype(BF16), outs)


def reverse(value, count):
    bits = count.bit_length() - 1
    return sum(((value >> b) & 1) << (bits - 1 - b) for b in range(bits))


def update_kernel(ranks, step, me, *refs):
    lists, pieces = refs[:ranks], refs[ranks : 2 * ranks]
    edges, upstream, w_out, updated, term = refs[2 * ranks : 2 * ranks + 5]
    edges_v, upstream_v, w_out_v, updated_v, hidden, sems, out_sems = refs[2 * ranks + 5 :]
    arrive = loads([w_out, edges, upstream], [w_out_v, edges_v, upstream_v], sems)
    home = gathered(pieces)
    rows = edges.shape[0]
    hot_t = hot_edges(lists, me[0], True, pieces[0].shape[0], rows)
    turns = rows // step
    spans = [pl.ds(i * step, step) for i in range(turns)]
    leave = [
        pltpu.make_async_copy(updated_v.at[at, :], updated.at[at, :], out_sems.at[i])
        for i, at in enumerate(spans)
    ]
    fresh = [
        silu_parts(0.5 * dot(hot_t[i * step : (i + 1) * step], home))[0].astype(BF16)
        for i in range(turns)
    ]
    waited(arrive)
    for i, at in enumerate(spans):
        total = edges_v[at, :].astype(F32) + dot(fresh[i], w_out_v[...])
        updated_v[at, :] = total.astype(BF16)
        leave[i].start()
        hidden[:, at] = fresh[i].T
    total = dot(hidden[...], upstream_v[...]).astype(BF16)
    if len(term.shape) == 2:
        term[...] = total
    else:
        parts, part = term.shape[0], term.shape[1]
        copies = parts // ranks
        for k in range(parts):
            block = reverse(k % copies, copies) * ranks + reverse(k // copies, ranks)
            term[k] = total[block * part : (block + 1) * part]
    waited(leave)


def backward_kernel(ranks, step, place, count, *refs):
    fetched, pieces = refs[:ranks], refs[ranks : 2 * ranks]
    src, dst, weight, basis, kept, away = refs[2 * ranks : 2 * ranks + 6]
    out = refs[2 * ranks + 6]
    basis_v, message, dpre, hot, back_hot, total, sems = refs[2 * ranks + 7 :]
    arrive = loads([basis], [basis_v], sems)
    per_owner = out.shape[1]
    slots, block = ranks * per_owner, src.shape[1]
    src_t = turned(src, per_owner, ranks, place[0])
    dst_t = turned(dst, per_owner, ranks, place[0])
    near, back = gathered(fetched).T, gathered(pieces).T
    weight_t = (0.5 * weight[...]).T
    each = step // block
    spans = [pl.ds(i * step, step) for i in range(basis.shape[0] // step)]
    for i, at in enumerate(spans):
        hot[:, at] = hot_lanes(src_t, i * each, each, slots)
        back_hot[:, at] = hot_lanes(dst_t, i * each, each, slots, count[0, 0])
    waited(arrive)
    for at in spans:
        act, slope = silu_parts(dot(weight_t, basis_v[at, :], NT))
        rows = dot(back, back_hot[:, at]).astype(BF16)
        message[:, at] = rows * act.astype(BF16)
        dpre[:, at] = rows * dot(near, hot[:, at]).astype(BF16) * slope.astype(BF16)
    total[...] = dot(dpre[...], basis_v[...]).T
    half = kept.shape[0]
    kept[...] = total[pl.ds(pl.multiple_of(place[1] * half, half), half), :]
    away[...] = total[pl.ds(pl.multiple_of((1 - place[1]) * half, half), half), :].astype(BF16)
    result = dot(hot[...], message[...], NT).astype(BF16)
    for s in range(ranks):
        piece = result[s * per_owner : (s + 1) * per_owner]
        out[(place[0] + s) % ranks] = piece


def final_kernel(ranks, step, me, *refs):
    lists, pieces = refs[:ranks], refs[ranks]
    upstream, out, upstream_v, out_v, sems, out_sems = refs[ranks + 1 :]
    arrive = loads([upstream], [upstream_v], sems)
    back = jnp.concatenate(
        [pieces[(me[0] - s + ranks) % ranks] for s in range(ranks)], axis=0
    )
    rows = upstream.shape[0]
    hot_t = hot_edges(lists, me[0], False, pieces.shape[1], rows)
    waited(arrive)
    leave = []
    for i in range(rows // step):
        at = pl.ds(i * step, step)
        total = upstream_v[at, :].astype(F32) + dot(hot_t[i * step : (i + 1) * step], back)
        out_v[at, :] = total.astype(BF16)
        leave.append(pltpu.make_async_copy(out_v.at[at, :], out.at[at, :], out_sems.at[i]))
        leave[i].start()
    waited(leave)


def finish_kernel(scales, low, out, out_got, basis, basis_got, out_full, basis_full):
    for own, got, full, scale in (
        (out, out_got, out_full, scales[0]),
        (basis, basis_got, basis_full, scales[1]),
    ):
        rows = own.shape[0]
        mine = pl.multiple_of(low[1] * rows, rows)
        other = pl.multiple_of((1 - low[1]) * rows, rows)
        full[pl.ds(mine, rows), :] = own[...].astype(F32) * scale
        full[pl.ds(other, rows), :] = got[...].astype(F32) * scale


def swap(value, axis, mask):
    return lax.ppermute(value, axis, [(k, k ^ mask) for k in range(lax.axis_size(axis))])


def shift(value, axis, by):
    count = lax.axis_size(axis)
    return lax.ppermute(value, axis, [(k, (k + by) % count) for k in range(count)])


def exchange(pieces, sign):
    return [pieces[0]] + [shift(pieces[s], "graph", sign * s) for s in range(1, len(pieces))]


def halve(value, axis, bit):
    half = value.reshape(2, value.shape[0] // 2, value.shape[1])
    own = (lax.axis_index(axis) >> bit) & 1
    away = lax.dynamic_index_in_dim(half, 1 - own, 0, keepdims=False).astype(BF16)
    kept = lax.dynamic_index_in_dim(half, own, 0, keepdims=False)
    return kept.astype(F32) + swap(away, axis, 1 << bit).astype(F32)


def double(value, got, axis, bit):
    low = ((lax.axis_index(axis) >> bit) & 1) == 0
    return jnp.where(low, jnp.concatenate([value, got]), jnp.concatenate([got, value]))


def bits_of(axis):
    return range(lax.axis_size(axis).bit_length() - 1)


def joined(kept, away):
    return kept + swap(away, "dp", 1).astype(F32)


def doubled(out, basis, axis, bit):
    rows = basis.shape[0]
    got = swap(jnp.concatenate([basis, out]), axis, 1 << bit)
    return got[:rows], double(out, got[rows:], axis, bit)


def per_device(
    edge_emb,
    cotangent,
    fetch_rows,
    store_rows,
    trip_src,
    trip_dst,
    trip_basis,
    block_count,
    w_basis,
    w_out,
):
    edges, upstream, basis = edge_emb[0], cotangent[0], trip_basis[0]
    ranks, copies = lax.axis_size("graph"), lax.axis_size("dp")
    place = jnp.stack([lax.axis_index("graph"), lax.axis_index("dp") & 1]).astype(jnp.int32)
    edge_dev, width = edges.shape
    per_owner = fetch_rows.shape[3]
    slots = ranks * per_owner
    blocks, block_rows = trip_src.shape[1:]
    triplets, basis_width = basis.shape
    src, dst = trip_src[0], trip_dst[0]
    pieces = [shape((per_owner, width))] * ranks
    plane, hot = shape((width, triplets)), shape((slots, triplets))
    step = 256
    wide = 2 * triplets * slots * width
    narrow = 2 * triplets * basis_width * width
    dma = pltpu.SemaphoreType.DMA

    (both,) = call(
        pair_kernel,
        [shape((ranks, 2 * per_owner), jnp.int32)],
        [fetch_rows[0, 0], store_rows[0, 0]],
        far=(0, 1),
        scratch=[pltpu.VMEM((ranks, per_owner), jnp.int32)] * 2 + [dma((2,))],
        pin=True,
    )
    lists = exchange([both] * ranks, 1)
    (near,) = call(
        near_kernel,
        [shape(edges.shape)],
        [edges],
        far=(0,),
        flops=wide,
        scratch=[dma((1,))],
        order=[both],
        pin=True,
    )
    lend = call(
        functools.partial(lend_kernel, ranks),
        pieces,
        [place] + lists + [near],
        smem=(0,),
        flops=2 * slots * edge_dev * width,
    )
    fetched = exchange(lend, -1)
    same, dhidden = call(
        functools.partial(owner_kernel, ranks),
        [shape((slots, slots)), shape((slots, width), F32)],
        [place] + lists + [upstream, w_out],
        smem=(0,),
        far=(ranks + 1, ranks + 2),
        flops=4 * slots * edge_dev * width,
        scratch=[held(upstream), held(w_out), dma((2,))],
        order=[lend[0]],
        pin=True,
    )
    partial_rows = call(
        functools.partial(forward_kernel, ranks, step),
        pieces,
        [place, block_count] + fetched + [src, dst, w_basis, basis],
        smem=(0, 1),
        far=(ranks + 5,),
        flops=2 * wide + narrow,
        scratch=[held(basis), held(plane), held(hot), held(hot), dma((1,))],
        order=[same],
        vmem=30,
        pin=True,
    )
    home = exchange(partial_rows, 1)
    back = call(
        functools.partial(return_kernel, ranks),
        pieces,
        home + [same, dhidden],
        flops=2 * slots * slots * width,
    )
    dpartial = exchange(back, -1)
    parts = ranks * copies
    part = width // parts
    term_dims = (width, width) if part % 16 else (parts, part, width)
    updated, out_term = call(
        functools.partial(update_kernel, ranks, 256),
        [shape((edge_dev, width)), shape(term_dims)],
        [place] + lists + home + [edges, upstream, w_out],
        smem=(0,),
        far=(2 * ranks + 1, 2 * ranks + 2, 2 * ranks + 3),
        far_out=(0,),
        flops=2 * edge_dev * width * (2 * width + slots),
        scratch=[held(edges), held(upstream), held(w_out), held(edges)]
        + [pltpu.VMEM((width, edge_dev), BF16), dma((3,)), dma((edge_dev // 256,))],
        order=[back[0]],
    )
    sent = out_term
    if part % 16:
        blocks_of = [
            reverse(k % copies, copies) * ranks + reverse(k // copies, ranks) for k in range(parts)
        ]
        split = out_term.reshape(parts, part, width)
        sent = jnp.stack([split[block] for block in blocks_of])
    out_parts = lax.all_to_all(sent, ("graph", "dp"), split_axis=0, concat_axis=0, tiled=True)
    basis_half = basis_width // 2
    basis_kept, basis_away, dfetch = call(
        functools.partial(backward_kernel, ranks, step),
        [shape((basis_half, width), F32), shape((basis_half, width))]
        + [shape((ranks, per_owner, width))],
        [place, block_count] + fetched + dpartial + [src, dst, w_basis, basis],
        smem=(0, 1),
        far=(2 * ranks + 5,),
        flops=3 * wide + 2 * narrow,
        scratch=[held(basis), held(plane), held(plane), held(hot), held(hot)]
        + [pltpu.VMEM((basis_width, width), F32), dma((1,))],
        order=[out_term],
        vmem=36,
        pin=True,
    )
    returned = lax.all_to_all(dfetch, "graph", split_axis=0, concat_axis=0, tiled=True)
    basis_part = joined(basis_kept, basis_away)
    for bit in bits_of("dp")[1:]:
        basis_part = halve(basis_part, "dp", bit)
    out_part = jnp.sum(out_parts.astype(F32), axis=0)
    out, total = out_part.astype(BF16), basis_part.astype(BF16)
    for bit in reversed(bits_of("graph")):
        got, out = doubled(out, total, "graph", bit)
        total = (total.astype(F32) + got.astype(F32)).astype(BF16)
    (grad_edge,) = call(
        functools.partial(final_kernel, ranks, 256),
        [shape((edge_dev, width))],
        [place] + lists + [returned, upstream],
        smem=(0,),
        far=(ranks + 2,),
        far_out=(0,),
        flops=2 * slots * edge_dev * width,
        scratch=[held(upstream), held(upstream), dma((1,)), dma((edge_dev // 256,))],
    )
    for bit in reversed(bits_of("dp")[1:]):
        got, out = doubled(out, total, "dp", bit)
        total = double(total, got, "dp", bit)
    out, total, grad_edge = lax.optimization_barrier((out, total, grad_edge))
    rows = total.shape[0]
    got = swap(jnp.concatenate([total, out]), "dp", 1)
    out_scale = 1.0 / math.sqrt(copies * ranks * edge_dev)
    basis_scale = 0.5 / math.sqrt(copies * ranks * blocks * block_rows)
    grad_w_out, grad_w_basis = call(
        functools.partial(finish_kernel, (out_scale, basis_scale)),
        [shape((width, width), F32), shape((basis_width, width), F32)],
        [place, out, got[rows:], total, got[:rows]],
        smem=(0,),
    )
    return (updated[None], grad_edge[None], grad_w_out, grad_w_basis)


def solution(mesh):
    placed = (
        P(("groups", "dp"), "graph", None),
        P(("groups", "dp"), "graph", None),
        P(("groups", "dp"), "graph", None, None),
        P(("groups", "dp"), "graph", None, None),
        P(("groups", "dp"), "graph", None),
        P(("groups", "dp"), "graph", None),
        P(("groups", "dp"), "graph", None),
        P(("groups", "dp"), "graph"),
        P(),
        P(),
    )
    return jax.shard_map(
        per_device,
        mesh=mesh,
        in_specs=placed,
        out_specs=(
            P(("groups", "dp"), "graph", None),
            P(("groups", "dp"), "graph", None),
            P("groups", None),
            P("groups", None),
        ),
        check_vma=False,
    )
```

```python
import functools
import math

import jax
import jax.numpy as jnp
from jax import lax
from jax.experimental import pallas as pl
from jax.experimental.pallas import tpu as pltpu
from jax.sharding import PartitionSpec as P

BF16 = jnp.bfloat16
F32 = jnp.float32
VMEM = pl.BlockSpec(memory_space=pltpu.VMEM)
SMEM = pl.BlockSpec(memory_space=pltpu.SMEM)
ANY = pl.BlockSpec(memory_space=pl.ANY)
HBM = pl.BlockSpec(memory_space=pltpu.HBM)
NN = (((1,), (0,)), ((), ()))
NT = (((1,), (1,)), ((), ()))


def dot(a, b, dims=NN):
    return lax.dot_general(a, b, dims, preferred_element_type=F32)


def silu_parts(half):
    tanh = jnp.tanh(half)
    upper = 1.0 + tanh
    act = half * upper
    return act, upper + act * (1.0 - tanh)


def call(body, outs, args, flops=0, scratch=(), smem=(), far=(), far_out=(), order=(), vmem=16, pin=False):
    args = [
        pltpu.with_memory_space_constraint(a, pltpu.HBM) if pin and i in far else a
        for i, a in enumerate(args)
    ] + list(order)
    moved = sum(a.size * a.dtype.itemsize for a in args) + sum(
        o.size * o.dtype.itemsize for o in outs
    )
    keep = len(args) - len(order)
    specs = [
        SMEM if i in smem else ANY if i >= keep else HBM if i in far else VMEM
        for i in range(len(args))
    ]

    def inner(*refs):
        body(*refs[:keep], *refs[len(args) :])

    return pl.pallas_call(
        inner if order else body,
        out_shape=tuple(outs),
        in_specs=specs,
        out_specs=tuple(HBM if i in far_out else VMEM for i in range(len(outs))),
        scratch_shapes=list(scratch),
        cost_estimate=pl.CostEstimate(flops=flops, bytes_accessed=moved, transcendentals=0),
        compiler_params=pltpu.CompilerParams(vmem_limit_bytes=vmem << 20),
    )(*args)


def shape(dims, dtype=BF16):
    return jax.ShapeDtypeStruct(dims, dtype)


def held(array):
    return pltpu.VMEM(array.shape, array.dtype)


def started(copies):
    for copy in copies:
        copy.start()
    return copies


def waited(copies):
    for copy in copies:
        copy.wait()


def loads(sources, targets, sems):
    return started(
        [pltpu.make_async_copy(a, b, sems.at[i]) for i, (a, b) in enumerate(zip(sources, targets))]
    )


def hot_lanes(index, first, count, slots, dead=None):
    block = index.shape[1]
    rows = lax.broadcasted_iota(jnp.int32, (slots, block), 0)
    parts = []
    for b in range(first, first + count):
        slot = index[pl.ds(b, 1), :]
        if dead is not None:
            slot = jnp.where(b < dead, slot, -1)
        parts.append(jnp.where(rows == slot, 1.0, 0.0).astype(BF16))
    return jnp.concatenate(parts, axis=1)


def turned(index, per_owner, ranks, me):
    slot = index[...] - me * per_owner
    return jnp.where(slot < 0, slot + ranks * per_owner, slot)


def gathered(pieces):
    return jnp.concatenate([p[...] for p in pieces], axis=0)


def scattered(value, outs):
    per = outs[0].shape[0]
    for s, out in enumerate(outs):
        out[...] = value[s * per : (s + 1) * per]


def columns_of(lists, me, kept, per_owner):
    parts = []
    for ref in lists:
        row = ref[pl.ds(me, 1), :].astype(F32)
        column = jnp.broadcast_to(row, (8, row.shape[1])).T[:, :1]
        parts.append(column[per_owner : 2 * per_owner] if kept else column[:per_owner])
    return jnp.concatenate(parts, axis=0)


def hot_edges(lists, me, kept, per_owner, edge_dev):
    first = per_owner if kept else 0
    row = jnp.concatenate(
        [ref[pl.ds(me, 1), :][:, first : first + per_owner] for ref in lists], axis=1
    )
    edges = lax.broadcasted_iota(jnp.int32, (edge_dev, row.shape[1]), 0)
    return jnp.where(edges == row, 1.0, 0.0).astype(BF16)


def hot_rows(column, edge_dev):
    edges = lax.broadcasted_iota(jnp.int32, (column.shape[0], edge_dev), 1).astype(F32)
    return jnp.where(column == edges, 1.0, 0.0).astype(BF16)


def pair_kernel(fetch, store, out, fetch_v, store_v, sems):
    waited(loads([fetch, store], [fetch_v, store_v], sems))
    out[...] = jnp.concatenate([fetch_v[...], store_v[...]], axis=1)


def near_kernel(edges, out, sems):
    waited(loads([edges], [out], sems))


def lend_kernel(ranks, me, *refs):
    lists, edges, outs = refs[:ranks], refs[ranks], refs[ranks + 1 :]
    hot = hot_rows(columns_of(lists, me[0], False, outs[0].shape[0]), edges.shape[0])
    scattered(dot(hot, edges[...]).astype(BF16), outs)


def owner_kernel(ranks, me, *refs):
    lists, (upstream, w_out, same, dhidden) = refs[:ranks], refs[ranks : ranks + 4]
    upstream_v, w_out_v, sems = refs[ranks + 4 :]
    arrive = loads([upstream, w_out], [upstream_v, w_out_v], sems)
    hot = hot_rows(columns_of(lists, me[0], True, same.shape[0] // ranks), upstream.shape[0])
    same[...] = dot(hot, hot, NT).astype(BF16)
    waited(arrive)
    dhidden[...] = dot(dot(hot, upstream_v[...]).astype(BF16), w_out_v[...], NT)


def forward_kernel(ranks, step, place, count, *refs):
    pieces, (src, dst, weight, basis) = refs[:ranks], refs[ranks : ranks + 4]
    outs = refs[ranks + 4 : 2 * ranks + 4]
    basis_v, message, hot, near_hot, sems = refs[2 * ranks + 4 :]
    arrive = loads([basis], [basis_v], sems)
    per_owner = outs[0].shape[0]
    slots, block = ranks * per_owner, src.shape[1]
    table, weight_t = gathered(pieces).T, (0.5 * weight[...]).T
    src_t = turned(src, per_owner, ranks, place[0])
    dst_t = turned(dst, per_owner, ranks, place[0])
    each = step // block
    spans = [pl.ds(i * step, step) for i in range(basis.shape[0] // step)]
    for i, at in enumerate(spans):
        near_hot[:, at] = hot_lanes(src_t, i * each, each, slots)
        hot[:, at] = hot_lanes(dst_t, i * each, each, slots, count[0, 0])
    waited(arrive)
    for at in spans:
        act = silu_parts(dot(weight_t, basis_v[at, :], NT))[0]
        message[:, at] = dot(table, near_hot[:, at]).astype(BF16) * act.astype(BF16)
    scattered(dot(hot[...], message[...], NT).astype(BF16), outs)


def return_kernel(ranks, *refs):
    pieces, (same, dhidden), outs = refs[:ranks], refs[ranks : ranks + 2], refs[ranks + 2 :]
    agg = dot(same[...], gathered(pieces))
    scattered((dhidden[...] * (0.5 * silu_parts(0.5 * agg)[1])).astype(BF16), outs)


def reverse(value, count):
    bits = count.bit_length() - 1
    return sum(((value >> b) & 1) << (bits - 1 - b) for b in range(bits))


def update_kernel(ranks, step, me, *refs):
    lists, pieces = refs[:ranks], refs[ranks : 2 * ranks]
    edges, upstream, w_out, updated, term = refs[2 * ranks : 2 * ranks + 5]
    edges_v, upstream_v, w_out_v, updated_v, hidden, sems, out_sems = refs[2 * ranks + 5 :]
    arrive = loads([w_out, edges, upstream], [w_out_v, edges_v, upstream_v], sems)
    home = gathered(pieces)
    rows = edges.shape[0]
    hot_t = hot_edges(lists, me[0], True, pieces[0].shape[0], rows)
    turns = rows // step
    spans = [pl.ds(i * step, step) for i in range(turns)]
    leave = [
        pltpu.make_async_copy(updated_v.at[at, :], updated.at[at, :], out_sems.at[i])
        for i, at in enumerate(spans)
    ]
    fresh = [
        silu_parts(0.5 * dot(hot_t[i * step : (i + 1) * step], home))[0].astype(BF16)
        for i in range(turns)
    ]
    waited(arrive)
    for i, at in enumerate(spans):
        total = edges_v[at, :].astype(F32) + dot(fresh[i], w_out_v[...])
        updated_v[at, :] = total.astype(BF16)
        leave[i].start()
        hidden[:, at] = fresh[i].T
    total = dot(hidden[...], upstream_v[...]).astype(BF16)
    if len(term.shape) == 2:
        term[...] = total
    else:
        parts, part = term.shape[0], term.shape[1]
        copies = parts // ranks
        for k in range(parts):
            block = reverse(k % copies, copies) * ranks + reverse(k // copies, ranks)
            term[k] = total[block * part : (block + 1) * part]
    waited(leave)


def backward_kernel(ranks, step, place, count, *refs):
    fetched, pieces = refs[:ranks], refs[ranks : 2 * ranks]
    src, dst, weight, basis, kept, away = refs[2 * ranks : 2 * ranks + 6]
    out = refs[2 * ranks + 6]
    basis_v, message, dpre, hot, back_hot, total, sems = refs[2 * ranks + 7 :]
    arrive = loads([basis], [basis_v], sems)
    per_owner = out.shape[1]
    slots, block = ranks * per_owner, src.shape[1]
    src_t = turned(src, per_owner, ranks, place[0])
    dst_t = turned(dst, per_owner, ranks, place[0])
    near, back = gathered(fetched).T, gathered(pieces).T
    weight_t = (0.5 * weight[...]).T
    each = step // block
    spans = [pl.ds(i * step, step) for i in range(basis.shape[0] // step)]
    for i, at in enumerate(spans):
        hot[:, at] = hot_lanes(src_t, i * each, each, slots)
        back_hot[:, at] = hot_lanes(dst_t, i * each, each, slots, count[0, 0])
    waited(arrive)
    for at in spans:
        act, slope = silu_parts(dot(weight_t, basis_v[at, :], NT))
        rows = dot(back, back_hot[:, at]).astype(BF16)
        message[:, at] = rows * act.astype(BF16)
        dpre[:, at] = rows * dot(near, hot[:, at]).astype(BF16) * slope.astype(BF16)
    total[...] = dot(dpre[...], basis_v[...]).T
    half = kept.shape[0]
    kept[...] = total[pl.ds(pl.multiple_of(place[1] * half, half), half), :]
    away[...] = total[pl.ds(pl.multiple_of((1 - place[1]) * half, half), half), :].astype(BF16)
    result = dot(hot[...], message[...], NT).astype(BF16)
    for s in range(ranks):
        piece = result[s * per_owner : (s + 1) * per_owner]
        out[(place[0] + s) % ranks] = piece


def final_kernel(ranks, step, me, *refs):
    lists, pieces = refs[:ranks], refs[ranks]
    upstream, out, upstream_v, out_v, sems, out_sems = refs[ranks + 1 :]
    arrive = loads([upstream], [upstream_v], sems)
    back = jnp.concatenate(
        [pieces[(me[0] - s + ranks) % ranks] for s in range(ranks)], axis=0
    )
    rows = upstream.shape[0]
    hot_t = hot_edges(lists, me[0], False, pieces.shape[1], rows)
    waited(arrive)
    leave = []
    for i in range(rows // step):
        at = pl.ds(i * step, step)
        total = upstream_v[at, :].astype(F32) + dot(hot_t[i * step : (i + 1) * step], back)
        out_v[at, :] = total.astype(BF16)
        leave.append(pltpu.make_async_copy(out_v.at[at, :], out.at[at, :], out_sems.at[i]))
        leave[i].start()
    waited(leave)


def finish_kernel(scales, low, out, out_got, basis, basis_got, out_full, basis_full):
    for own, got, full, scale in (
        (out, out_got, out_full, scales[0]),
        (basis, basis_got, basis_full, scales[1]),
    ):
        rows = own.shape[0]
        mine = pl.multiple_of(low[1] * rows, rows)
        other = pl.multiple_of((1 - low[1]) * rows, rows)
        full[pl.ds(mine, rows), :] = own[...].astype(F32) * scale
        full[pl.ds(other, rows), :] = got[...].astype(F32) * scale


def swap(value, axis, mask):
    return lax.ppermute(value, axis, [(k, k ^ mask) for k in range(lax.axis_size(axis))])


def shift(value, axis, by):
    count = lax.axis_size(axis)
    return lax.ppermute(value, axis, [(k, (k + by) % count) for k in range(count)])


def exchange(pieces, sign):
    return [pieces[0]] + [shift(pieces[s], "graph", sign * s) for s in range(1, len(pieces))]


def halve(value, axis, bit):
    half = value.reshape(2, value.shape[0] // 2, value.shape[1])
    own = (lax.axis_index(axis) >> bit) & 1
    away = lax.dynamic_index_in_dim(half, 1 - own, 0, keepdims=False).astype(BF16)
    kept = lax.dynamic_index_in_dim(half, own, 0, keepdims=False)
    return kept.astype(F32) + swap(away, axis, 1 << bit).astype(F32)


def double(value, got, axis, bit):
    low = ((lax.axis_index(axis) >> bit) & 1) == 0
    return jnp.where(low, jnp.concatenate([value, got]), jnp.concatenate([got, value]))


def bits_of(axis):
    return range(lax.axis_size(axis).bit_length() - 1)


def joined(kept, away):
    return kept + swap(away, "dp", 1).astype(F32)


def doubled(out, basis, axis, bit):
    rows = basis.shape[0]
    got = swap(jnp.concatenate([basis, out]), axis, 1 << bit)
    return got[:rows], double(out, got[rows:], axis, bit)


def per_device(
    edge_emb,
    cotangent,
    fetch_rows,
    store_rows,
    trip_src,
    trip_dst,
    trip_basis,
    block_count,
    w_basis,
    w_out,
):
    edges, upstream, basis = edge_emb[0], cotangent[0], trip_basis[0]
    ranks, copies = lax.axis_size("graph"), lax.axis_size("dp")
    place = jnp.stack([lax.axis_index("graph"), lax.axis_index("dp") & 1]).astype(jnp.int32)
    edge_dev, width = edges.shape
    per_owner = fetch_rows.shape[3]
    slots = ranks * per_owner
    blocks, block_rows = trip_src.shape[1:]
    triplets, basis_width = basis.shape
    src, dst = trip_src[0], trip_dst[0]
    pieces = [shape((per_owner, width))] * ranks
    plane, hot = shape((width, triplets)), shape((slots, triplets))
    step = 256
    wide = 2 * triplets * slots * width
    narrow = 2 * triplets * basis_width * width
    dma = pltpu.SemaphoreType.DMA

    (both,) = call(
        pair_kernel,
        [shape((ranks, 2 * per_owner), jnp.int32)],
        [fetch_rows[0, 0], store_rows[0, 0]],
        far=(0, 1),
        scratch=[pltpu.VMEM((ranks, per_owner), jnp.int32)] * 2 + [dma((2,))],
        pin=True,
    )
    lists = exchange([both] * ranks, 1)
    (near,) = call(
        near_kernel,
        [shape(edges.shape)],
        [edges],
        far=(0,),
        flops=wide,
        scratch=[dma((1,))],
        order=[both],
        pin=True,
    )
    lend = call(
        functools.partial(lend_kernel, ranks),
        pieces,
        [place] + lists + [near],
        smem=(0,),
        flops=2 * slots * edge_dev * width,
    )
    fetched = exchange(lend, -1)
    same, dhidden = call(
        functools.partial(owner_kernel, ranks),
        [shape((slots, slots)), shape((slots, width), F32)],
        [place] + lists + [upstream, w_out],
        smem=(0,),
        far=(ranks + 1, ranks + 2),
        flops=4 * slots * edge_dev * width,
        scratch=[held(upstream), held(w_out), dma((2,))],
        order=[lend[0]],
        pin=True,
    )
    partial_rows = call(
        functools.partial(forward_kernel, ranks, step),
        pieces,
        [place, block_count] + fetched + [src, dst, w_basis, basis],
        smem=(0, 1),
        far=(ranks + 5,),
        flops=2 * wide + narrow,
        scratch=[held(basis), held(plane), held(hot), held(hot), dma((1,))],
        order=[same],
        vmem=30,
        pin=True,
    )
    home = exchange(partial_rows, 1)
    back = call(
        functools.partial(return_kernel, ranks),
        pieces,
        home + [same, dhidden],
        flops=2 * slots * slots * width,
    )
    dpartial = exchange(back, -1)
    parts = ranks * copies
    part = width // parts
    term_dims = (width, width) if part % 16 else (parts, part, width)
    updated, out_term = call(
        functools.partial(update_kernel, ranks, 256),
        [shape((edge_dev, width)), shape(term_dims)],
        [place] + lists + home + [edges, upstream, w_out],
        smem=(0,),
        far=(2 * ranks + 1, 2 * ranks + 2, 2 * ranks + 3),
        far_out=(0,),
        flops=2 * edge_dev * width * (2 * width + slots),
        scratch=[held(edges), held(upstream), held(w_out), held(edges)]
        + [pltpu.VMEM((width, edge_dev), BF16), dma((3,)), dma((edge_dev // 256,))],
        order=[back[0]],
    )
    sent = out_term
    if part % 16:
        blocks_of = [
            reverse(k % copies, copies) * ranks + reverse(k // copies, ranks) for k in range(parts)
        ]
        split = out_term.reshape(parts, part, width)
        sent = jnp.stack([split[block] for block in blocks_of])
    out_parts = lax.all_to_all(sent, ("graph", "dp"), split_axis=0, concat_axis=0, tiled=True)
    basis_half = basis_width // 2
    basis_kept, basis_away, dfetch = call(
        functools.partial(backward_kernel, ranks, step),
        [shape((basis_half, width), F32), shape((basis_half, width))]
        + [shape((ranks, per_owner, width))],
        [place, block_count] + fetched + dpartial + [src, dst, w_basis, basis],
        smem=(0, 1),
        far=(2 * ranks + 5,),
        flops=3 * wide + 2 * narrow,
        scratch=[held(basis), held(plane), held(plane), held(hot), held(hot)]
        + [pltpu.VMEM((basis_width, width), F32), dma((1,))],
        order=[out_term],
        vmem=36,
        pin=True,
    )
    returned = lax.all_to_all(dfetch, "graph", split_axis=0, concat_axis=0, tiled=True)
    basis_part = joined(basis_kept, basis_away)
    for bit in bits_of("dp")[1:]:
        basis_part = halve(basis_part, "dp", bit)
    out_part = jnp.sum(out_parts.astype(F32), axis=0)
    out, total = out_part.astype(BF16), basis_part.astype(BF16)
    for bit in reversed(bits_of("graph")):
        got, out = doubled(out, total, "graph", bit)
        total = (total.astype(F32) + got.astype(F32)).astype(BF16)
    (grad_edge,) = call(
        functools.partial(final_kernel, ranks, 256),
        [shape((edge_dev, width))],
        [place] + lists + [returned, upstream],
        smem=(0,),
        far=(ranks + 2,),
        far_out=(0,),
        flops=2 * slots * edge_dev * width,
        scratch=[held(upstream), held(upstream), dma((1,)), dma((edge_dev // 256,))],
    )
    for bit in reversed(bits_of("dp")[1:]):
        got, out = doubled(out, total, "dp", bit)
        total = double(total, got, "dp", bit)
    out, total, grad_edge = lax.optimization_barrier((out, total, grad_edge))
    rows = total.shape[0]
    got = swap(jnp.concatenate([total, out]), "dp", 1)
    out_scale = 1.0 / math.sqrt(copies * ranks * edge_dev)
    basis_scale = 0.5 / math.sqrt(copies * ranks * blocks * block_rows)
    grad_w_out, grad_w_basis = call(
        functools.partial(finish_kernel, (out_scale, basis_scale)),
        [shape((width, width), F32), shape((basis_width, width), F32)],
        [place, out, got[rows:], total, got[:rows]],
        smem=(0,),
    )
    return (updated[None], grad_edge[None], grad_w_out, grad_w_basis)


def solution(mesh):
    placed = (
        P(("groups", "dp"), "graph", None),
        P(("groups", "dp"), "graph", None),
        P(("groups", "dp"), "graph", None, None),
        P(("groups", "dp"), "graph", None, None),
        P(("groups", "dp"), "graph", None),
        P(("groups", "dp"), "graph", None),
        P(("groups", "dp"), "graph", None),
        P(("groups", "dp"), "graph"),
        P(),
        P(),
    )
    return jax.shard_map(
        per_device,
        mesh=mesh,
        in_specs=placed,
        out_specs=(
            P(("groups", "dp"), "graph", None),
            P(("groups", "dp"), "graph", None),
            P("groups", None),
            P("groups", None),
        ),
        check_vma=False,
    )
```
